32 devices in a mesh: dp: 8 (over z, y), fsdp: 4 (over x, core).
Axes of the slice: x: 2, y: 2, z: 4, core: 2. Of those that a mesh axis runs over, the one named last changes fastest.
Arguments:
- inputs: bfloat16 [16, 1024, 1024], P('dp', 'fsdp'), may hold values from -6 to 6
- timestep: int32 [16], P('dp'), may hold values from 0 to 4999, as said below
- bucket_count: int32 [8], replicated, may hold values from 1 to 2, as said below
- upstream: bfloat16 [16, 1024, 1024], P('dp', 'fsdp'), may hold values from -6 to 6
- query_weight: bfloat16 [1024, 1024], P('fsdp'), may hold values from -0.1875 to 0.1875
- key_weight: bfloat16 [1024, 1024], P('fsdp'), may hold values from -0.1875 to 0.1875
- value_weight: bfloat16 [1024, 1024], P('fsdp'), may hold values from -0.1875 to 0.1875
- output_weight: bfloat16 [1024, 1024], P('fsdp'), may hold values from -1 to 1
- up_weight: bfloat16 [1024, 4096], P('fsdp'), may hold values from -0.1875 to 0.1875
- down_weight: bfloat16 [4096, 1024], P('fsdp'), may hold values from -0.09375 to 0.09375
- query_bias: bfloat16 [1024], P('fsdp'), may hold values from -2 to 2
- value_bias: bfloat16 [1024], P('fsdp'), may hold values from -2 to 2
- output_bias: bfloat16 [1024], P('fsdp'), may hold values from -2 to 2
- up_bias: bfloat16 [4096], P('fsdp'), may hold values from -2 to 2
- down_bias: bfloat16 [1024], P('fsdp'), may hold values from -2 to 2
- first_gain: bfloat16 [1024], P('fsdp'), may hold values from 0.5 to 1.5
- first_shift: bfloat16 [1024], P('fsdp'), may hold values from -2 to 2
- second_gain: bfloat16 [1024], P('fsdp'), may hold values from 0.5 to 1.5
- second_shift: bfloat16 [1024], P('fsdp'), may hold values from -2 to 2
Outputs:
- activations: bfloat16 [16, 1024, 1024], P('dp', 'fsdp')
- input_gradient: float32 [16, 1024, 1024], P('dp', 'fsdp')
- time_gradient: float32 [16, 1024], P('dp', 'fsdp')
- query_weight_gradient: float32 [1024, 1024], P('fsdp')
- key_weight_gradient: float32 [1024, 1024], P('fsdp')
- value_weight_gradient: float32 [1024, 1024], P('fsdp')
- output_weight_gradient: float32 [1024, 1024], P('fsdp')
- up_weight_gradient: float32 [1024, 4096], P('fsdp')
- down_weight_gradient: float32 [4096, 1024], P('fsdp')
- query_bias_gradient: float32 [1024], P('fsdp')
- value_bias_gradient: float32 [1024], P('fsdp')
- output_bias_gradient: float32 [1024], P('fsdp')
- up_bias_gradient: float32 [4096], P('fsdp')
- down_bias_gradient: float32 [1024], P('fsdp')
- first_gain_gradient: float32 [1024], P('fsdp')
- first_shift_gradient: float32 [1024], P('fsdp')
- second_gain_gradient: float32 [1024], P('fsdp')
- second_shift_gradient: float32 [1024], P('fsdp')
The draws below stay inside these ranges and needn't reach their ends.
Inputs may be any that keep to these rules, and one draw needn't show every extreme that they name: Slots 0 to bucket_count[b] - 1 of bucket b are live, the others carry no gradient; the last bucket is always full. The timestep of sequence s lies in [b W, (b + 1) W) with b = s // 2 and W = 5000 divided by the number of buckets, rounded down.
All inputs are finite; a program needn't handle non-finite values.
Results may differ from the reference program's by a relative error of at most 0.017.
Values may be sent and summed in bfloat16 or wider, within the bound.
No kernel may reach another device: no remote copies, remote signals or barrier semaphores. Data moves between devices by JAX's collectives and lax.ppermute only.
A program may use at most 256 MiB of HBM per device.

```python
import math
import jax
import jax.numpy as jnp
from jax import lax

D = 1024
FF = 4096
HEADS = 16
HEAD_DIM = 64
SEQ_DEV = 2
NSTEPS = 5000
SEQ_LEN = 1024
SEQS = 16
N_DP = 8


def draw_timestep(key, part):
    key = jax.random.fold_in(key, 11)
    bucket_width = NSTEPS // N_DP
    bucket = jnp.arange(SEQS, dtype=jnp.int32) // SEQ_DEV
    drawn = bucket * bucket_width + jax.random.randint(key, (SEQS,), 0, bucket_width, dtype=jnp.int32)
    drawn = drawn.at[0].set(0)
    return drawn.at[SEQS - 1].set(N_DP * bucket_width - 1)


def draw_bucket_count(key, part):
    key = jax.random.fold_in(key, 23)
    random_rolls = jax.random.randint(key, (N_DP, SEQ_DEV - 1), 0, N_DP, dtype=jnp.int32)
    levels = jnp.arange(N_DP, dtype=jnp.int32)[:, None]
    return 1 + jnp.sum((random_rolls <= levels).astype(jnp.int32), axis=1)


def shard_levels(own_key, shape, cuts, low, top_value):
    def one(axis_at, blocks):
        heights = jax.random.uniform(jax.random.fold_in(jax.random.fold_in(own_key, 6), axis_at), (blocks,), jnp.float32, low / len(cuts), top_value / len(cuts))
        return jnp.repeat(jnp.exp(heights), shape[axis_at] // blocks).reshape((-1,) + (1,) * (len(shape) - axis_at - 1))

    loudness = one(*cuts[0])
    for cut in cuts[1:]:
        loudness = loudness * one(*cut)
    return loudness


def centred(own_key, shape, deviation, most, cuts=(), kind=jnp.bfloat16):
    level = shard_levels(own_key, shape, cuts, -0.22, 0.18) if cuts else 1.0
    values = jax.random.normal(own_key, shape, jnp.float32) * deviation * level
    return jnp.minimum(jnp.maximum(values, -most), most).astype(kind)


def setup_inputs(seed: int = 0) -> dict:
    key_of = jax.random.split(jax.random.key(seed), 20)
    inputs = centred(key_of[0], (SEQS, SEQ_LEN, D), 1.0, 6.0, ((0, 8), (1, 4)))
    timestep = draw_timestep(jax.random.fold_in(key_of[19], 71), 0)
    bucket_count = draw_bucket_count(jax.random.fold_in(key_of[19], 71), 0)
    upstream = centred(key_of[3], (SEQS, SEQ_LEN, D), 1.0, 6.0, ((0, 8), (1, 4)))
    query_weight = centred(key_of[4], (D, D), D ** -0.5, 0.1875, ((0, 4),))
    key_weight = centred(key_of[5], (D, D), D ** -0.5, 0.1875, ((0, 4),))
    value_weight = centred(key_of[6], (D, D), D ** -0.5, 0.1875, ((0, 4),))
    output_weight = centred(key_of[7], (D, D), (D // 32) ** -0.5, 1.0, ((0, 4),))
    up_weight = centred(key_of[8], (D, FF), D ** -0.5, 0.1875, ((0, 4),))
    down_weight = centred(key_of[9], (FF, D), FF ** -0.5, 0.09375, ((0, 4),))
    query_bias = centred(key_of[10], (D,), 0.3, 2.0, ((0, 4),))
    value_bias = centred(key_of[11], (D,), 0.3, 2.0, ((0, 4),))
    output_bias = centred(key_of[12], (D,), 0.3, 2.0, ((0, 4),))
    up_bias = centred(key_of[13], (FF,), 0.3, 2.0, ((0, 4),))
    down_bias = centred(key_of[14], (D,), 0.3, 2.0, ((0, 4),))
    first_gain = jnp.clip(1.0 + 0.1 * jax.random.normal(key_of[15], (D,), jnp.float32), 0.5, 1.5).astype(jnp.bfloat16)
    first_shift = centred(key_of[16], (D,), 0.3, 2.0, ((0, 4),))
    second_gain = jnp.clip(1.0 + 0.1 * jax.random.normal(key_of[17], (D,), jnp.float32), 0.5, 1.5).astype(jnp.bfloat16)
    second_shift = centred(key_of[18], (D,), 0.3, 2.0, ((0, 4),))
    return {"inputs": inputs, "timestep": timestep, "bucket_count": bucket_count, "upstream": upstream, "query_weight": query_weight, "key_weight": key_weight, "value_weight": value_weight, "output_weight": output_weight, "up_weight": up_weight, "down_weight": down_weight, "query_bias": query_bias, "value_bias": value_bias, "output_bias": output_bias, "up_bias": up_bias, "down_bias": down_bias, "first_gain": first_gain, "first_shift": first_shift, "second_gain": second_gain, "second_shift": second_shift}


@jax.custom_vjp
def low(v):
    return lax.optimization_barrier(v.astype(jnp.bfloat16)).astype(jnp.float32)

@jax.custom_vjp
def low_back(v):
    return v

def low_keep(v):
    return (low(v), None)

def low_pass(kept, grad):
    return (grad,)

def back_keep(v):
    return (v, None)

def back_low(kept, grad):
    return (low(grad),)
low.defvjp(low_keep, low_pass)
low_back.defvjp(back_keep, back_low)

def matmul(left_side, right_side):
    return jnp.dot(left_side, right_side, precision=lax.Precision.HIGHEST, preferred_element_type=jnp.float32)

def sinusoid(timestep):
    halves = D // 2
    frequency = jnp.exp(jnp.arange(halves, dtype=jnp.float32) * (-math.log(10000.0) / halves))
    angles = timestep.astype(jnp.float32)[:, None] * frequency[None, :]
    return jnp.concatenate([jnp.sin(angles), jnp.cos(angles)], axis=1)

def layer_norm(residual, norm_gain, norm_shift):
    row_mean = lax.optimization_barrier(jnp.mean(residual, axis=-1, keepdims=True))
    centered = residual - row_mean
    row_var = lax.optimization_barrier(jnp.mean(centered * centered, axis=-1, keepdims=True))
    return centered * lax.rsqrt(row_var + 1e-05) * norm_gain + norm_shift

def sequence_forward(tokens, embedding, params):
    query_weight, key_weight, value_weight, output_weight, up_weight, down_weight, query_bias, value_bias, output_bias, up_bias, down_bias, first_gain, first_shift, second_gain, second_shift = params
    scaling = HEAD_DIM ** (-0.5)
    hidden = tokens + embedding[None, :]
    rounded = low(hidden)
    queries = low(low_back(matmul(rounded, query_weight) + query_bias))
    key_rows = low(low_back(matmul(rounded, key_weight)))
    values = low(low_back(matmul(rounded, value_weight) + value_bias))
    query_heads = queries.reshape(-1, HEADS, HEAD_DIM)
    key_heads = key_rows.reshape(-1, HEADS, HEAD_DIM)
    value_heads = values.reshape(-1, HEADS, HEAD_DIM)
    scores = low_back(jnp.einsum('qhd,khd->hqk', query_heads, key_heads, precision=lax.Precision.HIGHEST) * scaling)
    row_peak = lax.optimization_barrier(jnp.max(scores, axis=-1, keepdims=True))
    exponent = jnp.exp(scores - row_peak)
    attention = exponent / lax.optimization_barrier(jnp.sum(exponent, axis=-1, keepdims=True))
    mixed_rows = jnp.einsum('hqk,khd->qhd', low(attention), value_heads, precision=lax.Precision.HIGHEST).reshape(-1, D)
    mixed_rows = low(low_back(mixed_rows))
    branch = low_back(matmul(mixed_rows, output_weight) + output_bias)
    first_norm = layer_norm(hidden + branch, first_gain, first_shift)
    upward = low_back(matmul(low(first_norm), up_weight) + up_bias)
    activated = low(jax.nn.gelu(upward, approximate=False))
    downward = low_back(matmul(activated, down_weight) + down_bias)
    return layer_norm(first_norm + downward, second_gain, second_shift)

def reference(inputs, timestep, bucket_count, upstream, query_weight, key_weight, value_weight, output_weight, up_weight, down_weight, query_bias, value_bias, output_bias, up_bias, down_bias, first_gain, first_shift, second_gain, second_shift):
    params = tuple((weight_array.astype(jnp.float32) for weight_array in (query_weight, key_weight, value_weight, output_weight, up_weight, down_weight, query_bias, value_bias, output_bias, up_bias, down_bias, first_gain, first_shift, second_gain, second_shift)))
    embeddings = sinusoid(timestep)
    position = jnp.arange(SEQS)
    live_slot = position % SEQ_DEV < bucket_count[position // SEQ_DEV]
    seq_weight = live_slot.astype(jnp.float32) * (SEQS / jnp.sum(bucket_count).astype(jnp.float32))
    cotangent = upstream.astype(jnp.float32) * seq_weight[:, None, None]

    def whole(tokens, embedding, weights_all):

        def single(operands):
            return sequence_forward(operands[0], operands[1], weights_all)
        return lax.map(jax.checkpoint(single), (tokens, embedding))
    result, pullback = jax.vjp(whole, inputs.astype(jnp.float32), embeddings, params)
    input_gradient, time_gradient, grads = pullback(cotangent)
    return (result.astype(jnp.bfloat16), input_gradient, time_gradient, grads[0], grads[1], grads[2], grads[3], grads[4], grads[5], grads[6], grads[7], grads[8], grads[9], grads[10], grads[11], grads[12], grads[13], grads[14])
```

```python
import functools
import math

import jax
import jax.numpy as jnp
from jax import lax
from jax.experimental import pallas as pl
from jax.experimental.pallas import tpu as pltpu
from jax.sharding import PartitionSpec as P

D = 1024
HEADS = 16
HEAD_DIM = 64
GROUP = 256
GROUP_HEADS = GROUP // HEAD_DIM
F32 = jnp.float32
BF16 = jnp.bfloat16
ROWS_ROWS = (((0,), (0,)), ((), ()))
COLS_COLS = (((1,), (1,)), ((), ()))
KERNEL = pltpu.CompilerParams(vmem_limit_bytes=50 * 2**20)
ANY = pl.BlockSpec(memory_space=pl.ANY)


def sinusoid(timestep):
    halves = D // 2
    frequency = jnp.exp(jnp.arange(halves, dtype=F32) * (-math.log(10000.0) / halves))
    angles = timestep.astype(F32)[:, None] * frequency[None, :]
    return jnp.concatenate([jnp.sin(angles), jnp.cos(angles)], axis=1)


def head_mask(head):
    return lax.broadcasted_iota(jnp.int32, (1, GROUP), 1) // HEAD_DIM == head


def cost(flops, nbytes):
    return pl.CostEstimate(flops=flops, bytes_accessed=nbytes, transcendentals=0)


def attend_kernel(tile, q_ref, k1_ref, k2_ref, v1_ref, v2_ref, out_ref, lse_ref):
    keys = jnp.concatenate([k1_ref[...], k2_ref[...]], axis=0)
    values_t = jnp.concatenate([v1_ref[...], v2_ref[...]], axis=0).T
    for start in range(0, q_ref.shape[0], tile):
        rows = pl.ds(start, tile)
        queries = q_ref[rows, :] * jnp.asarray(HEAD_DIM**-0.5, BF16)
        outs = []
        for head in range(GROUP_HEADS):
            masked = jnp.where(head_mask(head), queries, jnp.zeros_like(queries))
            scores = lax.dot_general(keys, masked, COLS_COLS, preferred_element_type=F32)
            peak = jnp.max(scores, axis=0, keepdims=True)
            exponent = jnp.exp(scores - peak)
            total = jnp.sum(exponent, axis=0, keepdims=True)
            attention = (exponent * (1.0 / total)).astype(BF16)
            lse_ref[0, head : head + 1, rows] = peak + jnp.log(total)
            own = values_t[head * HEAD_DIM : (head + 1) * HEAD_DIM, :]
            outs.append(jnp.dot(own, attention, preferred_element_type=F32))
        out_ref[rows, :] = jnp.concatenate(outs, axis=0).astype(BF16).T


def group_columns(rows, first=0):
    return pl.BlockSpec((rows, GROUP), lambda g: (0, first + g))


def attend(queries, k1, k2, v1, v2):
    tokens, width = queries.shape
    keys = k1.shape[0]
    groups = width // GROUP
    return pl.pallas_call(
        functools.partial(attend_kernel, min(512, tokens)),
        grid=(groups,),
        in_specs=[group_columns(tokens)] + [group_columns(keys)] * 4,
        out_specs=[
            group_columns(tokens),
            pl.BlockSpec((1, GROUP_HEADS, tokens), lambda g: (g, 0, 0)),
        ],
        out_shape=[
            jax.ShapeDtypeStruct((tokens, width), BF16),
            jax.ShapeDtypeStruct((groups, GROUP_HEADS, tokens), F32),
        ],
        compiler_params=KERNEL,
        cost_estimate=cost(20 * 10**9, 6 * 2**20),
        name="attend",
    )(queries, k1, k2, v1, v2)


def attend_back_kernel(
    tile, q_ref, k1_ref, k2_ref, v1_ref, v2_ref, lse_ref, grad_ref,
    dq_ref, dk1_ref, dk2_ref, dv1_ref, dv2_ref, p_all, ds_all, dk_sum, dv_sum,
):
    half = k1_ref.shape[0]
    keys = jnp.concatenate([k1_ref[...], k2_ref[...]], axis=0)
    values = jnp.concatenate([v1_ref[...], v2_ref[...]], axis=0)
    keys_t = keys.T
    for start in range(0, q_ref.shape[0], tile):
        rows = pl.ds(start, tile)
        queries = q_ref[rows, :] * jnp.asarray(HEAD_DIM**-0.5, BF16)
        grads = grad_ref[rows, :]
        query_parts, grad_parts, dq_parts = [], [], []
        for head in range(GROUP_HEADS):
            query_one = jnp.where(head_mask(head), queries, jnp.zeros_like(queries))
            grad_one = jnp.where(head_mask(head), grads, jnp.zeros_like(grads))
            scores = lax.dot_general(keys, query_one, COLS_COLS, preferred_element_type=F32)
            attention = jnp.exp(scores - lse_ref[0, head : head + 1, rows])
            prob_grad = lax.dot_general(values, grad_one, COLS_COLS, preferred_element_type=F32)
            weighted = jnp.sum(attention * prob_grad, axis=0, keepdims=True)
            score_grad = (attention * (prob_grad - weighted)).astype(BF16)
            place = slice(head * tile, (head + 1) * tile)
            p_all[:, place] = attention.astype(BF16)
            ds_all[:, place] = score_grad
            own = keys_t[head * HEAD_DIM : (head + 1) * HEAD_DIM, :]
            dq_parts.append(jnp.dot(own, score_grad, preferred_element_type=F32))
            query_parts.append(query_one)
            grad_parts.append(grad_one)
        dv_tile = jnp.dot(p_all[...], jnp.concatenate(grad_parts, axis=0), preferred_element_type=F32)
        dk_tile = jnp.dot(ds_all[...], jnp.concatenate(query_parts, axis=0), preferred_element_type=F32)
        if start == 0:
            dv_sum[...] = dv_tile
            dk_sum[...] = dk_tile
        else:
            dv_sum[...] += dv_tile
            dk_sum[...] += dk_tile
        dq_ref[rows, :] = (jnp.concatenate(dq_parts, axis=0) * HEAD_DIM**-0.5).astype(BF16).T
    dk1_ref[...] = dk_sum[:half, :]
    dk2_ref[...] = dk_sum[half:, :].astype(BF16)
    dv1_ref[...] = dv_sum[:half, :]
    dv2_ref[...] = dv_sum[half:, :].astype(BF16)


def attend_back(queries, k1, k2, v1, v2, lse, mixed_grad, first, groups):
    tokens = queries.shape[0]
    keys = k1.shape[0]
    tile = min(512, tokens)
    width = groups * GROUP
    lse_spec = pl.BlockSpec((1, GROUP_HEADS, tokens), lambda g: (first + g, 0, 0))
    return pl.pallas_call(
        functools.partial(attend_back_kernel, tile),
        grid=(groups,),
        in_specs=[group_columns(tokens, first)]
        + [group_columns(keys, first)] * 4
        + [lse_spec, group_columns(tokens, first)],
        out_specs=[group_columns(tokens)] + [group_columns(keys)] * 4,
        out_shape=[
            jax.ShapeDtypeStruct((tokens, width), BF16),
            jax.ShapeDtypeStruct((keys, width), F32),
            jax.ShapeDtypeStruct((keys, width), BF16),
            jax.ShapeDtypeStruct((keys, width), F32),
            jax.ShapeDtypeStruct((keys, width), BF16),
        ],
        scratch_shapes=[
            pltpu.VMEM((2 * keys, GROUP_HEADS * tile), BF16),
            pltpu.VMEM((2 * keys, GROUP_HEADS * tile), BF16),
            pltpu.VMEM((2 * keys, GROUP), F32),
            pltpu.VMEM((2 * keys, GROUP), F32),
        ],
        compiler_params=KERNEL,
        cost_estimate=cost(8 * 10**9 * groups, 4 * 2**20 * groups),
        name="attend_back",
    )(queries, k1, k2, v1, v2, lse, mixed_grad)


def gelu_and_slope(upward):
    size = jnp.abs(upward) * (2.0**-0.5)
    bell = jnp.exp(-0.5 * (upward * upward))
    t = 1.0 / (1.0 + 0.3275911 * size)
    series = t * (
        0.254829592
        + t * (-0.284496736 + t * (1.421413741 + t * (-1.453152027 + t * 1.061405429)))
    )
    tail = 0.5 * series * bell
    cdf = jnp.where(upward >= 0, 1.0 - tail, tail)
    return upward * cdf, cdf + upward * (bell * (2 * math.pi) ** -0.5)


def up_kernel(rows_ref, weight_ref, bias_ref, active_ref, slope_ref):
    upward = jnp.dot(rows_ref[...], weight_ref[...], preferred_element_type=F32)
    active, slope = gelu_and_slope(upward + bias_ref[...].astype(F32))
    active_ref[...] = active.astype(BF16)
    slope_ref[...] = slope.astype(BF16)


def up_project(rows_in, weight, bias):
    tokens, width = rows_in.shape
    columns = weight.shape[1]
    step = 512
    by_column = lambda rows: pl.BlockSpec((rows, step), lambda j: (0, j))
    return pl.pallas_call(
        up_kernel,
        grid=(columns // step,),
        in_specs=[pl.BlockSpec((tokens, width), lambda j: (0, 0)), by_column(width), by_column(1)],
        out_specs=[by_column(tokens)] * 2,
        out_shape=[jax.ShapeDtypeStruct((tokens, columns), BF16)] * 2,
        compiler_params=KERNEL,
        cost_estimate=cost(15 * 10**9, 17 * 2**20),
        name="up_project",
    )(rows_in, weight, bias.reshape(1, columns))


def place_kernel(place_ref, *refs):
    pieces, out_ref = refs[:-1], refs[-1]
    for i, piece in enumerate(pieces):
        start = pl.multiple_of(place_ref[i], 16)
        out_ref[pl.ds(start, piece.shape[0]), :] = piece[...]


def place(places, pieces):
    rows = sum(piece.shape[0] for piece in pieces)
    columns = pieces[0].shape[1]
    step = min(columns, 2**20 // rows)
    by_column = lambda n: pl.BlockSpec((n, step), lambda j, at: (0, j))
    return pl.pallas_call(
        place_kernel,
        grid_spec=pltpu.PrefetchScalarGridSpec(
            num_scalar_prefetch=1,
            grid=(columns // step,),
            in_specs=[by_column(piece.shape[0]) for piece in pieces],
            out_specs=by_column(rows),
        ),
        out_shape=jax.ShapeDtypeStruct((rows, columns), pieces[0].dtype),
        compiler_params=KERNEL,
        cost_estimate=cost(0, 4 * rows * columns),
        name="place",
    )(places, *pieces)


def grad_kernel(where_ref, left_ref, right_ref, far_left_ref, far_right_ref, out_ref):
    near = lax.dot_general(left_ref[...], right_ref[...], ROWS_ROWS, preferred_element_type=F32)
    far = lax.dot_general(far_left_ref[...], far_right_ref[...], ROWS_ROWS, preferred_element_type=F32)
    out_ref[...] = (near + far).astype(BF16)


def grad_rows(left, right, far_left, far_right, near_row, far_row, rows, first_column=0, columns=None):
    tokens = right.shape[0]
    columns = right.shape[1] if columns is None else columns
    step = 256
    row_steps = rows // step
    at_column = first_column // D
    where = jnp.stack([near_row // step, far_row // step]).astype(jnp.int32)
    return pl.pallas_call(
        grad_kernel,
        grid_spec=pltpu.PrefetchScalarGridSpec(
            num_scalar_prefetch=1,
            grid=(columns // D, row_steps),
            in_specs=[
                pl.BlockSpec((tokens, step), lambda j, i, at: (0, at[0] + i)),
                pl.BlockSpec((tokens, D), lambda j, i, at: (0, at_column + j)),
                pl.BlockSpec((tokens, step), lambda j, i, at: (0, at[1] + i)),
                pl.BlockSpec((tokens, D), lambda j, i, at: (0, at_column + j)),
            ],
            out_specs=pl.BlockSpec((step, D), lambda j, i, at: (j * row_steps + i, 0)),
        ),
        out_shape=jax.ShapeDtypeStruct((rows * columns // D, D), BF16),
        compiler_params=KERNEL,
        cost_estimate=cost(4 * tokens * rows * columns, 2 * (rows * columns + 2 * tokens * columns)),
        name="grad_rows",
    )(where, left, right, far_left, far_right)


def project(rows_in, matrix):
    return jnp.dot(rows_in, matrix, preferred_element_type=F32)


def project_back(rows_in, matrix):
    return lax.dot_general(rows_in, matrix, COLS_COLS, preferred_element_type=F32)


def normalise(residual):
    centered = residual - jnp.mean(residual, axis=-1, keepdims=True)
    scale = lax.rsqrt(jnp.mean(centered * centered, axis=-1, keepdims=True) + 1e-05)
    return centered * scale, scale


def normalise_back(unit, scale, gain, grad_rows_in):
    scaled = grad_rows_in * gain
    inner = jnp.mean(scaled * unit, axis=-1, keepdims=True)
    return scale * (scaled - jnp.mean(scaled, axis=-1, keepdims=True) - unit * inner)


def column_sum(rows_in):
    return jnp.sum(rows_in.astype(F32), axis=0)


def after(value, *others):
    return lax.optimization_barrier((value, *others))[0]


def dynamic_rows(array, start, rows):
    return lax.dynamic_slice_in_dim(array, start, rows, axis=0)


def per_device(
    n_dp,
    inputs,
    timestep,
    bucket_count,
    upstream,
    query_weight,
    key_weight,
    value_weight,
    output_weight,
    up_weight,
    down_weight,
    *vectors,
):
    device = lax.axis_index("fsdp")
    chip, core = device // 2, device % 2
    bucket = lax.axis_index("dp")

    def swap(value, axis, bit):
        size = 4 if axis == "fsdp" else n_dp
        return lax.ppermute(value, axis, [(i, i ^ bit) for i in range(size)])

    def swap_core(value):
        return swap(value, "fsdp", 1)

    def swap_chip(value):
        return swap(value, "fsdp", 2)

    def split_pair(pair):
        mine = lax.dynamic_index_in_dim(pair, chip, keepdims=False)
        theirs = lax.dynamic_index_in_dim(pair, 1 - chip, keepdims=False)
        return mine, theirs

    def from_sequence(mine, received):
        order = lambda first, second: jnp.stack([first, second])
        return jnp.where(chip == 0, order(mine, received), order(received, mine))

    def fetch(shard, bit, *before):
        rows = shard.shape[0]
        side = (bucket // bit) % 2
        return swap_chip(after(dynamic_rows(shard, side * (rows // 2), rows // 2), *before))

    def gather(shard, first, bit):
        rows = shard.shape[0]
        side = (bucket // bit) % 2
        second = swap(first, "dp", bit)
        pieces = [shard, first, second]
        pieces = pieces + [swap_core(piece) for piece in pieces]
        far = device ^ 2
        places = []
        for flip in (0, 1):
            places += [
                (device ^ flip) * rows,
                (far ^ flip) * rows + side * (rows // 2),
                (far ^ flip) * rows + (1 - side) * (rows // 2),
            ]
        return place(jnp.stack(places).astype(jnp.int32), pieces)

    y_bit, z_bit = 1, min(2, n_dp // 2)
    tokens_mine, tokens_theirs = split_pair(inputs)
    tokens = jnp.concatenate([tokens_mine, swap_chip(tokens_theirs)], axis=0)
    qkv_weight = jnp.concatenate([query_weight, key_weight, value_weight], axis=1)
    qkv_first = fetch(qkv_weight, y_bit)
    qkv_full = gather(qkv_weight, qkv_first, y_bit)
    small = jnp.concatenate(vectors)
    pair = jnp.stack([small, swap_chip(small)])
    quad = jnp.stack([pair, swap_core(pair)])
    shares = [quad[i & 1, i >> 1] for i in range(4)]
    ordered = [
        jnp.where(device == 0, shares[i], jnp.where(device == 1, shares[i ^ 1], jnp.where(device == 2, shares[i ^ 2], shares[i ^ 3])))
        for i in range(4)
    ]
    full, at = [], 0
    for vector in vectors:
        n = vector.shape[0]
        full.append(jnp.concatenate([share[at : at + n] for share in ordered]).astype(F32))
        at += n
    query_bias, value_bias, output_bias, up_bias, down_bias, gain1, shift1, gain2, shift2 = full
    output_first = fetch(output_weight, z_bit, tokens)
    up_first = fetch(up_weight, z_bit, tokens)
    down_first = fetch(down_weight, y_bit, qkv_first)
    output_full = gather(output_weight, output_first, z_bit)
    up_full = gather(up_weight, up_first, z_bit)
    down_full = gather(down_weight, down_first, y_bit)
    upstream_mine, upstream_theirs = split_pair(upstream)
    upstream_theirs = after(upstream_theirs, output_first)
    cotangent_rows = jnp.concatenate([upstream_mine, swap_chip(upstream_theirs)], axis=0)

    embedding = lax.dynamic_index_in_dim(sinusoid(timestep), chip, keepdims=False)
    hidden = tokens.astype(F32) + embedding[None, :]
    rounded = hidden.astype(BF16)
    key_rows = project(rounded, qkv_full[:, D : 2 * D]).astype(BF16)
    values = (project(rounded, qkv_full[:, 2 * D :]) + value_bias).astype(BF16)
    far_keys, far_values = swap_core(key_rows), swap_core(values)
    queries = (project(rounded, qkv_full[:, :D]) + query_bias).astype(BF16)
    mixed, lse = attend(queries, key_rows, far_keys, values, far_values)

    unit1, scale1 = normalise(hidden + (project(mixed, output_full) + output_bias))
    first_norm = unit1 * gain1 + shift1
    first_low = first_norm.astype(BF16)
    activated, slope = up_project(first_low, up_full, up_bias)
    unit2, scale2 = normalise(first_norm + (project(activated, down_full) + down_bias))
    activations = (unit2 * gain2 + shift2).astype(BF16)
    split = inputs.shape[1]

    live = chip < bucket_count[bucket]
    seq_weight = live.astype(F32) * (2 * n_dp / jnp.sum(bucket_count).astype(F32))
    cotangent = cotangent_rows.astype(F32) * seq_weight
    gain2_part = column_sum(cotangent * unit2)
    shift2_part = column_sum(cotangent)
    second_grad = normalise_back(unit2, scale2, gain2, cotangent)
    down_delta = second_grad.astype(BF16)
    down_bias_part = column_sum(down_delta)

    low_bits = [bit for bit in (1, 2) if bit < n_dp]
    high_bits = [1 << i for i in range(2, n_dp.bit_length()) if 1 << i < n_dp]
    sides = [(bucket // bit) % 2 for bit in low_bits]

    def both_cores(left, right):
        rows = left.shape[1] // 4
        away = jnp.concatenate(
            [
                lax.dynamic_slice_in_dim(left, (2 * i + 1 - core) * rows, rows, axis=1)
                for i in (0, 1)
            ],
            axis=1,
        )
        return left, right, swap_core(away), swap_core(right)

    def grad_part(sides_of, to_chip, rows, first_row=0, **columns):
        whole = sides_of[0].shape[1] // 4
        near, far = (2 * to_chip + core) * whole + first_row, to_chip * whole + first_row
        return grad_rows(*sides_of, near, far, rows, **columns)

    def fold(mine, received, level):
        half = mine.shape[0] // 2
        side = sides[level]
        add = lambda start: (
            dynamic_rows(mine, start, half).astype(F32) + dynamic_rows(received, start, half).astype(F32)
        ).astype(BF16)
        return add(side * half), add((1 - side) * half)

    def finish(mine, received):
        for level in range(1, len(low_bits)):
            mine, away = fold(mine, received, level)
            received = swap(away, "dp", low_bits[level])
        total = (mine.astype(F32) + received.astype(F32)).astype(BF16)
        for bit in high_bits:
            total = (total.astype(F32) + swap(total, "dp", bit).astype(F32)).astype(BF16)
        for bit, side in reversed(list(zip(low_bits, sides))):
            other = swap(total, "dp", bit)
            total = jnp.where(side == 0, jnp.stack([total, other]), jnp.stack([other, total])).reshape(-1, total.shape[1])
        return total.astype(F32)

    class Chunk:
        def __init__(self, make):
            self.sent = make(1 - chip)
            self.make = make
            self.received = swap_chip(self.sent)

        def second(self):
            self.mine, self.away = fold(self.make(chip), self.received, 0)
            self.arrived = swap(self.away, "dp", low_bits[0])
            return self.away

        def result(self):
            return finish(self.mine, self.arrived)

    down_sides = both_cores(activated, down_delta)
    half_rows = activated.shape[1] // 8
    up_grad_in = project_back(down_delta, down_full)
    up_delta = (up_grad_in * slope.astype(F32)).astype(BF16)
    up_bias_part = column_sum(up_delta)
    down1 = Chunk(lambda to: grad_part(down_sides, to, half_rows))
    down2 = Chunk(lambda to: grad_part(down_sides, to, half_rows, half_rows))
    up_sides = both_cores(first_low, up_delta)
    up_delta = after(up_delta, down1.sent, down2.sent)
    up_columns = up_delta.shape[1] // 2
    up1 = Chunk(lambda to: grad_part(up_sides, to, D // 4, first_column=0, columns=up_columns))
    up2 = Chunk(lambda to: grad_part(up_sides, to, D // 4, first_column=up_columns, columns=up_columns))
    first_grad = second_grad + project_back(up_delta, up_full)
    gain1_part = column_sum(first_grad * unit1)
    shift1_part = column_sum(first_grad)
    first_input_grad = normalise_back(unit1, scale1, gain1, first_grad)
    out_delta = first_input_grad.astype(BF16)
    output_bias_part = column_sum(out_delta)
    mixed_grad = project_back(out_delta, output_full).astype(BF16)
    output_sides = both_cores(mixed, out_delta)
    output1 = Chunk(lambda to: grad_part(output_sides, to, D // 4))
    mixed_grad = after(mixed_grad, up1.sent, up2.sent, down1.second())
    activations_away = after(activations[split:], output1.sent)

    qkv_forward = (queries, key_rows, far_keys, values, far_values, lse)
    groups = D // GROUP // 2
    first_half = attend_back(*qkv_forward, mixed_grad, 0, groups)
    mixed_grad = after(mixed_grad, first_half[0], down2.second(), down1.arrived, output1.sent)
    second_half = attend_back(*qkv_forward, mixed_grad, groups, groups)
    query_delta, dk_mine, dk_far, dv_mine, dv_far = [
        jnp.concatenate(halves, axis=1) for halves in zip(first_half, second_half)
    ]
    key_delta = (dk_mine + swap_core(dk_far).astype(F32)).astype(BF16)
    value_delta = (dv_mine + swap_core(dv_far).astype(F32)).astype(BF16)
    query_bias_part = column_sum(query_delta)
    value_bias_part = column_sum(value_delta)
    deltas = jnp.concatenate([query_delta, key_delta, value_delta], axis=1)
    qkv_sides = both_cores(rounded, deltas)
    qkv1 = Chunk(lambda to: grad_part(qkv_sides, to, D // 4, first_column=0, columns=2 * D))
    qkv2 = Chunk(lambda to: grad_part(qkv_sides, to, D // 4, first_column=2 * D, columns=D))
    for chunk in (up1, up2, output1, qkv1, qkv2):
        chunk.second()
    deltas = after(deltas, qkv1.sent, qkv2.sent)
    input_grad = first_input_grad + project_back(deltas, qkv_full)
    received = swap_chip(input_grad[split:].astype(BF16)).astype(F32)
    input_gradient = from_sequence(input_grad[:split], received)
    activations_out = from_sequence(activations[:split], swap_chip(activations_away))

    time_sum = column_sum(input_grad)
    time_sum = time_sum + swap_core(time_sum)
    time_both = from_sequence(time_sum, swap_chip(time_sum))
    time_gradient = lax.dynamic_slice_in_dim(time_both, device * (D // 4), D // 4, axis=1)

    parts = [
        query_bias_part, value_bias_part, output_bias_part, up_bias_part, down_bias_part,
        gain1_part, shift1_part, gain2_part, shift2_part,
    ]
    packed = jnp.concatenate(parts).reshape(-1, 128)
    for axis, size in (("fsdp", 4), ("dp", n_dp)):
        bit = 1
        while bit < size:
            packed = packed + swap(packed, axis, bit)
            bit *= 2
    packed = packed.reshape(-1)
    vector_grads, at = [], 0
    for part in parts:
        n = part.shape[0]
        vector_grads.append(lax.dynamic_slice_in_dim(packed[at : at + n], device * (n // 4), n // 4))
        at += n

    qkv_total = qkv1.result()
    up_total = jnp.concatenate([up1.result(), up2.result()]).reshape(-1, D // 4, D)
    return (
        activations_out,
        input_gradient,
        time_gradient,
        qkv_total[: D // 4],
        qkv_total[D // 4 :],
        qkv2.result(),
        output1.result(),
        up_total.transpose(1, 0, 2).reshape(D // 4, -1),
        jnp.concatenate([down1.result(), down2.result()], axis=0),
        *vector_grads,
    )


def solution(mesh):
    rows, wide, flat = P("dp", "fsdp", None), P("fsdp", None), P("fsdp")
    return jax.shard_map(
        functools.partial(per_device, mesh.shape["dp"]),
        mesh=mesh,
        in_specs=(rows, P("dp"), P(), rows) + (wide,) * 6 + (flat,) * 9,
        out_specs=(rows, rows, P("dp", "fsdp")) + (wide,) * 6 + (flat,) * 9,
        check_vma=False,
    )
```

```python
import functools
import math

import jax
import jax.numpy as jnp
from jax import lax
from jax.experimental import pallas as pl
from jax.experimental.pallas import tpu as pltpu
from jax.sharding import PartitionSpec as P

D = 1024
HEAD_DIM = 64
GROUP = 256
GROUP_HEADS = GROUP // HEAD_DIM
F32 = jnp.float32
BF16 = jnp.bfloat16
ROWS_ROWS = (((0,), (0,)), ((), ()))
COLS_COLS = (((1,), (1,)), ((), ()))
ANY = pl.BlockSpec(memory_space=pl.ANY)
VMEM_MB = 60
COST = 10**11
MICROSECONDS = dict(
    pick=2, cut=2, pack=3, split=2, copy=2, relay=2, columns=2, remote=3, key_value=7, query=4, attend=9, output=6,
    up=13, down=11, up_delta=8, first=11, grad_x=8, grad_y=5, grad_z=3, grad_add=2, grad_join=3,
    grad_out=3, attend_back=15, delta=5, input=8, lines_in=2, lines=2, lines_add=1, pair=3,
)


def run_kernel(place, name, body, grid, ins, outs, later_than=(), scratch=(), aliases=None, vmem=16):
    count, waits = len(ins), len(later_than)

    def kernel(*refs):
        body(*refs[: 1 + count], *refs[1 + count + waits :])

    spec = lambda block, index: ANY if block is None else pl.BlockSpec(block, index)
    shapes = [jax.ShapeDtypeStruct(shape, dtype) for shape, dtype, _, _ in outs]
    out_specs = [spec(block, index) for _, _, block, index in outs]
    single = len(outs) == 1
    return pl.pallas_call(
        kernel,
        grid_spec=pltpu.PrefetchScalarGridSpec(
            num_scalar_prefetch=1,
            grid=grid,
            in_specs=[spec(block, index) for _, block, index in ins] + [ANY] * waits,
            out_specs=out_specs[0] if single else out_specs,
            scratch_shapes=list(scratch),
        ),
        out_shape=shapes[0] if single else shapes,
        input_output_aliases={1 + i: o for i, o in (aliases or {}).items()},
        compiler_params=pltpu.CompilerParams(vmem_limit_bytes=max(vmem, VMEM_MB) * 2**20),
        cost_estimate=pl.CostEstimate(flops=int(MICROSECONDS[name] * COST), bytes_accessed=0, transcendentals=0),
        name=name,
    )(place, *[array for array, _, _ in ins], *later_than)


CHIP, CORE, SIDE_Y, SIDE_Z = range(4)
LINES = 16
QUERY_BIAS, VALUE_BIAS, OUTPUT_BIAS, DOWN_BIAS, GAIN1, SHIFT1, GAIN2, SHIFT2, EMBED, WEIGHT = range(10)


def device_of(at):
    return 2 * at[CHIP] + at[CORE]


def their(flip, at):
    return 2 * (at[CHIP] ^ flip) + (at[CORE] ^ 1)


def line(lines_ref, i):
    return lines_ref[i : i + 1, :]


def whole(array):
    return (array, array.shape, lambda *_: (0,) * array.ndim)


def whole_out(shape, dtype):
    return (shape, dtype, shape, lambda *_: (0,) * len(shape))


def sinusoid(timestep):
    halves = D // 2
    frequency = jnp.exp(jnp.arange(halves, dtype=F32) * (-math.log(10000.0) / halves))
    angles = timestep.astype(F32)[:, None] * frequency[None, :]
    return jnp.concatenate([jnp.sin(angles), jnp.cos(angles)], axis=1)


def dot(left, right):
    return jnp.dot(left, right, preferred_element_type=F32)


def dot_back(left, right):
    return lax.dot_general(left, right, COLS_COLS, preferred_element_type=F32)


def outer(left, right):
    return lax.dot_general(left, right, ROWS_ROWS, preferred_element_type=F32)


def total(rows):
    return jnp.sum(rows, axis=0, keepdims=True)


def mean(rows):
    return jnp.mean(rows, axis=-1, keepdims=True)


def normalise(residual):
    centered = residual - mean(residual)
    scale = lax.rsqrt(mean(centered * centered) + 1e-05)
    return centered * scale, scale


def normalise_back(unit, scale, gain, grad):
    scaled = grad * gain
    return scale * (scaled - mean(scaled) - unit * mean(scaled * unit))


def gelu_and_slope(upward):
    size = jnp.abs(upward) * (2.0**-0.5)
    bell = jnp.exp(-0.5 * (upward * upward))
    t = 1.0 / (1.0 + 0.3275911 * size)
    series = t * (
        0.254829592
        + t * (-0.284496736 + t * (1.421413741 + t * (-1.453152027 + t * 1.061405429)))
    )
    tail = 0.5 * series * bell
    cdf = jnp.where(upward >= 0, 1.0 - tail, tail)
    return upward * cdf, cdf + upward * (bell * (2 * math.pi) ** -0.5)


def order_rows(at, pieces, weight_ref):
    for flip, piece in zip((0, 2, 1, 3), pieces):
        rows = piece.shape[0]
        start = pl.multiple_of((device_of(at) ^ flip) * rows, 16)
        weight_ref[pl.ds(start, rows), :] = piece[...]
    return weight_ref[...]


def pieces_in(pieces, step, firsts):
    return [(piece, (piece.shape[0], step), lambda j, *_, k=k: (0, k + j)) for piece, k in zip(pieces, firsts)]


def lines_in_kernel(at, shares_ref, embeds_ref, weight_ref, lines_ref, up_ref):
    devices, _, share = shares_ref.shape
    for i in range(devices):
        values = shares_ref[i].astype(F32)
        extra = values.shape[0] - 8
        place = slice(i * share, (i + 1) * share)
        lines_ref[0:3, place] = values[0:3, :]
        lines_ref[3:8, place] = values[3 + extra :, :]
        for e in range(extra):
            start = (i * extra + e) * share
            up_ref[:, start : start + share] = values[3 + e : 4 + e, :]
    lines_ref[EMBED : EMBED + 1, :] = embeds_ref[pl.ds(at[CHIP], 1), :]
    lines_ref[WEIGHT:LINES, :] = jnp.broadcast_to(weight_ref[...], (LINES - WEIGHT, D))


def key_value_kernel(at, mine_ref, got_ref, lines_ref, *refs):
    *pieces, keys_ref, values_ref, weight_ref, rounded_ref = refs
    j = pl.program_id(0)

    @pl.when(j == 0)
    def _():
        half = mine_ref.shape[0]
        embed = line(lines_ref, EMBED)
        rounded_ref[:half, :] = (mine_ref[...].astype(F32) + embed).astype(BF16)
        rounded_ref[half:, :] = (got_ref[...].astype(F32) + embed).astype(BF16)

    product = dot(rounded_ref[...], order_rows(at, pieces, weight_ref))

    @pl.when(j == 0)
    def _():
        keys_ref[...] = product.astype(BF16)

    @pl.when(j == 1)
    def _():
        values_ref[...] = (product + line(lines_ref, VALUE_BIAS)).astype(BF16)


def query_kernel(at, rounded_ref, lines_ref, *refs):
    *pieces, _, out_ref, weight_ref = refs
    weight = order_rows(at, pieces, weight_ref)
    out_ref[...] = (dot(rounded_ref[...], weight) + line(lines_ref, QUERY_BIAS)).astype(BF16)


def head_mask(head):
    return lax.broadcasted_iota(jnp.int32, (1, GROUP), 1) // HEAD_DIM == head


def attend_kernel(_, q_ref, k1_ref, v1_ref, k2_ref, v2_ref, __, out_ref, lse_ref):
    keys = jnp.concatenate([k1_ref[...], k2_ref[...]], axis=0)
    values_t = jnp.concatenate([v1_ref[...], v2_ref[...]], axis=0).T
    queries = q_ref[...] * jnp.asarray(HEAD_DIM**-0.5, BF16)
    outs = []
    for head in range(GROUP_HEADS):
        masked = jnp.where(head_mask(head), queries, jnp.zeros_like(queries))
        scores = dot_back(keys, masked)
        peak = jnp.max(scores, axis=0, keepdims=True)
        exponent = jnp.exp(scores - peak)
        summed = total(exponent)
        attention = (exponent * (1.0 / summed)).astype(BF16)
        lse_ref[0, head : head + 1, :] = peak + jnp.log(summed)
        outs.append(dot(values_t[head * HEAD_DIM : (head + 1) * HEAD_DIM, :], attention))
    out_ref[...] = jnp.concatenate(outs, axis=0).astype(BF16).T


def output_kernel(at, rounded_ref, mixed_ref, mine_ref, got_ref, lines_ref, *refs):
    *pieces, weight_ref, unit_ref, scale_ref, low_ref, away_ref = refs
    product = dot(mixed_ref[...], order_rows(at, pieces, weight_ref))
    half = mine_ref.shape[0]
    for start, tokens_ref in ((0, mine_ref), (half, got_ref)):
        place = pl.ds(start, half)
        hidden = tokens_ref[...].astype(F32) + line(lines_ref, EMBED)
        unit, scale = normalise(hidden + (product[start : start + half, :] + line(lines_ref, OUTPUT_BIAS)))
        unit_ref[place, :] = unit
        scale_ref[place, :] = scale
        low_ref[place, :] = (unit * line(lines_ref, GAIN1) + line(lines_ref, SHIFT1)).astype(BF16)
    width = D // 4
    for k, left_ref in enumerate((low_ref, rounded_ref, mixed_ref)):
        for flip in (1, 0):
            column = pl.multiple_of(their(flip, at) * width, width)
            block = 2 * k + 1 - flip
            away_ref[:, block * width : (block + 1) * width] = left_ref[:, pl.ds(column, width)]


def up_kernel(at, low_ref, bias_ref, *refs):
    *pieces, active_ref, slope_ref, weight_ref, send_ref, keep_ref = refs
    weight = order_rows(at, pieces, weight_ref)
    active, slope = gelu_and_slope(dot(low_ref[...], weight) + bias_ref[...])
    active_ref[...] = active.astype(BF16)
    slope_ref[...] = slope.astype(BF16)
    for flip, copy_ref in ((1, send_ref), (0, keep_ref)):

        @pl.when(pl.program_id(0) == their(flip, at))
        def _(copy_ref=copy_ref):
            copy_ref[...] = active_ref[...]


def down_kernel(_, active_ref, weight_ref, unit1_ref, mine_ref, got_ref, lines_ref, *refs):
    final_ref, away_ref, grad_ref, delta_ref, sums_ref, sum_ref = refs
    step = weight_ref.shape[1]
    j = pl.program_id(0)
    sum_ref[:, pl.ds(pl.multiple_of(j * step, step), step)] = dot(active_ref[...], weight_ref[...])

    @pl.when(j == pl.num_programs(0) - 1)
    def _():
        row = lambda i: line(lines_ref, i)
        half = mine_ref.shape[0]
        sums = [0.0, 0.0, 0.0]
        for start, upstream_ref, out_ref in ((0, mine_ref, final_ref), (half, got_ref, away_ref)):
            place = pl.ds(start, half)
            first_norm = unit1_ref[place, :] * row(GAIN1) + row(SHIFT1)
            unit, scale = normalise(first_norm + (sum_ref[place, :] + row(DOWN_BIAS)))
            out_ref[...] = (unit * row(GAIN2) + row(SHIFT2)).astype(BF16)
            cotangent = upstream_ref[...].astype(F32) * row(WEIGHT)
            grad = normalise_back(unit, scale, row(GAIN2), cotangent)
            delta = grad.astype(BF16)
            grad_ref[place, :] = grad
            delta_ref[place, :] = delta
            parts = (cotangent * unit, cotangent, delta.astype(F32))
            sums = [one + total(part) for one, part in zip(sums, parts)]
        for i, one in enumerate(sums):
            sums_ref[i : i + 1, :] = one


def up_delta_kernel(_, delta_ref, weight_ref, slope_ref, out_ref, sums_ref):
    delta = (dot_back(delta_ref[...], weight_ref[...]) * slope_ref[...].astype(F32)).astype(BF16)
    out_ref[...] = delta
    sums_ref[pl.ds(pl.program_id(0), 1), :] = total(delta.astype(F32))


def first_kernel(_, delta_ref, weight_ref, grad_ref, unit_ref, scale_ref, lines_ref, output_ref, *refs):
    input_ref, out_ref, rights_ref, mixed_ref, sums_ref, sum_ref = refs
    j = pl.program_id(0)
    part = dot_back(delta_ref[...], weight_ref[...])

    @pl.when(j == 0)
    def _():
        sum_ref[...] = grad_ref[...] + part

    @pl.when(j > 0)
    def _():
        sum_ref[...] += part

    @pl.when(j == pl.num_programs(0) - 1)
    def _():
        half = sum_ref.shape[0] // 2
        sums = [0.0, 0.0, 0.0]
        for start in (0, half):
            place = pl.ds(start, half)
            grad, unit = sum_ref[place, :], unit_ref[place, :]
            below = normalise_back(unit, scale_ref[place, :], line(lines_ref, GAIN1), grad)
            delta = below.astype(BF16)
            input_ref[place, :] = below
            out_ref[place, :] = delta
            rights_ref[place, :] = delta
            mixed_ref[place, :] = dot_back(delta, output_ref[...]).astype(BF16)
            parts = (grad * unit, grad, delta.astype(F32))
            sums = [one + total(part) for one, part in zip(sums, parts)]
        for i, one in enumerate(sums):
            sums_ref[i : i + 1, :] = one


def attend_back_kernel(
    _, q_ref, k1_ref, v1_ref, k2_ref, v2_ref, lse_ref, grad_ref, __, ___, dq_ref, rights_ref, near_ref, far_ref, p_all, ds_all
):
    half, tokens = k1_ref.shape[0], q_ref.shape[0]
    keys = jnp.concatenate([k1_ref[...], k2_ref[...]], axis=0)
    values = jnp.concatenate([v1_ref[...], v2_ref[...]], axis=0)
    keys_t = keys.T
    queries = q_ref[...] * jnp.asarray(HEAD_DIM**-0.5, BF16)
    grads = grad_ref[...]
    query_parts, grad_parts, dq_parts = [], [], []
    for head in range(GROUP_HEADS):
        query_one = jnp.where(head_mask(head), queries, jnp.zeros_like(queries))
        grad_one = jnp.where(head_mask(head), grads, jnp.zeros_like(grads))
        attention = jnp.exp(dot_back(keys, query_one) - lse_ref[0, head : head + 1, :])
        prob_grad = dot_back(values, grad_one)
        weighted = total(attention * prob_grad)
        score_grad = (attention * (prob_grad - weighted)).astype(BF16)
        place = slice(head * tokens, (head + 1) * tokens)
        p_all[:, place] = attention.astype(BF16)
        ds_all[:, place] = score_grad
        dq_parts.append(dot(keys_t[head * HEAD_DIM : (head + 1) * HEAD_DIM, :], score_grad))
        query_parts.append(query_one)
        grad_parts.append(grad_one)
    value_grad = dot(p_all[...], jnp.concatenate(grad_parts, axis=0))
    key_grad = dot(ds_all[...], jnp.concatenate(query_parts, axis=0))
    dq_ref[...] = (jnp.concatenate(dq_parts, axis=0) * HEAD_DIM**-0.5).astype(BF16).T
    rights_ref[...] = dq_ref[...]
    near_ref[:, :GROUP] = key_grad[:half, :]
    near_ref[:, GROUP:] = value_grad[:half, :]
    far_ref[:, :GROUP] = key_grad[half:, :].astype(BF16)
    far_ref[:, GROUP:] = value_grad[half:, :].astype(BF16)


def delta_kernel(_, *refs):
    groups = D // GROUP
    nears, fars = refs[:groups], refs[groups : 2 * groups]
    queries_ref, __, keys_ref, values_ref, rights_ref, sums_ref = refs[2 * groups :]
    i = pl.program_id(0)
    for g in range(groups):
        place = slice(g * GROUP, (g + 1) * GROUP)
        rights_ref[:, place] = (nears[g][...] + fars[g][...].astype(F32)).astype(BF16)
    sums_ref[pl.ds(1 + i, 1), :] = total(rights_ref[...].astype(F32))

    @pl.when(i == 0)
    def _():
        sums_ref[0:1, :] = total(queries_ref[...].astype(F32))
        keys_ref[...] = rights_ref[...]

    @pl.when(i == 1)
    def _():
        values_ref[...] = rights_ref[...]


def input_kernel(_, delta_ref, weight_ref, grad_ref, mine_ref, away_ref, time_ref, sum_ref):
    j = pl.program_id(0)
    part = dot_back(delta_ref[...], weight_ref[...])

    @pl.when(j == 0)
    def _():
        sum_ref[...] = grad_ref[...] + part

    @pl.when(j > 0)
    def _():
        sum_ref[...] += part

    @pl.when(j == pl.num_programs(0) - 1)
    def _():
        half = mine_ref.shape[0]
        mine_ref[...] = sum_ref[:half, :]
        away_ref[...] = sum_ref[half:, :].astype(BF16)
        time_ref[...] = total(sum_ref[...])


def grad_block(which, left_ref, right_ref, far_left_ref, fars, sum_ref, *more):
    for k, far_ref in enumerate(fars):

        @pl.when((which == k) if len(fars) > 1 else (which >= 0))
        def _(far_ref=far_ref):
            sum_ref[...] = outer(far_left_ref[...], far_ref[...])

    block = outer(left_ref[...], right_ref[...]) + sum_ref[...]
    for one_ref in more:
        block = block + one_ref[...].astype(F32)
    return block.astype(BF16)


def grad_x_kernel(_, left_ref, right_ref, far_left_ref, *refs):
    *fars, out_ref, sum_ref = refs
    out_ref[...] = grad_block(pl.program_id(0), left_ref, right_ref, far_left_ref, fars, sum_ref)


def grad_y_kernel(at_ref, left_ref, right_ref, far_left_ref, other_ref, *refs):
    *fars, away_ref, keep_ref, sum_ref = refs
    i, half = pl.program_id(0), pl.num_programs(0) // 2
    which = jnp.where(i < half, 1 - at_ref[SIDE_Y], at_ref[SIDE_Y])
    block = grad_block(which, left_ref, right_ref, far_left_ref, fars, sum_ref, other_ref)

    @pl.when(i < half)
    def _():
        away_ref[...] = block

    @pl.when(i >= half)
    def _():
        keep_ref[...] = block


def fold_kernel(_, keep1_ref, keep2_ref, away1_ref, away2_ref, keep_ref, away_ref):
    keep_ref[...] = (keep1_ref[...].astype(F32) + keep2_ref[...].astype(F32)).astype(BF16)
    away_ref[...] = (away1_ref[...].astype(F32) + away2_ref[...].astype(F32)).astype(BF16)


def add_kernel(_, one_ref, two_ref, out_ref):
    out_ref[...] = (one_ref[...].astype(F32) + two_ref[...].astype(F32)).astype(out_ref.dtype)


def join_kernel(at_ref, mine_ref, other_ref, out_ref):
    rows = mine_ref.shape[0]
    out_ref[pl.ds(pl.multiple_of(at_ref[SIDE_Z] * rows, 16), rows), :] = mine_ref[...]
    out_ref[pl.ds(pl.multiple_of((1 - at_ref[SIDE_Z]) * rows, 16), rows), :] = other_ref[...]


def finish_kernel(_, mine_ref, other_ref, *refs):
    out_ref = refs[-1]
    i, half = pl.program_id(0), pl.num_programs(0) // 2

    @pl.when(i < half)
    def _():
        out_ref[...] = mine_ref[...].astype(F32)

    @pl.when(i >= half)
    def _():
        out_ref[...] = other_ref[...].astype(F32)


def copy_kernel(_, in_ref, out_ref):
    out_ref[...] = in_ref[...]


def pair_kernel(_, mine_ref, received_ref, out_ref):
    @pl.when(pl.program_id(0) == 0)
    def _():
        out_ref[...] = mine_ref[...]

    @pl.when(pl.program_id(0) == 1)
    def _():
        out_ref[...] = received_ref[...].astype(out_ref.dtype)


def side_by_side_kernel(_, *refs):
    out_ref, at = refs[-1], 0
    for piece in refs[:-1]:
        out_ref[:, at : at + piece.shape[1]] = piece[...]
        at += piece.shape[1]


def split_kernel(_, in_ref, first_ref, second_ref):
    rows = first_ref.shape[0]
    first_ref[...] = in_ref[:rows, :]
    second_ref[...] = in_ref[rows:, :]


def parity(at):
    return (at[SIDE_Y] + at[SIDE_Z]) % 2


def remote_kernel(at, half_ref, third_ref, fourth_ref, *outs):
    columns = 0
    for out_ref in outs:
        width = out_ref.shape[1]
        place = slice(columns, columns + width)
        columns += width
        remote_rows(at, half_ref.at[:, place], third_ref.at[:, place], fourth_ref.at[:, place], out_ref)


def remote_rows(at, half_ref, third_ref, fourth_ref, out_ref):
    half, quarter = half_ref.shape[0], third_ref.shape[0]
    missing = (1 - parity(at)) * half
    out_ref[pl.ds(pl.multiple_of(parity(at) * half, 16), half), :] = half_ref[...]
    out_ref[pl.ds(pl.multiple_of(missing, 16), quarter), :] = third_ref[...]
    out_ref[pl.ds(pl.multiple_of(missing + quarter, 16), quarter), :] = fourth_ref[...]


def lines_kernel(at, down_ref, first_ref, delta_ref, up_ref, time_ref, out_ref):
    out_ref[0:8, :] = down_ref[...]
    out_ref[8:16, :] = first_ref[...]
    out_ref[16:24, :] = delta_ref[...]
    out_ref[24:28, :] = up_ref[0:4, :]
    row = lax.broadcasted_iota(jnp.int32, (4, D), 0)
    out_ref[28:32, :] = jnp.where(row == at[CHIP], time_ref[...], 0.0)


def per_device(n_dp, inputs, timestep, bucket_count, upstream, *params):
    query_weight, key_weight, value_weight, output_weight, up_weight, down_weight = params[:6]
    vectors = params[6:]
    device = lax.axis_index("fsdp")
    chip, core = device // 2, device % 2
    bucket = lax.axis_index("dp")
    half = inputs.shape[1]
    tokens = 2 * half
    hidden_width = up_weight.shape[1]
    side_y, side_z = bucket % 2, (bucket // 2) % 2
    place = jnp.stack([chip, core, side_y, side_z]).astype(jnp.int32)
    run = functools.partial(run_kernel, place)

    def swap(value, axis, bit):
        size = 4 if axis == "fsdp" else n_dp
        return lax.ppermute(value, axis, [(i, i ^ bit) for i in range(size)])

    swap_core = lambda value: swap(value, "fsdp", 1)
    swap_chip = lambda value: swap(value, "fsdp", 2)
    swap_y = lambda value: swap(value, "dp", 1)
    swap_z = lambda value: swap(value, "dp", 2)

    def pick(array, flip, *later_than):
        _, rows, columns = array.shape
        ins = [(array, (None, rows, columns), lambda _, at: (at[CHIP] ^ flip, 0, 0))]
        return run("pick", copy_kernel, (1,), ins, [whole_out((rows, columns), array.dtype)], later_than)

    def pack(arrays, *later_than):
        shape = (arrays[0].shape[0], sum(array.shape[1] for array in arrays))
        return run("pack", side_by_side_kernel, (1,), [whole(a) for a in arrays], [whole_out(shape, BF16)], later_than)

    def cut(shards, *later_than):
        rows = shards[0].shape[0]
        columns = sum(shard.shape[1] for shard in shards)
        ins = [(shard, (rows // 2, shard.shape[1]), lambda _, at: (parity(at), 0)) for shard in shards]
        outs = [whole_out((rows // 2, columns), BF16)]
        return run("cut", side_by_side_kernel, (1,), ins, outs, later_than)

    def split(first, *later_than):
        rows, columns = first.shape
        outs = [whole_out((rows // 2, columns), BF16)] * 2
        to_y, to_z = run("split", split_kernel, (1,), [whole(first)], outs, later_than)
        return (first, swap_y(to_y), swap_z(to_z)), to_y

    def remote(parts, widths, *later_than):
        outs = [whole_out((2 * parts[0].shape[0], width), BF16) for width in widths]
        return run("remote", remote_kernel, (1,), [whole(part) for part in parts], outs, later_than)

    tokens_away = pick(inputs, 1)
    tokens_got = swap_chip(tokens_away)
    three = (query_weight, key_weight, value_weight)
    two_weights = (output_weight, up_weight)
    three_cut = cut(three, tokens_away)
    three_first = swap_chip(three_cut)
    three_own = pack(three, three_cut)
    three_sibling = swap_core(three_own)
    tokens_mine = pick(inputs, 0, three_own)
    two_own = pack(two_weights, tokens_mine)
    two_sibling = swap_core(two_own)
    down_copy = run("copy", copy_kernel, (1,), [whole(down_weight)], [whole_out(down_weight.shape, BF16)], (two_own,))
    two_cut = cut(two_weights, tokens_got, down_copy)
    two_first = swap_chip(two_cut)
    small = jnp.concatenate([vector.reshape(-1, D // 4) for vector in vectors], axis=0)
    live = chip < bucket_count[bucket]
    seq_weight = live.astype(F32) * (2 * n_dp / jnp.sum(bucket_count).astype(F32))
    small_all = lax.all_gather(small, "fsdp")
    three_parts, split_done = split(three_first, three_sibling, two_sibling, two_cut, small_all)
    down_matrix = lax.all_gather(down_copy, "fsdp", axis=0, tiled=True)
    lines, up_bias = run(
        "lines_in", lines_in_kernel, (1,),
        [whole(a) for a in (small_all, sinusoid(timestep), seq_weight.reshape(1, 1))],
        [whole_out((LINES, D), F32), whole_out((1, hidden_width), F32)], (split_done,),
    )
    query_remote, kv_remote = remote(three_parts, (D, 2 * D), lines)
    upstream_mine = pick(upstream, 0, kv_remote)
    kv_pieces = [three_own, kv_remote, three_sibling, swap_core(kv_remote)]
    query_pieces = [three_own, query_remote, three_sibling, swap_core(query_remote)]
    keys, values, qkv_matrix, lefts = run(
        "key_value", key_value_kernel, (2,),
        [whole(tokens_mine), whole(tokens_got), whole(lines)] + pieces_in(kv_pieces, D, (1, 0, 1, 0)),
        [
            whole_out((tokens, D), BF16),
            whole_out((tokens, D), BF16),
            ((D, 3 * D), BF16, (D, D), lambda j, *_: (0, 1 + j)),
            ((tokens, 2 * D), BF16, (tokens, D), lambda j, *_: (0, 0)),
        ],
        (upstream_mine,),
    )
    far_keys, far_values = swap_core(keys), swap_core(values)
    queries, qkv_matrix = run(
        "query", query_kernel, (1,),
        [(lefts, (tokens, D), lambda j, *_: (0, 0)), whole(lines)] + pieces_in(query_pieces, D, (0, 0, 0, 0))
        + [(qkv_matrix, None, None)],
        [((tokens, D), BF16, (tokens, D), lambda j, *_: (0, 0)), ((D, 3 * D), BF16, (D, D), lambda j, *_: (0, 0))],
        aliases={2 + len(query_pieces): 1},
    )
    groups = D // GROUP
    group_of = lambda array, first: (array, (array.shape[0], GROUP), lambda g, *_: (0, first + g))

    def attend(first, count, lefts, *later_than):
        return run(
            "attend", attend_kernel, (count,),
            [group_of(a, first) for a in (queries, keys, values, far_keys, far_values)] + [(lefts, None, None)],
            [
                ((tokens, 2 * D), BF16, (tokens, GROUP), lambda g, *_: (0, groups + first + g)),
                ((count, GROUP_HEADS, tokens), F32, (1, GROUP_HEADS, tokens), lambda g, *_: (g, 0, 0)),
            ],
            later_than, aliases={5: 0}, vmem=32,
        )

    lefts, lse1 = attend(0, groups // 2, lefts)
    two_parts, split_done = split(two_first, lse1)
    lefts, lse2 = attend(groups // 2, groups // 2, lefts, split_done)
    two_remote = remote(two_parts, (two_own.shape[1],), lse2)
    upstream_away = pick(upstream, 1, two_remote)
    upstream_got = swap_chip(upstream_away)
    two_pieces = [two_own, two_remote, two_sibling, swap_core(two_remote)]
    output_matrix, unit1, scale1, first_low, lefts_away = run(
        "output", output_kernel, (1,),
        [(lefts, (tokens, D), lambda j, *_: (0, 0)), (lefts, (tokens, D), lambda j, *_: (0, 1))]
        + [whole(tokens_mine), whole(tokens_got), whole(lines)]
        + pieces_in(two_pieces, D, (0, 0, 0, 0)),
        [
            whole_out((D, D), BF16),
            whole_out((tokens, D), F32),
            whole_out((tokens, 1), F32),
            whole_out((tokens, D), BF16),
            whole_out((tokens, 6 * D // 4), BF16),
        ],
        (upstream_away,),
    )
    lefts_away = swap_core(lefts_away)
    step = hidden_width // 4
    steps = D // step
    activated, slope, up_matrix, active_send, active_keep = run(
        "up", up_kernel, (4,),
        [whole(first_low), (up_bias, (1, step), lambda j, *_: (0, j))] + pieces_in(two_pieces, step, [steps] * 4),
        [((tokens, hidden_width), BF16, (tokens, step), lambda j, *_: (0, j))] * 2
        + [((D, hidden_width), BF16, (D, step), lambda j, *_: (0, j))]
        + [whole_out((tokens, step), BF16)] * 2,
    )
    active_send, active_keep = swap_core(active_send), swap_core(active_keep)
    step = 512
    final_mine, final_away, second_grad, down_delta, down_sums = run(
        "down", down_kernel, (D // step,),
        [whole(activated), (down_matrix, (hidden_width, step), lambda j, *_: (0, j)), whole(unit1), whole(upstream_mine), whole(upstream_got)]
        + [whole(lines)],
        [
            whole_out((half, D), BF16),
            whole_out((half, D), BF16),
            whole_out((tokens, D), F32),
            whole_out((tokens, D), BF16),
            whole_out((8, D), F32),
        ],
        (lefts_away,), [pltpu.VMEM((tokens, D), F32)], vmem=48,
    )

    block_rows = D // 4

    class Grads:
        def __init__(self, left, right, send, keep, fars, near, right_column):
            self.left, self.right, self.send_far, self.keep_far = left, right, send, keep
            self.fars, self.near, self.right_column = fars, near, right_column

        def ins(self, flip, far, block):
            far_left, far_column = far
            shard = lambda at: 2 * (at[CHIP] ^ flip) + at[CORE]
            return [
                (self.left, (tokens, block_rows), lambda i, at: (0, self.near(shard(at), block(i, at)))),
                (self.right, (tokens, D), lambda i, at: (0, self.right_column(block(i, at)))),
                (far_left, (tokens, block_rows), lambda i, at: (0, far_column(block(i, at)))),
            ]

        def far_ins(self, block, first, count):
            if len(self.fars) > 1:
                return [whole(a) for a in self.fars[first : first + count]]
            return [(self.fars[0], (tokens, D), lambda i, at: (0, self.right_column(block(i, at))))]

        def four(self, name, body, flip, far, more, last):
            out = ((4 * block_rows, D), BF16, (block_rows, D), lambda i, at: (i, 0))
            block = lambda i, at: i
            ins = self.ins(flip, far, block) + more + self.far_ins(block, 0, 4)
            return run(name, body, (4,), ins, [out], (last,), [pltpu.VMEM((block_rows, D), F32)])

        def start(self, last):
            sent = self.four("grad_x", grad_x_kernel, 1, self.send_far, [], last)
            self.got = swap_chip(sent)
            return sent

    class Chunk:
        def __init__(self, grads, first, count):
            self.grads, self.first, self.half = grads, first, count // 2

        def over_y(self, last):
            grads, first, half = self.grads, self.first, self.half
            block = lambda i, at: first + jnp.where(
                i < half, (1 - at[SIDE_Y]) * half + i, at[SIDE_Y] * half + i - half
            )
            other = (grads.got, (block_rows, D), lambda i, at: (block(i, at), 0))
            shape = (half * block_rows, D)
            away, self.keep = run(
                "grad_y", grad_y_kernel, (2 * half,),
                grads.ins(0, grads.keep_far, block) + [other] + grads.far_ins(block, first, 2),
                [
                    (shape, BF16, (block_rows, D), lambda i, at: (jnp.minimum(i, half - 1), 0)),
                    (shape, BF16, (block_rows, D), lambda i, at: (jnp.maximum(i - half, 0), 0)),
                ],
                (last,), [pltpu.VMEM((block_rows, D), F32)],
            )
            self.got = swap_y(away)
            return self.keep

        def over_z(self, last):
            block = (self.keep.shape[0] // 2, D)
            kept = [(a, block, lambda _, at: (at[SIDE_Z], 0)) for a in (self.keep, self.got)]
            given = [(a, block, lambda _, at: (1 - at[SIDE_Z], 0)) for a in (self.keep, self.got)]
            self.keep, away = run("grad_z", fold_kernel, (1,), kept + given, [whole_out(block, BF16)] * 2, (last,))
            self.got = swap_z(away)
            return self.keep

        def add(self, bit, last):
            ins = [whole(self.keep), whole(self.got)]
            self.keep = run("grad_add", add_kernel, (1,), ins, [whole_out(self.keep.shape, BF16)], (last,))
            self.got = swap(self.keep, "dp", bit)
            return self.keep

        def add_high(self, last):
            for bit in high_bits:
                last = self.add(bit, last)
            return last

        def add_low(self, last):
            return self.add(2, last)

        def back(self, last):
            ins = [whole(self.keep), whole(self.got)]
            shape = (2 * self.keep.shape[0], D)
            self.keep = run("grad_join", join_kernel, (1,), ins, [whole_out(shape, BF16)], (last,))
            self.got = swap_y(self.keep)
            return self.keep

        def finish(self, last, shape, index):
            half = self.half
            ins = [
                (self.keep, (block_rows, D), lambda i, at: (jnp.minimum(i, half - 1), 0)),
                (self.got, (block_rows, D), lambda i, at: (jnp.maximum(i - half, 0), 0)),
            ]
            place = lambda i, at: jnp.where(i < half, at[SIDE_Y] * half + i, (1 - at[SIDE_Y]) * half + i - half)
            out = (shape, F32, (block_rows, D), lambda i, at: index(place(i, at)))
            return run("grad_out", finish_kernel, (2 * half,), ins, [out], (last,))

    def pair_of(mine, received, dtype, last):
        out = ((2, half, D), dtype, (None, half, D), lambda i, at: (at[CHIP] ^ i, 0, 0))
        return run("pair", pair_kernel, (2,), [whole(mine), whole(received)], [out], (last,))

    high_bits = [1 << i for i in range(2, n_dp.bit_length()) if 1 << i < n_dp]
    relay = lambda array, last: run("relay", copy_kernel, (1,), [whole(array)], [whole_out(array.shape, array.dtype)], (last,))

    down_far = swap_core(down_delta)
    step = 1024
    up_delta, up_sums = run(
        "up_delta", up_delta_kernel, (hidden_width // step,),
        [whole(down_delta), (down_matrix, (step, D), lambda j, *_: (j, 0)), (slope, (tokens, step), lambda j, *_: (0, j))],
        [((tokens, hidden_width), BF16, (tokens, step), lambda j, *_: (0, j)), whole_out((8, D), F32)],
        (active_send, active_keep),
    )
    up_far = swap_core(up_delta)
    four_blocks = hidden_width // D
    grads_down = Grads(
        activated, down_delta, (active_send, lambda b: b), (active_keep, lambda b: b), [down_far],
        lambda shard, b: shard * four_blocks + b, lambda b: 0,
    )
    last = grads_down.start(up_delta)
    grads_up = Grads(
        first_low, up_delta, (lefts_away, lambda b: 0), (lefts_away, lambda b: 1), [up_far],
        lambda shard, b: shard, lambda b: b,
    )
    last = grads_up.start(last)
    step = 1024
    input_part, out_delta, rights, mixed_grad, first_sums = run(
        "first", first_kernel, (hidden_width // step,),
        [
            (up_delta, (tokens, step), lambda j, *_: (0, j)),
            (up_matrix, (D, step), lambda j, *_: (0, j)),
            whole(second_grad), whole(unit1), whole(scale1),
            whole(lines), whole(output_matrix),
        ],
        [
            whole_out((tokens, D), F32),
            whole_out((tokens, D), BF16),
            ((tokens, 4 * D), BF16, (tokens, D), lambda j, *_: (0, 3)),
            whole_out((tokens, D), BF16),
            whole_out((8, D), F32),
        ],
        (last,), [pltpu.VMEM((tokens, D), F32)],
    )
    out_far = swap_core(out_delta)

    def attend_back(first, count, later_than, rights, query_delta):
        lse = lse1 if first == 0 else lse2
        return run(
            "attend_back", attend_back_kernel, (count,),
            [group_of(a, first) for a in (queries, keys, values, far_keys, far_values)]
            + [(lse, (1, GROUP_HEADS, tokens), lambda g, *_: (g, 0, 0)), group_of(mixed_grad, first)]
            + [(query_delta, None, None), (rights, None, None)],
            [
                ((tokens, D), BF16, (tokens, GROUP), lambda g, *_: (0, first + g)),
                ((tokens, 4 * D), BF16, (tokens, GROUP), lambda g, *_: (0, first + g)),
                ((tokens, 2 * count * GROUP), F32, (tokens, 2 * GROUP), lambda g, *_: (0, g)),
                ((tokens, 2 * count * GROUP), BF16, (tokens, 2 * GROUP), lambda g, *_: (0, g)),
            ],
            later_than, [pltpu.VMEM((2 * tokens, GROUP_HEADS * tokens), BF16)] * 2, aliases={7: 0, 8: 1},
        )

    per_call = groups // 2
    query_delta, rights, near1, far1 = attend_back(0, per_call, (mixed_grad,), rights, jnp.zeros((tokens, D), BF16))
    far1 = swap_core(far1)
    query_delta, rights, near2, far2 = attend_back(per_call, per_call, (near1, out_far), rights, query_delta)
    far2, query_far = swap_core(far2), swap_core(query_delta)
    down = Chunk(grads_down, 0, 4)
    last = down.over_y(near2)
    key_delta, value_delta, rights, delta_sums = run(
        "delta", delta_kernel, (2,),
        [
            (a, (tokens, GROUP), lambda i, *_, g=g: (0, 2 * g + i))
            for call in ((near1, near2), (far1, far2))
            for a in call
            for g in range(per_call)
        ]
        + [whole(query_delta), (rights, None, None)],
        [
            whole_out((tokens, D), BF16),
            whole_out((tokens, D), BF16),
            ((tokens, 4 * D), BF16, (tokens, D), lambda i, *_: (0, 1 + i)),
            whole_out((8, D), F32),
        ],
        (last,), aliases={2 * groups + 1: 2},
    )
    key_far, value_far = swap_core(key_delta), swap_core(value_delta)
    step = D
    input_mine, input_away, time_sum = run(
        "input", input_kernel, (3,),
        [(rights, (tokens, D), lambda j, *_: (0, j)), (qkv_matrix, (D, D), lambda j, *_: (0, j)), whole(input_part)],
        [whole_out((half, D), F32), whole_out((half, D), BF16), whole_out((1, D), F32)],
        (delta_sums,), [pltpu.VMEM((tokens, D), F32)],
    )
    last_one = lambda b: jnp.where(b == 3, 1, 0)
    grads_four = Grads(
        lefts, rights, (lefts_away, lambda b: 2 + 2 * last_one(b)), (lefts_away, lambda b: 3 + 2 * last_one(b)),
        [query_far, key_far, value_far, out_far], lambda shard, b: shard + 4 * last_one(b), lambda b: b,
    )
    last = grads_four.start(time_sum)

    packed = run(
        "lines", lines_kernel, (1,), [whole(a) for a in (down_sums, first_sums, delta_sums, up_sums, time_sum)],
        [whole_out((32, D), F32)], (last,),
    )
    hops = [("fsdp", 1), ("fsdp", 2)] + [("dp", 1 << i) for i in range(n_dp.bit_length() - 1)]
    line_parts, line_got = [packed], [swap(packed, *hops[0])]

    def add_lines(last):
        ins = [whole(line_parts[-1]), whole(line_got[-1])]
        line_parts.append(run("lines_add", add_kernel, (1,), ins, [whole_out((32, D), F32)], (last,)))
        if len(line_parts) <= len(hops) - 0 and len(line_got) < len(hops):
            line_got.append(swap(line_parts[-1], *hops[len(line_got)]))
        return line_parts[-1]

    up = Chunk(grads_up, 0, 4)
    qk, vo = Chunk(grads_four, 0, 2), Chunk(grads_four, 2, 2)
    last = final_away = relay(final_away, packed)
    final_got = swap_chip(final_away)
    last = down.over_z(last)
    last = up.over_y(last)
    last = add_lines(last)
    last = down.add_high(last)
    last = up.over_z(last)
    last = qk.over_y(last)
    last = vo.over_y(last)
    last = add_lines(last)
    last = down.add_low(last)
    last = up.add_high(last)
    last = final = pair_of(final_mine, final_got, BF16, last)
    last = qk.over_z(last)
    last = vo.over_z(last)
    last = down.back(last)
    last = add_lines(last)
    last = input_away = relay(input_away, last)
    input_got = swap_chip(input_away)
    last = qk.add_high(last)
    last = vo.add_high(last)
    last = up.add_low(last)
    last = add_lines(last)
    last = down_grad = down.finish(last, down_weight.shape, lambda s: (s, 0))
    last = qk.add_low(last)
    last = vo.add_low(last)
    last = up.back(last)
    last = input_gradient = pair_of(input_mine, input_got, F32, last)
    while len(line_parts) <= len(hops):
        last = add_lines(last)
    last = qk.back(last)
    last = vo.back(last)
    last = up_grad = up.finish(last, up_weight.shape, lambda s: (0, s))

    def two(chunk):
        mine, other = chunk.keep, chunk.got
        return (
            jnp.where(side_y == 0, mine, other).astype(F32),
            jnp.where(side_y == 0, other, mine).astype(F32),
        )

    query_grad, key_grad = two(qk)
    value_grad, output_grad = two(vo)

    times = lax.dynamic_slice_in_dim(line_parts[2], device * (D // 4), D // 4, axis=1)
    time_gradient = times[28:30]
    packed = line_parts[-1]
    mine = lax.dynamic_slice_in_dim(packed, device * (D // 4), D // 4, axis=1)
    up_bias_grad = lax.dynamic_slice_in_dim(packed[24:28], device, 1, axis=0).reshape(-1)
    vector_grads = (mine[16], mine[18], mine[10], up_bias_grad, mine[2], mine[8], mine[9], mine[0], mine[1])

    return (
        final,
        input_gradient,
        time_gradient,
        query_grad,
        key_grad,
        value_grad,
        output_grad,
        up_grad,
        down_grad,
        *vector_grads,
    )


def solution(mesh):
    rows, wide, flat = P("dp", "fsdp", None), P("fsdp", None), P("fsdp")
    return jax.shard_map(
        functools.partial(per_device, mesh.shape["dp"]),
        mesh=mesh,
        in_specs=(rows, P("dp"), P(), rows) + (wide,) * 6 + (flat,) * 9,
        out_specs=(rows, rows, P("dp", "fsdp")) + (wide,) * 6 + (flat,) * 9,
        check_vma=False,
    )
```

```python
import functools
import math

import jax
import jax.numpy as jnp
from jax import lax
from jax.experimental import pallas as pl
from jax.experimental.pallas import tpu as pltpu
from jax.sharding import PartitionSpec as P

D = 1024
HEAD_DIM = 64
GROUP = 256
GROUP_HEADS = GROUP // HEAD_DIM
F32 = jnp.float32
BF16 = jnp.bfloat16
ROWS_ROWS = (((0,), (0,)), ((), ()))
COLS_COLS = (((1,), (1,)), ((), ()))
ANY = pl.BlockSpec(memory_space=pl.ANY)
VMEM_MB = dict(grad_z=16,grad_add=16,grad_join=16,lines_add=16,lines=16,relay=16,pair=16,two=16,grad_out=16,grad_y=24)
COST = 10**11
MICROSECONDS = dict(
    pick=2, cut=2, pack=3, split=2, copy=2, relay=2, columns=2, remote=3, key_value=7, query=4, attend=9, output=6,
    feed_forward=40, two=2, grad_x=8, grad_y=5, grad_z=3, grad_add=2, grad_join=3,
    grad_out=3, attend_back=15, delta=5, input=8, input_query=5, lines_in=2, lines=2, lines_add=1, pair=3,
)


def run_kernel(place, name, body, grid, ins, outs, later_than=(), scratch=(), aliases=None, vmem=16):
    count, waits = len(ins), len(later_than)

    def kernel(*refs):
        body(*refs[: 1 + count], *refs[1 + count + waits :])

    def spec(block, index, *buffers):
        if block is None:
            return ANY
        modes = dict(pipeline_mode=pl.Buffered(buffers[0])) if buffers else {}
        return pl.BlockSpec(block, index, **modes)

    shapes = [jax.ShapeDtypeStruct(shape, dtype) for shape, dtype, _, _ in outs]
    out_specs = [spec(block, index) for _, _, block, index in outs]
    single = len(outs) == 1
    return pl.pallas_call(
        kernel,
        grid_spec=pltpu.PrefetchScalarGridSpec(
            num_scalar_prefetch=1,
            grid=grid,
            in_specs=[spec(*one[1:]) for one in ins] + [ANY] * waits,
            out_specs=out_specs[0] if single else out_specs,
            scratch_shapes=list(scratch),
        ),
        out_shape=shapes[0] if single else shapes,
        input_output_aliases={1 + i: o for i, o in (aliases or {}).items()},
        compiler_params=pltpu.CompilerParams(vmem_limit_bytes=VMEM_MB.get(name, 60) * 2**20),
        cost_estimate=pl.CostEstimate(flops=int(MICROSECONDS[name] * COST), bytes_accessed=0, transcendentals=0),
        name=name,
    )(place, *[one[0] for one in ins], *later_than)


CHIP, CORE, SIDE_Y, SIDE_Z = range(4)
LINES = 16
QUERY_BIAS, VALUE_BIAS, OUTPUT_BIAS, DOWN_BIAS, GAIN1, SHIFT1, GAIN2, SHIFT2, EMBED, WEIGHT = range(10)


def device_of(at):
    return 2 * at[CHIP] + at[CORE]


def their(flip, at):
    return 2 * (at[CHIP] ^ flip) + (at[CORE] ^ 1)


def line(lines_ref, i):
    return lines_ref[i : i + 1, :]


def whole(array):
    return (array, array.shape, lambda *_: (0,) * array.ndim)


def held(array):
    return (*whole(array), 1)


def whole_out(shape, dtype):
    return (shape, dtype, shape, lambda *_: (0,) * len(shape))


def sinusoid(timestep):
    halves = D // 2
    frequency = jnp.exp(jnp.arange(halves, dtype=F32) * (-math.log(10000.0) / halves))
    angles = timestep.astype(F32)[:, None] * frequency[None, :]
    return jnp.concatenate([jnp.sin(angles), jnp.cos(angles)], axis=1)


def dot(left, right):
    return jnp.dot(left, right, preferred_element_type=F32)


def dot_back(left, right):
    return lax.dot_general(left, right, COLS_COLS, preferred_element_type=F32)


def outer(left, right):
    return lax.dot_general(left, right, ROWS_ROWS, preferred_element_type=F32)


def total(rows):
    return jnp.sum(rows, axis=0, keepdims=True)


def mean(rows):
    return jnp.mean(rows, axis=-1, keepdims=True)


def normalise(residual):
    centered = residual - mean(residual)
    scale = lax.rsqrt(mean(centered * centered) + 1e-05)
    return centered * scale, scale


def normalise_back(unit, scale, gain, grad):
    scaled = grad * gain
    return scale * (scaled - mean(scaled) - unit * mean(scaled * unit))


def gelu_and_slope(upward):
    size = jnp.abs(upward) * (2.0**-0.5)
    bell = jnp.exp(-0.5 * (upward * upward))
    t = 1.0 / (1.0 + 0.3275911 * size)
    series = t * (
        0.254829592
        + t * (-0.284496736 + t * (1.421413741 + t * (-1.453152027 + t * 1.061405429)))
    )
    tail = 0.5 * series * bell
    cdf = jnp.where(upward >= 0, 1.0 - tail, tail)
    return upward * cdf, cdf + upward * (bell * (2 * math.pi) ** -0.5)


def order_rows(at, pieces, weight_ref):
    for flip, piece in zip((0, 2, 1, 3), pieces):
        rows = piece.shape[0]
        start = pl.multiple_of((device_of(at) ^ flip) * rows, 16)
        weight_ref[pl.ds(start, rows), :] = piece[...]
    return weight_ref[...]


def pieces_in(pieces, step, firsts):
    return [(piece, (piece.shape[0], step), lambda j, *_, k=k: (0, k + j)) for piece, k in zip(pieces, firsts)]


def lines_in_kernel(at, own_ref, far_ref, embeds_ref, weight_ref, lines_ref, up_ref):
    share = D // 4
    extra = up_ref.shape[1] // D
    for flip, shares_ref, first in ((0, own_ref, 0), (2, own_ref, 16), (1, far_ref, 0), (3, far_ref, 16)):
        device = device_of(at) ^ flip
        rows = shares_ref[first : first + 16, :].astype(F32)
        piece = lambda i, rows=rows: rows[i // 4 : i // 4 + 1, i % 4 * share : (i % 4 + 1) * share]
        place = pl.ds(pl.multiple_of(device * share, share), share)
        for i in range(8):
            lines_ref[i : i + 1, place] = piece(i if i < 3 else i + extra)
        for e in range(extra):
            start = pl.multiple_of((device * extra + e) * share, share)
            up_ref[:, pl.ds(start, share)] = piece(3 + e)
    lines_ref[EMBED : EMBED + 1, :] = embeds_ref[pl.ds(at[CHIP], 1), :]
    lines_ref[WEIGHT:LINES, :] = jnp.broadcast_to(weight_ref[...], (LINES - WEIGHT, D))


def key_value_kernel(at, mine_ref, got_ref, lines_ref, *refs):
    *pieces, keys_ref, values_ref, weight_ref, rounded_ref = refs
    j = pl.program_id(0)

    @pl.when(j == 0)
    def _():
        half = mine_ref.shape[0]
        embed = line(lines_ref, EMBED)
        rounded_ref[:half, :] = (mine_ref[...].astype(F32) + embed).astype(BF16)
        rounded_ref[half:, :] = (got_ref[...].astype(F32) + embed).astype(BF16)

    product = dot(rounded_ref[...], order_rows(at, pieces, weight_ref))

    @pl.when(j == 0)
    def _():
        keys_ref[...] = product.astype(BF16)

    @pl.when(j == 1)
    def _():
        values_ref[...] = (product + line(lines_ref, VALUE_BIAS)).astype(BF16)


def query_kernel(at, rounded_ref, lines_ref, *refs):
    *pieces, _, out_ref, weight_ref = refs
    weight = order_rows(at, pieces, weight_ref)
    out_ref[...] = (dot(rounded_ref[...], weight) + line(lines_ref, QUERY_BIAS)).astype(BF16)


def head_mask(head):
    return lax.broadcasted_iota(jnp.int32, (1, GROUP), 1) // HEAD_DIM == head


def attend_kernel(_, q_ref, k1_ref, v1_ref, k2_ref, v2_ref, *refs):
    out_ref, lse_ref = refs[-2:]
    keys = jnp.concatenate([k1_ref[...], k2_ref[...]], axis=0)
    values_t = jnp.concatenate([v1_ref[...], v2_ref[...]], axis=0).T
    queries = q_ref[...] * jnp.asarray(HEAD_DIM**-0.5, BF16)
    outs = []
    for head in range(GROUP_HEADS):
        masked = jnp.where(head_mask(head), queries, jnp.zeros_like(queries))
        scores = dot_back(keys, masked)
        peak = jnp.max(scores, axis=0, keepdims=True)
        exponent = jnp.exp(scores - peak)
        summed = total(exponent)
        attention = (exponent * (1.0 / summed)).astype(BF16)
        lse_ref[0, head : head + 1, :] = peak + jnp.log(summed)
        outs.append(dot(values_t[head * HEAD_DIM : (head + 1) * HEAD_DIM, :], attention))
    out_ref[...] = jnp.concatenate(outs, axis=0).astype(BF16).T


def output_kernel(at, rounded_ref, mixed_ref, mine_ref, got_ref, lines_ref, *refs):
    *pieces, weight_ref, unit_ref, scale_ref, low_ref, away_ref = refs
    product = dot(mixed_ref[...], order_rows(at, pieces, weight_ref))
    half = mine_ref.shape[0]
    for start, tokens_ref in ((0, mine_ref), (half, got_ref)):
        place = pl.ds(start, half)
        hidden = tokens_ref[...].astype(F32) + line(lines_ref, EMBED)
        unit, scale = normalise(hidden + (product[start : start + half, :] + line(lines_ref, OUTPUT_BIAS)))
        unit_ref[place, :] = unit
        scale_ref[place, :] = scale
        low_ref[place, :] = (unit * line(lines_ref, GAIN1) + line(lines_ref, SHIFT1)).astype(BF16)
    width = D // 4
    for k, left_ref in enumerate((low_ref, rounded_ref, mixed_ref)):
        for flip in (1, 0):
            column = pl.multiple_of(their(flip, at) * width, width)
            block = 2 * k + 1 - flip
            away_ref[:, block * width : (block + 1) * width] = left_ref[:, pl.ds(column, width)]


def feed_forward_kernel(
    at, low_ref, bias_ref, unit1_ref, scale1_ref, mine_ref, got_ref, lines_ref, down_ref, output_ref, *refs
):
    pieces, refs = refs[:4], refs[4:]
    active_ref, active_away_ref, final_ref, away_ref, delta_ref, up_delta_ref, down_sums_ref, up_sums_ref = refs[:8]
    input_ref, out_ref, rights_ref, mixed_ref, first_sums_ref, up_all, active_all, slope_all, sum_ref = refs[8:]
    j = pl.program_id(0)
    row = lambda i: line(lines_ref, i)
    half = mine_ref.shape[0]

    @pl.when(j < 4)
    def _():
        weight = order_rows(at, pieces, up_all.at[j])
        for start in (0, half):
            place = pl.ds(start, half)
            active, slope = gelu_and_slope(dot(low_ref[place, :], weight) + bias_ref[...])
            active_ref[place, :] = active.astype(BF16)
            slope_all[j, place, :] = slope.astype(BF16)
        active_all[j] = active_ref[...]

    for flip in (1, 0):

        @pl.when(j == their(flip, at))
        def _(flip=flip):
            width = active_ref.shape[1]
            active_away_ref[:, (1 - flip) * width : (2 - flip) * width] = active_ref[...]

    @pl.when(j == 4)
    def _():
        sum_ref[...] = dot(active_all[0], down_ref[...])

    @pl.when((j > 4) & (j < 8))
    def _():
        sum_ref[...] += dot(active_all[j - 4], down_ref[...])

    @pl.when(j == 7)
    def _():
        sums = [0.0, 0.0, 0.0]
        for start, upstream_ref, one_ref in ((0, mine_ref, final_ref), (half, got_ref, away_ref)):
            place = pl.ds(start, half)
            first_norm = unit1_ref[place, :] * row(GAIN1) + row(SHIFT1)
            unit, scale = normalise(first_norm + (sum_ref[place, :] + row(DOWN_BIAS)))
            one_ref[...] = (unit * row(GAIN2) + row(SHIFT2)).astype(BF16)
            cotangent = upstream_ref[...].astype(F32) * row(WEIGHT)
            grad = normalise_back(unit, scale, row(GAIN2), cotangent)
            delta = grad.astype(BF16)
            sum_ref[place, :] = grad
            delta_ref[place, :] = delta
            parts = (cotangent * unit, cotangent, delta.astype(F32))
            sums = [one + total(part) for one, part in zip(sums, parts)]
        for i, one in enumerate(sums):
            down_sums_ref[i : i + 1, :] = one

    @pl.when(j >= 8)
    def _():
        k = j - 8
        delta = (dot_back(delta_ref[...], down_ref[...]) * slope_all[k].astype(F32)).astype(BF16)
        up_delta_ref[...] = delta
        up_sums_ref[pl.ds(k, 1), :] = total(delta.astype(F32))
        sum_ref[...] += dot_back(delta, up_all[k])

    @pl.when(j == 11)
    def _():
        sums = [0.0, 0.0, 0.0]
        for start in (0, half):
            place = pl.ds(start, half)
            grad, unit = sum_ref[place, :], unit1_ref[place, :]
            below = normalise_back(unit, scale1_ref[place, :], row(GAIN1), grad)
            delta = below.astype(BF16)
            input_ref[place, :] = below
            out_ref[place, :] = delta
            rights_ref[place, :] = delta
            mixed_ref[place, :] = dot_back(delta, output_ref[...]).astype(BF16)
            parts = (grad * unit, grad, delta.astype(F32))
            sums = [one + total(part) for one, part in zip(sums, parts)]
        for i, one in enumerate(sums):
            first_sums_ref[i : i + 1, :] = one


def attend_back_kernel(
    _, q_ref, k1_ref, v1_ref, k2_ref, v2_ref, lse_ref, grad_ref, *refs
):
    dq_ref, rights_ref, near_ref, far_ref, p_all, ds_all = refs[-6:]
    half, tokens = k1_ref.shape[0], q_ref.shape[0]
    keys = jnp.concatenate([k1_ref[...], k2_ref[...]], axis=0)
    values = jnp.concatenate([v1_ref[...], v2_ref[...]], axis=0)
    keys_t = keys.T
    queries = q_ref[...] * jnp.asarray(HEAD_DIM**-0.5, BF16)
    grads = grad_ref[...]
    query_parts, grad_parts, dq_parts = [], [], []
    for head in range(GROUP_HEADS):
        query_one = jnp.where(head_mask(head), queries, jnp.zeros_like(queries))
        grad_one = jnp.where(head_mask(head), grads, jnp.zeros_like(grads))
        attention = jnp.exp(dot_back(keys, query_one) - lse_ref[0, head : head + 1, :])
        prob_grad = dot_back(values, grad_one)
        weighted = total(attention * prob_grad)
        score_grad = (attention * (prob_grad - weighted)).astype(BF16)
        place = slice(head * tokens, (head + 1) * tokens)
        p_all[:, place] = attention.astype(BF16)
        ds_all[:, place] = score_grad
        dq_parts.append(dot(keys_t[head * HEAD_DIM : (head + 1) * HEAD_DIM, :], score_grad))
        query_parts.append(query_one)
        grad_parts.append(grad_one)
    value_grad = dot(p_all[...], jnp.concatenate(grad_parts, axis=0))
    key_grad = dot(ds_all[...], jnp.concatenate(query_parts, axis=0))
    dq_ref[...] = (jnp.concatenate(dq_parts, axis=0) * HEAD_DIM**-0.5).astype(BF16).T
    rights_ref[...] = dq_ref[...]
    near_ref[:, :GROUP] = key_grad[:half, :]
    near_ref[:, GROUP:] = value_grad[:half, :]
    far_ref[:, :GROUP] = key_grad[half:, :].astype(BF16)
    far_ref[:, GROUP:] = value_grad[half:, :].astype(BF16)


def delta_kernel(_, *refs):
    groups = D // GROUP
    nears, fars = refs[:groups], refs[groups : 2 * groups]
    queries_ref, __, keys_ref, values_ref, rights_ref, sums_ref = refs[2 * groups :]
    i = pl.program_id(0)
    for g in range(groups):
        place = slice(g * GROUP, (g + 1) * GROUP)
        rights_ref[:, place] = (nears[g][...] + fars[g][...].astype(F32)).astype(BF16)
    sums_ref[pl.ds(1 + i, 1), :] = total(rights_ref[...].astype(F32))

    @pl.when(i == 0)
    def _():
        sums_ref[0:1, :] = total(queries_ref[...].astype(F32))
        keys_ref[...] = rights_ref[...]

    @pl.when(i == 1)
    def _():
        values_ref[...] = rights_ref[...]


def input_query_kernel(_, delta_ref, weight_ref, grad_ref, out_ref):
    out_ref[...] = grad_ref[...] + dot_back(delta_ref[...], weight_ref[...])


def input_kernel(_, delta_ref, weight_ref, grad_ref, mine_ref, away_ref, time_ref, sum_ref):
    j = pl.program_id(0)
    part = dot_back(delta_ref[...], weight_ref[...])

    @pl.when(j == 0)
    def _():
        sum_ref[...] = grad_ref[...] + part

    @pl.when(j > 0)
    def _():
        sum_ref[...] += part

    @pl.when(j == pl.num_programs(0) - 1)
    def _():
        half = mine_ref.shape[0]
        mine_ref[...] = sum_ref[:half, :]
        away_ref[...] = sum_ref[half:, :].astype(BF16)
        time_ref[...] = total(sum_ref[...])


def grad_block(which, left_ref, right_ref, far_left_ref, fars, sum_ref, *more):
    for k, far_ref in enumerate(fars):

        @pl.when((which == k) if len(fars) > 1 else (which >= 0))
        def _(far_ref=far_ref):
            sum_ref[...] = outer(far_left_ref[...], far_ref[...])

    block = outer(left_ref[...], right_ref[...]) + sum_ref[...]
    for one_ref in more:
        block = block + one_ref[...].astype(F32)
    return block.astype(BF16)


def grad_x_kernel(_, left_ref, right_ref, far_left_ref, *refs):
    *fars, out_ref, sum_ref = refs
    out_ref[...] = grad_block(pl.program_id(0), left_ref, right_ref, far_left_ref, fars, sum_ref)


def grad_y_kernel(at_ref, left_ref, right_ref, far_left_ref, other_ref, *refs):
    *fars, away_ref, keep_ref, sum_ref = refs
    i, half = pl.program_id(0), pl.num_programs(0) // 2
    which = jnp.where(i < half, 1 - at_ref[SIDE_Y], at_ref[SIDE_Y])
    block = grad_block(which, left_ref, right_ref, far_left_ref, fars, sum_ref, other_ref)

    @pl.when(i < half)
    def _():
        away_ref[...] = block

    @pl.when(i >= half)
    def _():
        keep_ref[...] = block


def fold_kernel(_, keep1_ref, keep2_ref, away1_ref, away2_ref, keep_ref, away_ref):
    keep_ref[...] = (keep1_ref[...].astype(F32) + keep2_ref[...].astype(F32)).astype(BF16)
    away_ref[...] = (away1_ref[...].astype(F32) + away2_ref[...].astype(F32)).astype(BF16)


def add_kernel(_, one_ref, two_ref, out_ref):
    out_ref[...] = (one_ref[...].astype(F32) + two_ref[...].astype(F32)).astype(out_ref.dtype)


def join_kernel(at_ref, mine_ref, other_ref, out_ref):
    rows = mine_ref.shape[0]
    out_ref[pl.ds(pl.multiple_of(at_ref[SIDE_Z] * rows, 16), rows), :] = mine_ref[...]
    out_ref[pl.ds(pl.multiple_of((1 - at_ref[SIDE_Z]) * rows, 16), rows), :] = other_ref[...]


def finish_kernel(_, mine_ref, other_ref, *refs):
    out_ref = refs[-1]
    i, half = pl.program_id(0), pl.num_programs(0) // 2

    @pl.when(i < half)
    def _():
        out_ref[...] = mine_ref[...].astype(F32)

    @pl.when(i >= half)
    def _():
        out_ref[...] = other_ref[...].astype(F32)


def copy_kernel(_, in_ref, out_ref):
    out_ref[...] = in_ref[...]


def two_kernel(at, mine_ref, other_ref, first_ref, second_ref):
    first = at[SIDE_Y] == 0
    mine, other = mine_ref[...].astype(F32), other_ref[...].astype(F32)
    first_ref[...] = jnp.where(first, mine, other)
    second_ref[...] = jnp.where(first, other, mine)


def pair_kernel(_, mine_ref, received_ref, out_ref):
    @pl.when(pl.program_id(0) == 0)
    def _():
        out_ref[...] = mine_ref[...]

    @pl.when(pl.program_id(0) == 1)
    def _():
        out_ref[...] = received_ref[...].astype(out_ref.dtype)


def append_kernel(_, first_ref, *refs):
    *vectors, out_ref, small_ref = refs
    rows = first_ref.shape[0]
    out_ref[:rows, :] = first_ref[...]
    flat = jnp.concatenate([vector[...].astype(F32).reshape(1, -1) for vector in vectors], axis=1)
    lines = [flat[:, start : start + D] for start in range(0, flat.shape[1], D)]
    small = jnp.concatenate(lines + [jnp.zeros((16 - len(lines), D), F32)], axis=0).astype(BF16)
    small_ref[...] = small
    out_ref[rows:, :] = small


def side_by_side_kernel(_, *refs):
    out_ref, at = refs[-1], 0
    for piece in refs[:-1]:
        out_ref[:, at : at + piece.shape[1]] = piece[...]
        at += piece.shape[1]


def split_kernel(_, in_ref, first_ref, second_ref):
    rows = first_ref.shape[0]
    first_ref[...] = in_ref[:rows, :]
    second_ref[...] = in_ref[rows:, :]


def parity(at):
    return (at[SIDE_Y] + at[SIDE_Z]) % 2


def remote_kernel(at, half_ref, third_ref, fourth_ref, *outs):
    columns = 0
    for out_ref in outs:
        width = out_ref.shape[1]
        place = slice(columns, columns + width)
        columns += width
        remote_rows(at, half_ref.at[:, place], third_ref.at[:, place], fourth_ref.at[:, place], out_ref)


def remote_rows(at, half_ref, third_ref, fourth_ref, out_ref):
    half, quarter = half_ref.shape[0], third_ref.shape[0]
    missing = (1 - parity(at)) * half
    out_ref[pl.ds(pl.multiple_of(parity(at) * half, 16), half), :] = half_ref[...]
    out_ref[pl.ds(pl.multiple_of(missing, 16), quarter), :] = third_ref[...]
    out_ref[pl.ds(pl.multiple_of(missing + quarter, 16), quarter), :] = fourth_ref[...]


def lines_kernel(at, down_ref, first_ref, delta_ref, up_ref, time_ref, out_ref):
    out_ref[0:8, :] = down_ref[...]
    out_ref[8:16, :] = first_ref[...]
    out_ref[16:24, :] = delta_ref[...]
    out_ref[24:28, :] = up_ref[0:4, :]
    row = lax.broadcasted_iota(jnp.int32, (4, D), 0)
    out_ref[28:32, :] = jnp.where(row == at[CHIP], time_ref[...], 0.0)


def per_device(n_dp, inputs, timestep, bucket_count, upstream, *params):
    query_weight, key_weight, value_weight, output_weight, up_weight, down_weight = params[:6]
    vectors = params[6:]
    device = lax.axis_index("fsdp")
    chip, core = device // 2, device % 2
    bucket = lax.axis_index("dp")
    half = inputs.shape[1]
    tokens = 2 * half
    hidden_width = up_weight.shape[1]
    side_y, side_z = bucket % 2, (bucket // 2) % 2
    place = jnp.stack([chip, core, side_y, side_z]).astype(jnp.int32)
    run = functools.partial(run_kernel, place)

    def swap(value, axis, bit):
        size = 4 if axis == "fsdp" else n_dp
        return lax.ppermute(value, axis, [(i, i ^ bit) for i in range(size)])

    swap_core = lambda value: swap(value, "fsdp", 1)
    swap_chip = lambda value: swap(value, "fsdp", 2)
    swap_y = lambda value: swap(value, "dp", 1)
    swap_z = lambda value: swap(value, "dp", 2)

    def pick(array, flip, *later_than):
        _, rows, columns = array.shape
        ins = [(array, (None, rows, columns), lambda _, at: (at[CHIP] ^ flip, 0, 0))]
        return run("pick", copy_kernel, (1,), ins, [whole_out((rows, columns), array.dtype)], later_than)

    def pack(arrays, *later_than):
        shape = (arrays[0].shape[0], sum(array.shape[1] for array in arrays))
        return run("pack", side_by_side_kernel, (1,), [whole(a) for a in arrays], [whole_out(shape, BF16)], later_than)

    def cut(shards, *later_than):
        rows = shards[0].shape[0]
        columns = sum(shard.shape[1] for shard in shards)
        ins = [(shard, (rows // 2, shard.shape[1]), lambda _, at: (parity(at), 0)) for shard in shards]
        outs = [whole_out((rows // 2, columns), BF16)]
        return run("cut", side_by_side_kernel, (1,), ins, outs, later_than)

    def split(first, *later_than):
        rows, columns = first.shape
        outs = [whole_out((rows // 2, columns), BF16)] * 2
        to_y, to_z = run("split", split_kernel, (1,), [whole(first)], outs, later_than)
        return (first, swap_y(to_y), swap_z(to_z)), to_y

    def remote(parts, widths, *later_than):
        outs = [whole_out((2 * parts[0].shape[0], width), BF16) for width in widths]
        return run("remote", remote_kernel, (1,), [whole(part) for part in parts], outs, later_than)

    tokens_away, small = run(
        "pick", append_kernel, (1,),
        [(inputs, (None, half, D), lambda _, at: (at[CHIP] ^ 1, 0, 0))] + [whole(vector) for vector in vectors],
        [whole_out((half + 16, D), BF16), whole_out((16, D), BF16)],
    )
    tokens_got = swap_chip(tokens_away)
    got_half = (tokens_got, (half, D), lambda *_: (0, 0))
    three = (query_weight, key_weight, value_weight)
    two_weights = (output_weight, up_weight)
    three_cut = cut(three, tokens_away)
    three_first = swap_chip(three_cut)
    three_own = pack(three, three_cut)
    three_sibling = swap_core(three_own)
    two_own = pack(two_weights, three_own)
    two_sibling = swap_core(two_own)
    two_cut = cut(two_weights, tokens_got, two_own)
    two_first = swap_chip(two_cut)
    down_copy = run("copy", copy_kernel, (1,), [whole(down_weight)], [whole_out(down_weight.shape, BF16)], (two_cut,))
    live = chip < bucket_count[bucket]
    seq_weight = live.astype(F32) * (2 * n_dp / jnp.sum(bucket_count).astype(F32))
    small_two = jnp.concatenate([small, tokens_got[half:]], axis=0)
    small_far = swap_core(small_two)
    three_parts, split_done = split(three_first, three_sibling, two_sibling, down_copy, small_far)
    down_matrix = lax.all_gather(down_copy, "fsdp", axis=0, tiled=True)
    tokens_mine = pick(inputs, 0, split_done)
    query_remote, kv_remote = remote(three_parts, (D, 2 * D), tokens_mine)
    lines, up_bias = run(
        "lines_in", lines_in_kernel, (1,),
        [whole(a) for a in (small_two, small_far, sinusoid(timestep), seq_weight.reshape(1, 1))],
        [whole_out((LINES, D), F32), whole_out((1, hidden_width), F32)], (kv_remote,),
    )
    kv_pieces = [three_own, kv_remote, three_sibling, swap_core(kv_remote)]
    query_pieces = [three_own, query_remote, three_sibling, swap_core(query_remote)]
    keys, values, qkv_matrix, lefts = run(
        "key_value", key_value_kernel, (2,),
        [whole(tokens_mine), got_half, whole(lines)] + pieces_in(kv_pieces, D, (1, 0, 1, 0)),
        [
            whole_out((tokens, D), BF16),
            whole_out((tokens, D), BF16),
            ((D, 3 * D), BF16, (D, D), lambda j, *_: (0, 1 + j)),
            ((tokens, 2 * D), BF16, (tokens, D), lambda j, *_: (0, 0)),
        ],
    )
    far_keys, far_values = swap_core(keys), swap_core(values)
    queries, qkv_matrix = run(
        "query", query_kernel, (1,),
        [(lefts, (tokens, D), lambda j, *_: (0, 0)), whole(lines)] + pieces_in(query_pieces, D, (0, 0, 0, 0))
        + [(qkv_matrix, None, None)],
        [((tokens, D), BF16, (tokens, D), lambda j, *_: (0, 0)), ((D, 3 * D), BF16, (D, D), lambda j, *_: (0, 0))],
        aliases={2 + len(query_pieces): 1},
    )
    groups = D // GROUP
    group_of = lambda array, first: (array, (array.shape[0], GROUP), lambda g, *_: (0, first + g))

    def attend(first, count, lefts, lse, *later_than):
        return run(
            "attend", attend_kernel, (count,),
            [group_of(a, first) for a in (queries, keys, values, far_keys, far_values)] + [(lefts, None, None)]
            + ([] if lse is None else [(lse, None, None)]),
            [
                ((tokens, 2 * D), BF16, (tokens, GROUP), lambda g, *_: (0, groups + first + g)),
                ((groups, GROUP_HEADS, tokens), F32, (1, GROUP_HEADS, tokens), lambda g, *_: (first + g, 0, 0)),
            ],
            later_than, aliases={5: 0} if lse is None else {5: 0, 6: 1}, vmem=32,
        )

    lefts, lse = attend(0, groups // 2, lefts, None)
    two_parts, split_done = split(two_first, lse)
    upstream_away = pick(upstream, 1, split_done)
    upstream_got = swap_chip(upstream_away)
    lefts, lse = attend(groups // 2, groups // 2, lefts, lse, upstream_away)
    two_remote = remote(two_parts, (two_own.shape[1],), lse)
    upstream_mine = pick(upstream, 0, two_remote)
    two_pieces = [two_own, two_remote, two_sibling, swap_core(two_remote)]
    output_matrix, unit1, scale1, first_low, lefts_away = run(
        "output", output_kernel, (1,),
        [(lefts, (tokens, D), lambda j, *_: (0, 0)), (lefts, (tokens, D), lambda j, *_: (0, 1))]
        + [whole(tokens_mine), got_half, whole(lines)]
        + pieces_in(two_pieces, D, (0, 0, 0, 0)),
        [
            whole_out((D, D), BF16),
            whole_out((tokens, D), F32),
            whole_out((tokens, 1), F32),
            whole_out((tokens, D), BF16),
            whole_out((tokens, 6 * D // 4), BF16),
        ],
        (upstream_mine,),
    )
    lefts_away = swap_core(lefts_away)
    width = hidden_width // 4
    hidden_block = lambda j: jnp.minimum(j, 3)
    results = run(
        "feed_forward", feed_forward_kernel, (12,),
        [held(first_low), (up_bias, (1, width), lambda j, *_: (0, hidden_block(j))), held(unit1), held(scale1)]
        + [held(upstream_mine), held(upstream_got), held(lines)]
        + [(down_matrix, (width, D), lambda j, *_: (jnp.where(j < 4, 0, j % 4), 0)), held(output_matrix)]
        + [(piece, (piece.shape[0], width), lambda j, *_: (0, D // width + hidden_block(j))) for piece in two_pieces],
        [
            ((tokens, hidden_width), BF16, (tokens, width), lambda j, *_: (0, hidden_block(j))),
            whole_out((tokens, 2 * width), BF16),
            whole_out((half, D), BF16),
            whole_out((half, D), BF16),
            whole_out((tokens, D), BF16),
            ((tokens, hidden_width), BF16, (tokens, width), lambda j, *_: (0, jnp.maximum(j - 8, 0))),
            whole_out((8, D), F32),
            whole_out((8, D), F32),
            whole_out((tokens, D), F32),
            whole_out((tokens, D), BF16),
            ((tokens, 4 * D), BF16, (tokens, D), lambda j, *_: (0, 3)),
            whole_out((tokens, D), BF16),
            whole_out((8, D), F32),
        ],
        (),
        [
            pltpu.VMEM((4, D, width), BF16),
            pltpu.VMEM((4, tokens, width), BF16),
            pltpu.VMEM((4, tokens, width), BF16),
            pltpu.VMEM((tokens, D), F32),
        ],
    )
    activated, active_away, final_mine, final_away, down_delta, up_delta, down_sums, up_sums = results[:8]
    input_part, out_delta, rights, mixed_grad, first_sums = results[8:]
    active_away, down_far = swap_core(active_away), swap_core(down_delta)
    up_far, out_far = swap_core(up_delta), swap_core(out_delta)

    block_rows = D // 4

    class Grads:
        def __init__(self, left, right, send, keep, fars, near, right_column):
            self.left, self.right, self.send_far, self.keep_far = left, right, send, keep
            self.fars, self.near, self.right_column = fars, near, right_column

        def ins(self, flip, far, block):
            far_left, far_column = far
            shard = lambda at: 2 * (at[CHIP] ^ flip) + at[CORE]
            return [
                (self.left, (tokens, block_rows), lambda i, at: (0, self.near(shard(at), block(i, at)))),
                (self.right, (tokens, D), lambda i, at: (0, self.right_column(block(i, at)))),
                (far_left, (tokens, block_rows), lambda i, at: (0, far_column(block(i, at)))),
            ]

        def far_ins(self, block, first, count):
            if len(self.fars) > 1:
                return [whole(a) for a in self.fars[first : first + count]]
            return [(self.fars[0], (tokens, D), lambda i, at: (0, self.right_column(block(i, at))))]

        def four(self, name, body, flip, far, more, *later_than):
            out = ((4 * block_rows, D), BF16, (block_rows, D), lambda i, at: (i, 0))
            block = lambda i, at: i
            ins = self.ins(flip, far, block) + more + self.far_ins(block, 0, 4)
            return run(name, body, (4,), ins, [out], later_than, [pltpu.VMEM((block_rows, D), F32)])

        def start(self, *later_than):
            sent = self.four("grad_x", grad_x_kernel, 1, self.send_far, [], *later_than)
            self.got = swap_chip(sent)
            return sent

    class Chunk:
        def __init__(self, grads, first, count):
            self.grads, self.first, self.half = grads, first, count // 2

        def over_y(self, last):
            grads, first, half = self.grads, self.first, self.half
            block = lambda i, at: first + jnp.where(
                i < half, (1 - at[SIDE_Y]) * half + i, at[SIDE_Y] * half + i - half
            )
            other = (grads.got, (block_rows, D), lambda i, at: (block(i, at), 0))
            shape = (half * block_rows, D)
            away, self.keep = run(
                "grad_y", grad_y_kernel, (2 * half,),
                grads.ins(0, grads.keep_far, block) + [other] + grads.far_ins(block, first, 2),
                [
                    (shape, BF16, (block_rows, D), lambda i, at: (jnp.minimum(i, half - 1), 0)),
                    (shape, BF16, (block_rows, D), lambda i, at: (jnp.maximum(i - half, 0), 0)),
                ],
                (last,), [pltpu.VMEM((block_rows, D), F32)],
            )
            self.got = swap_y(away)
            return self.keep

        def over_z(self, last):
            block = (self.keep.shape[0] // 2, D)
            kept = [(a, block, lambda _, at: (at[SIDE_Z], 0)) for a in (self.keep, self.got)]
            given = [(a, block, lambda _, at: (1 - at[SIDE_Z], 0)) for a in (self.keep, self.got)]
            self.keep, away = run("grad_z", fold_kernel, (1,), kept + given, [whole_out(block, BF16)] * 2, (last,))
            self.got = swap_z(away)
            return self.keep

        def add(self, bit, last):
            ins = [whole(self.keep), whole(self.got)]
            self.keep = run("grad_add", add_kernel, (1,), ins, [whole_out(self.keep.shape, BF16)], (last,))
            self.got = swap(self.keep, "dp", bit)
            return self.keep

        def add_high(self, last):
            for bit in high_bits:
                last = self.add(bit, last)
            return last

        def add_low(self, last):
            return self.add(2, last)

        def back(self, last):
            ins = [whole(self.keep), whole(self.got)]
            shape = (2 * self.keep.shape[0], D)
            self.keep = run("grad_join", join_kernel, (1,), ins, [whole_out(shape, BF16)], (last,))
            self.got = swap_y(self.keep)
            return self.keep

        def finish(self, last, shape, index):
            half = self.half
            ins = [
                (self.keep, (block_rows, D), lambda i, at: (jnp.minimum(i, half - 1), 0)),
                (self.got, (block_rows, D), lambda i, at: (jnp.maximum(i - half, 0), 0)),
            ]
            place = lambda i, at: jnp.where(i < half, at[SIDE_Y] * half + i, (1 - at[SIDE_Y]) * half + i - half)
            out = (shape, F32, (block_rows, D), lambda i, at: index(place(i, at)))
            return run("grad_out", finish_kernel, (2 * half,), ins, [out], (last,))

    def pair_of(mine, received, dtype, last):
        out = ((2, half, D), dtype, (None, half, D), lambda i, at: (at[CHIP] ^ i, 0, 0))
        return run("pair", pair_kernel, (2,), [whole(mine), whole(received)], [out], (last,))

    high_bits = [1 << i for i in range(2, n_dp.bit_length()) if 1 << i < n_dp]
    relay = lambda array, last: run("relay", copy_kernel, (1,), [whole(array)], [whole_out(array.shape, array.dtype)], (last,))

    grads_down = Grads(
        activated, down_delta, (active_away, lambda b: b), (active_away, lambda b: 4 + b), [down_far],
        lambda shard, b: shard * (hidden_width // D) + b, lambda b: 0,
    )
    grads_up = Grads(
        first_low, up_delta, (lefts_away, lambda b: 0), (lefts_away, lambda b: 1), [up_far],
        lambda shard, b: shard, lambda b: b,
    )

    def attend_back(first, count, later_than, rights, query_delta):
        return run(
            "attend_back", attend_back_kernel, (count,),
            [group_of(a, first) for a in (queries, keys, values, far_keys, far_values)]
            + [(lse, (1, GROUP_HEADS, tokens), lambda g, *_: (first + g, 0, 0)), group_of(mixed_grad, first)]
            + [(rights, None, None)] + ([] if query_delta is None else [(query_delta, None, None)]),
            [
                ((tokens, D), BF16, (tokens, GROUP), lambda g, *_: (0, first + g)),
                ((tokens, 4 * D), BF16, (tokens, GROUP), lambda g, *_: (0, first + g)),
                ((tokens, 2 * count * GROUP), F32, (tokens, 2 * GROUP), lambda g, *_: (0, g)),
                ((tokens, 2 * count * GROUP), BF16, (tokens, 2 * GROUP), lambda g, *_: (0, g)),
            ],
            later_than, [pltpu.VMEM((2 * tokens, GROUP_HEADS * tokens), BF16)] * 2, aliases={7: 1} if query_delta is None else {7: 1, 8: 0},
        )

    first_call = 1
    query_delta, rights, near1, far1 = attend_back(0, first_call, (mixed_grad,), rights, None)
    far1 = swap_core(far1)
    last = grads_down.start(near1)
    last = grads_up.start(last, out_far)
    query_delta, rights, near2, far2 = attend_back(first_call, groups - first_call, (last, far1), rights, query_delta)
    far2, query_far = swap_core(far2), swap_core(query_delta)
    last = input_part = run(
        "input_query", input_query_kernel, (2,),
        [
            (query_delta, (half, D), lambda i, *_: (i, 0)),
            (qkv_matrix, (D, D), lambda i, *_: (0, 0)),
            (input_part, (half, D), lambda i, *_: (i, 0)),
        ],
        [((tokens, D), F32, (half, D), lambda i, *_: (i, 0))], (near2,),
    )
    key_delta, value_delta, rights, delta_sums = run(
        "delta", delta_kernel, (2,),
        [
            (a, (tokens, GROUP), lambda i, *_, g=g: (0, 2 * g + i))
            for one, two in ((near1, near2), (far1, far2))
            for a, count in ((one, first_call), (two, groups - first_call))
            for g in range(count)
        ]
        + [whole(query_delta), (rights, None, None)],
        [
            whole_out((tokens, D), BF16),
            whole_out((tokens, D), BF16),
            ((tokens, 4 * D), BF16, (tokens, D), lambda i, *_: (0, 1 + i)),
            whole_out((8, D), F32),
        ],
        (last,), aliases={2 * groups + 1: 2},
    )
    key_far, value_far = swap_core(key_delta), swap_core(value_delta)
    step = D
    input_mine, input_away, time_sum = run(
        "input", input_kernel, (2,),
        [(rights, (tokens, D), lambda j, *_: (0, 1 + j)), (qkv_matrix, (D, D), lambda j, *_: (0, 1 + j)), whole(input_part)],
        [whole_out((half, D), F32), whole_out((half, D), BF16), whole_out((1, D), F32)],
        (delta_sums,), [pltpu.VMEM((tokens, D), F32)],
    )
    last_one = lambda b: jnp.where(b == 3, 1, 0)
    grads_four = Grads(
        lefts, rights, (lefts_away, lambda b: 2 + 2 * last_one(b)), (lefts_away, lambda b: 3 + 2 * last_one(b)),
        [query_far, key_far, value_far, out_far], lambda shard, b: shard + 4 * last_one(b), lambda b: b,
    )
    last = grads_four.start(time_sum)

    packed = run(
        "lines", lines_kernel, (1,), [whole(a) for a in (down_sums, first_sums, delta_sums, up_sums, time_sum)],
        [whole_out((32, D), F32)], (last,),
    )
    hops = [("fsdp", 1), ("fsdp", 2)] + [("dp", 1 << i) for i in range(n_dp.bit_length() - 1)]
    line_parts, line_got = [packed], [swap(packed, *hops[0])]

    def add_lines(last):
        ins = [whole(line_parts[-1]), whole(line_got[-1])]
        line_parts.append(run("lines_add", add_kernel, (1,), ins, [whole_out((32, D), F32)], (last,)))
        if len(line_parts) <= len(hops) - 0 and len(line_got) < len(hops):
            line_got.append(swap(line_parts[-1], *hops[len(line_got)]))
        return line_parts[-1]

    down, up = Chunk(grads_down, 0, 4), Chunk(grads_up, 0, 4)
    qk, vo = Chunk(grads_four, 0, 2), Chunk(grads_four, 2, 2)
    last = down.over_y(packed)
    last = add_lines(last)
    last = down.over_z(last)
    last = up.over_y(last)
    last = down.add_high(last)
    last = up.over_z(last)
    last = qk.over_y(last)
    last = vo.over_y(last)
    last = down.add_low(last)
    last = up.add_high(last)
    last = qk.over_z(last)
    last = vo.over_z(last)
    last = add_lines(last)
    last = final_away = relay(final_away, last)
    final_got = swap_chip(final_away)
    last = qk.add_high(last)
    last = vo.add_high(last)
    last = down.back(last)
    last = up.add_low(last)
    last = add_lines(last)
    last = qk.add_low(last)
    last = vo.add_low(last)
    last = final = pair_of(final_mine, final_got, BF16, last)
    last = input_away = relay(input_away, last)
    input_got = swap_chip(input_away)
    last = up.back(last)
    last = qk.back(last)
    last = vo.back(last)
    while len(line_parts) < len(hops):
        last = add_lines(last)
    last = down_grad = down.finish(last, down_weight.shape, lambda s: (s, 0))
    last = input_gradient = pair_of(input_mine, input_got, F32, last)
    last = up_grad = up.finish(last, up_weight.shape, lambda s: (0, s))
    last = add_lines(last)

    def two(chunk, last):
        outs = [whole_out((block_rows, D), F32)] * 2
        return run("two", two_kernel, (1,), [whole(chunk.keep), whole(chunk.got)], outs, (last,))

    query_grad, key_grad = two(qk, last)
    value_grad, output_grad = two(vo, query_grad)
    times = lax.dynamic_slice_in_dim(line_parts[2], device * (D // 4), D // 4, axis=1)
    time_gradient = times[28:30]
    packed = line_parts[-1]
    mine = lax.dynamic_slice_in_dim(packed, device * (D // 4), D // 4, axis=1)
    up_bias_grad = lax.dynamic_slice_in_dim(packed[24:28], device, 1, axis=0).reshape(-1)
    vector_grads = (mine[16], mine[18], mine[10], up_bias_grad, mine[2], mine[8], mine[9], mine[0], mine[1])

    return (
        final,
        input_gradient,
        time_gradient,
        query_grad,
        key_grad,
        value_grad,
        output_grad,
        up_grad,
        down_grad,
        *vector_grads,
    )


def solution(mesh):
    rows, wide, flat = P("dp", "fsdp", None), P("fsdp", None), P("fsdp")
    return jax.shard_map(
        functools.partial(per_device, mesh.shape["dp"]),
        mesh=mesh,
        in_specs=(rows, P("dp"), P(), rows) + (wide,) * 6 + (flat,) * 9,
        out_specs=(rows, rows, P("dp", "fsdp")) + (wide,) * 6 + (flat,) * 9,
        check_vma=False,
    )
```

```python
import functools
import math

import jax
import jax.numpy as jnp
from jax import lax
from jax.experimental import pallas as pl
from jax.experimental.pallas import tpu as pltpu
from jax.sharding import PartitionSpec as P

D = 1024
HEAD_DIM = 64
GROUP = 256
GROUP_HEADS = GROUP // HEAD_DIM
F32 = jnp.float32
BF16 = jnp.bfloat16
ROWS_ROWS = (((0,), (0,)), ((), ()))
COLS_COLS = (((1,), (1,)), ((), ()))
ANY = pl.BlockSpec(memory_space=pl.ANY)
VMEM_MB = dict(grad_z=16,grad_add=16,grad_join=16,lines_add=16,lines=16,relay=16,grad_y=24)
COST = 10**11
MICROSECONDS = dict(
    pick=2, cut=2, pack=3, split=2, copy=2, relay=2, columns=2, remote=3, key_value=7, query=4, attend=9, output=6,
    feed_forward=40, two=2, grad_x=8, grad_y=5, grad_z=3, grad_add=2, grad_join=3,
    grad_out=3, attend_back=15, delta=5, input=8, input_query=5, lines_in=2, lines=2, lines_add=1, pair=3,
)


def run_kernel(place, name, body, grid, ins, outs, later_than=(), scratch=(), aliases=None, vmem=16):
    count, waits = len(ins), len(later_than)

    def kernel(*refs):
        body(*refs[: 1 + count], *refs[1 + count + waits :])

    def spec(block, index, *buffers):
        if block is None:
            return ANY
        modes = dict(pipeline_mode=pl.Buffered(buffers[0])) if buffers else {}
        return pl.BlockSpec(block, index, **modes)

    shapes = [jax.ShapeDtypeStruct(shape, dtype) for shape, dtype, _, _ in outs]
    out_specs = [spec(block, index) for _, _, block, index in outs]
    single = len(outs) == 1
    return pl.pallas_call(
        kernel,
        grid_spec=pltpu.PrefetchScalarGridSpec(
            num_scalar_prefetch=1,
            grid=grid,
            in_specs=[spec(*one[1:]) for one in ins] + [ANY] * waits,
            out_specs=out_specs[0] if single else out_specs,
            scratch_shapes=list(scratch),
        ),
        out_shape=shapes[0] if single else shapes,
        input_output_aliases={1 + i: o for i, o in (aliases or {}).items()},
        compiler_params=pltpu.CompilerParams(vmem_limit_bytes=VMEM_MB.get(name, 60) * 2**20),
        cost_estimate=pl.CostEstimate(flops=int(MICROSECONDS[name] * COST), bytes_accessed=0, transcendentals=0),
        name=name,
    )(place, *[one[0] for one in ins], *later_than)


CHIP, CORE, SIDE_Y, SIDE_Z = range(4)
LINES = 16
QUERY_BIAS, VALUE_BIAS, OUTPUT_BIAS, DOWN_BIAS, GAIN1, SHIFT1, GAIN2, SHIFT2, EMBED, WEIGHT = range(10)


def device_of(at):
    return 2 * at[CHIP] + at[CORE]


def their(flip, at):
    return 2 * (at[CHIP] ^ flip) + (at[CORE] ^ 1)


def line(lines_ref, i):
    return lines_ref[i : i + 1, :]


def whole(array):
    return (array, array.shape, lambda *_: (0,) * array.ndim)


def held(array):
    return (*whole(array), 1)


def whole_out(shape, dtype):
    return (shape, dtype, shape, lambda *_: (0,) * len(shape))


def sinusoid(timestep):
    halves = D // 2
    frequency = jnp.exp(jnp.arange(halves, dtype=F32) * (-math.log(10000.0) / halves))
    angles = timestep.astype(F32)[:, None] * frequency[None, :]
    return jnp.concatenate([jnp.sin(angles), jnp.cos(angles)], axis=1)


def dot(left, right):
    return jnp.dot(left, right, preferred_element_type=F32)


def dot_back(left, right):
    return lax.dot_general(left, right, COLS_COLS, preferred_element_type=F32)


def outer(left, right):
    return lax.dot_general(left, right, ROWS_ROWS, preferred_element_type=F32)


def total(rows):
    return jnp.sum(rows, axis=0, keepdims=True)


def mean(rows):
    return jnp.mean(rows, axis=-1, keepdims=True)


def normalise(residual):
    centered = residual - mean(residual)
    scale = lax.rsqrt(mean(centered * centered) + 1e-05)
    return centered * scale, scale


def normalise_back(unit, scale, gain, grad):
    scaled = grad * gain
    return scale * (scaled - mean(scaled) - unit * mean(scaled * unit))


def gelu_and_slope(upward):
    size = jnp.abs(upward) * (2.0**-0.5)
    bell = jnp.exp(-0.5 * (upward * upward))
    t = 1.0 / (1.0 + 0.3275911 * size)
    series = t * (
        0.254829592
        + t * (-0.284496736 + t * (1.421413741 + t * (-1.453152027 + t * 1.061405429)))
    )
    tail = 0.5 * series * bell
    cdf = jnp.where(upward >= 0, 1.0 - tail, tail)
    return upward * cdf, cdf + upward * (bell * (2 * math.pi) ** -0.5)


def order_rows(at, pieces, weight_ref):
    for flip, piece in zip((0, 2, 1, 3), pieces):
        rows = piece.shape[0]
        start = pl.multiple_of((device_of(at) ^ flip) * rows, 16)
        weight_ref[pl.ds(start, rows), :] = piece[...]
    return weight_ref[...]


def pieces_in(pieces, step, firsts):
    return [(piece, (piece.shape[0], step), lambda j, *_, k=k: (0, k + j)) for piece, k in zip(pieces, firsts)]


def lines_in_kernel(at, own_ref, far_ref, embeds_ref, weight_ref, lines_ref, up_ref):
    share = D // 4
    extra = up_ref.shape[1] // D
    for flip, shares_ref, first in ((0, own_ref, 0), (2, own_ref, 16), (1, far_ref, 0), (3, far_ref, 16)):
        device = device_of(at) ^ flip
        rows = shares_ref[first : first + 16, :].astype(F32)
        piece = lambda i, rows=rows: rows[i // 4 : i // 4 + 1, i % 4 * share : (i % 4 + 1) * share]
        place = pl.ds(pl.multiple_of(device * share, share), share)
        for i in range(8):
            lines_ref[i : i + 1, place] = piece(i if i < 3 else i + extra)
        for e in range(extra):
            start = pl.multiple_of((device * extra + e) * share, share)
            up_ref[:, pl.ds(start, share)] = piece(3 + e)
    lines_ref[EMBED : EMBED + 1, :] = embeds_ref[pl.ds(at[CHIP], 1), :]
    lines_ref[WEIGHT:LINES, :] = jnp.broadcast_to(weight_ref[...], (LINES - WEIGHT, D))


def key_value_kernel(at, mine_ref, got_ref, lines_ref, *refs):
    *pieces, keys_ref, values_ref, weight_ref, rounded_ref = refs
    j = pl.program_id(0)

    @pl.when(j == 0)
    def _():
        half = mine_ref.shape[0]
        embed = line(lines_ref, EMBED)
        rounded_ref[:half, :] = (mine_ref[...].astype(F32) + embed).astype(BF16)
        rounded_ref[half:, :] = (got_ref[...].astype(F32) + embed).astype(BF16)

    product = dot(rounded_ref[...], order_rows(at, pieces, weight_ref))

    @pl.when(j == 0)
    def _():
        keys_ref[...] = product.astype(BF16)

    @pl.when(j == 1)
    def _():
        values_ref[...] = (product + line(lines_ref, VALUE_BIAS)).astype(BF16)


def query_kernel(at, rounded_ref, lines_ref, *refs):
    *pieces, _, out_ref, weight_ref = refs
    weight = order_rows(at, pieces, weight_ref)
    out_ref[...] = (dot(rounded_ref[...], weight) + line(lines_ref, QUERY_BIAS)).astype(BF16)


def head_mask(head):
    return lax.broadcasted_iota(jnp.int32, (1, GROUP), 1) // HEAD_DIM == head


def attend_kernel(_, q_ref, k1_ref, v1_ref, k2_ref, v2_ref, *refs):
    out_ref, lse_ref = refs[-2:]
    keys = jnp.concatenate([k1_ref[...], k2_ref[...]], axis=0)
    values_t = jnp.concatenate([v1_ref[...], v2_ref[...]], axis=0).T
    queries = q_ref[...] * jnp.asarray(HEAD_DIM**-0.5, BF16)
    outs = []
    for head in range(GROUP_HEADS):
        masked = jnp.where(head_mask(head), queries, jnp.zeros_like(queries))
        scores = dot_back(keys, masked)
        peak = jnp.max(scores, axis=0, keepdims=True)
        exponent = jnp.exp(scores - peak)
        summed = total(exponent)
        attention = (exponent * (1.0 / summed)).astype(BF16)
        lse_ref[0, head : head + 1, :] = peak + jnp.log(summed)
        outs.append(dot(values_t[head * HEAD_DIM : (head + 1) * HEAD_DIM, :], attention))
    out_ref[...] = jnp.concatenate(outs, axis=0).astype(BF16).T


def output_kernel(at, rounded_ref, mixed_ref, mine_ref, got_ref, lines_ref, *refs):
    *pieces, weight_ref, unit_ref, scale_ref, low_ref, away_ref = refs
    product = dot(mixed_ref[...], order_rows(at, pieces, weight_ref))
    half = mine_ref.shape[0]
    for start, tokens_ref in ((0, mine_ref), (half, got_ref)):
        place = pl.ds(start, half)
        hidden = tokens_ref[...].astype(F32) + line(lines_ref, EMBED)
        unit, scale = normalise(hidden + (product[start : start + half, :] + line(lines_ref, OUTPUT_BIAS)))
        unit_ref[place, :] = unit
        scale_ref[place, :] = scale
        low_ref[place, :] = (unit * line(lines_ref, GAIN1) + line(lines_ref, SHIFT1)).astype(BF16)
    width = D // 4
    for k, left_ref in enumerate((low_ref, rounded_ref, mixed_ref)):
        for flip in (1, 0):
            column = pl.multiple_of(their(flip, at) * width, width)
            block = 2 * k + 1 - flip
            away_ref[:, block * width : (block + 1) * width] = left_ref[:, pl.ds(column, width)]


def feed_forward_kernel(
    at, low_ref, bias_ref, unit1_ref, scale1_ref, mine_ref, got_ref, lines_ref, down_ref, output_ref, *refs
):
    pieces, refs = refs[:4], refs[4:]
    active_ref, active_away_ref, final_ref, away_ref, delta_ref, up_delta_ref, down_sums_ref, up_sums_ref = refs[:8]
    input_ref, out_ref, rights_ref, mixed_ref, first_sums_ref, up_all, active_all, slope_all, sum_ref = refs[8:]
    j = pl.program_id(0)
    row = lambda i: line(lines_ref, i)
    half = mine_ref.shape[0]

    @pl.when(j < 4)
    def _():
        weight = order_rows(at, pieces, up_all.at[j])
        for start in (0, half):
            place = pl.ds(start, half)
            active, slope = gelu_and_slope(dot(low_ref[place, :], weight) + bias_ref[...])
            active_ref[place, :] = active.astype(BF16)
            slope_all[j, place, :] = slope.astype(BF16)
        active_all[j] = active_ref[...]

    for flip in (1, 0):

        @pl.when(j == their(flip, at))
        def _(flip=flip):
            width = active_ref.shape[1]
            active_away_ref[:, (1 - flip) * width : (2 - flip) * width] = active_ref[...]

    @pl.when(j == 4)
    def _():
        sum_ref[...] = dot(active_all[0], down_ref[...])

    @pl.when((j > 4) & (j < 8))
    def _():
        sum_ref[...] += dot(active_all[j - 4], down_ref[...])

    @pl.when(j == 7)
    def _():
        sums = [0.0, 0.0, 0.0]
        for start, upstream_ref, one_ref in ((0, mine_ref, final_ref), (half, got_ref, away_ref)):
            place = pl.ds(start, half)
            first_norm = unit1_ref[place, :] * row(GAIN1) + row(SHIFT1)
            unit, scale = normalise(first_norm + (sum_ref[place, :] + row(DOWN_BIAS)))
            one_ref[...] = (unit * row(GAIN2) + row(SHIFT2)).astype(BF16)
            cotangent = upstream_ref[...].astype(F32) * row(WEIGHT)
            grad = normalise_back(unit, scale, row(GAIN2), cotangent)
            delta = grad.astype(BF16)
            sum_ref[place, :] = grad
            delta_ref[place, :] = delta
            parts = (cotangent * unit, cotangent, delta.astype(F32))
            sums = [one + total(part) for one, part in zip(sums, parts)]
        for i, one in enumerate(sums):
            down_sums_ref[i : i + 1, :] = one

    @pl.when(j >= 8)
    def _():
        k = j - 8
        delta = (dot_back(delta_ref[...], down_ref[...]) * slope_all[k].astype(F32)).astype(BF16)
        up_delta_ref[...] = delta
        up_sums_ref[pl.ds(k, 1), :] = total(delta.astype(F32))
        sum_ref[...] += dot_back(delta, up_all[k])

    @pl.when(j == 11)
    def _():
        sums = [0.0, 0.0, 0.0]
        for start in (0, half):
            place = pl.ds(start, half)
            grad, unit = sum_ref[place, :], unit1_ref[place, :]
            below = normalise_back(unit, scale1_ref[place, :], row(GAIN1), grad)
            delta = below.astype(BF16)
            input_ref[place, :] = below
            out_ref[place, :] = delta
            rights_ref[place, :] = delta
            mixed_ref[place, :] = dot_back(delta, output_ref[...]).astype(BF16)
            parts = (grad * unit, grad, delta.astype(F32))
            sums = [one + total(part) for one, part in zip(sums, parts)]
        for i, one in enumerate(sums):
            first_sums_ref[i : i + 1, :] = one


def attend_back_kernel(
    _, q_ref, k1_ref, v1_ref, k2_ref, v2_ref, lse_ref, grad_ref, *refs
):
    dq_ref, rights_ref, near_ref, far_ref, p_all, ds_all = refs[-6:]
    half, tokens = k1_ref.shape[0], q_ref.shape[0]
    keys = jnp.concatenate([k1_ref[...], k2_ref[...]], axis=0)
    values = jnp.concatenate([v1_ref[...], v2_ref[...]], axis=0)
    keys_t = keys.T
    queries = q_ref[...] * jnp.asarray(HEAD_DIM**-0.5, BF16)
    grads = grad_ref[...]
    query_parts, grad_parts, dq_parts = [], [], []
    for head in range(GROUP_HEADS):
        query_one = jnp.where(head_mask(head), queries, jnp.zeros_like(queries))
        grad_one = jnp.where(head_mask(head), grads, jnp.zeros_like(grads))
        attention = jnp.exp(dot_back(keys, query_one) - lse_ref[0, head : head + 1, :])
        prob_grad = dot_back(values, grad_one)
        weighted = total(attention * prob_grad)
        score_grad = (attention * (prob_grad - weighted)).astype(BF16)
        place = slice(head * tokens, (head + 1) * tokens)
        p_all[:, place] = attention.astype(BF16)
        ds_all[:, place] = score_grad
        dq_parts.append(dot(keys_t[head * HEAD_DIM : (head + 1) * HEAD_DIM, :], score_grad))
        query_parts.append(query_one)
        grad_parts.append(grad_one)
    value_grad = dot(p_all[...], jnp.concatenate(grad_parts, axis=0))
    key_grad = dot(ds_all[...], jnp.concatenate(query_parts, axis=0))
    dq_ref[...] = (jnp.concatenate(dq_parts, axis=0) * HEAD_DIM**-0.5).astype(BF16).T
    rights_ref[...] = dq_ref[...]
    near_ref[:, :GROUP] = key_grad[:half, :]
    near_ref[:, GROUP:] = value_grad[:half, :]
    far_ref[:, :GROUP] = key_grad[half:, :].astype(BF16)
    far_ref[:, GROUP:] = value_grad[half:, :].astype(BF16)


def delta_kernel(_, *refs):
    groups = D // GROUP
    nears, fars = refs[:groups], refs[groups : 2 * groups]
    queries_ref, __, keys_ref, values_ref, rights_ref, sums_ref = refs[2 * groups :]
    i = pl.program_id(0)
    for g in range(groups):
        place = slice(g * GROUP, (g + 1) * GROUP)
        rights_ref[:, place] = (nears[g][...] + fars[g][...].astype(F32)).astype(BF16)
    sums_ref[pl.ds(1 + i, 1), :] = total(rights_ref[...].astype(F32))

    @pl.when(i == 0)
    def _():
        sums_ref[0:1, :] = total(queries_ref[...].astype(F32))
        keys_ref[...] = rights_ref[...]

    @pl.when(i == 1)
    def _():
        values_ref[...] = rights_ref[...]


def input_query_kernel(_, delta_ref, weight_ref, grad_ref, out_ref):
    out_ref[...] = grad_ref[...] + dot_back(delta_ref[...], weight_ref[...])


def input_kernel(_, delta_ref, weight_ref, grad_ref, mine_ref, away_ref, time_ref, sum_ref):
    j = pl.program_id(0)
    part = dot_back(delta_ref[...], weight_ref[...])

    @pl.when(j == 0)
    def _():
        sum_ref[...] = grad_ref[...] + part

    @pl.when(j > 0)
    def _():
        sum_ref[...] += part

    @pl.when(j == pl.num_programs(0) - 1)
    def _():
        half = mine_ref.shape[0]
        mine_ref[...] = sum_ref[:half, :]
        away_ref[...] = sum_ref[half:, :].astype(BF16)
        time_ref[...] = total(sum_ref[...])


def grad_block(which, left_ref, right_ref, far_left_ref, fars, sum_ref, *more):
    for k, far_ref in enumerate(fars):

        @pl.when((which == k) if len(fars) > 1 else (which >= 0))
        def _(far_ref=far_ref):
            sum_ref[...] = outer(far_left_ref[...], far_ref[...])

    block = outer(left_ref[...], right_ref[...]) + sum_ref[...]
    for one_ref in more:
        block = block + one_ref[...].astype(F32)
    return block.astype(BF16)


def grad_x_kernel(_, left_ref, right_ref, far_left_ref, *refs):
    *fars, out_ref, sum_ref = refs
    out_ref[...] = grad_block(pl.program_id(0), left_ref, right_ref, far_left_ref, fars, sum_ref)


def grad_y_kernel(at_ref, left_ref, right_ref, far_left_ref, other_ref, *refs):
    *fars, away_ref, keep_ref, sum_ref = refs
    i, half = pl.program_id(0), pl.num_programs(0) // 2
    which = jnp.where(i < half, 1 - at_ref[SIDE_Y], at_ref[SIDE_Y])
    block = grad_block(which, left_ref, right_ref, far_left_ref, fars, sum_ref, other_ref)

    @pl.when(i < half)
    def _():
        away_ref[...] = block

    @pl.when(i >= half)
    def _():
        keep_ref[...] = block


def fold_kernel(_, keep1_ref, keep2_ref, away1_ref, away2_ref, keep_ref, away_ref):
    keep_ref[...] = (keep1_ref[...].astype(F32) + keep2_ref[...].astype(F32)).astype(BF16)
    away_ref[...] = (away1_ref[...].astype(F32) + away2_ref[...].astype(F32)).astype(BF16)


def add_kernel(_, one_ref, two_ref, out_ref):
    out_ref[...] = (one_ref[...].astype(F32) + two_ref[...].astype(F32)).astype(out_ref.dtype)


def join_kernel(at_ref, mine_ref, other_ref, out_ref):
    rows = mine_ref.shape[0]
    out_ref[pl.ds(pl.multiple_of(at_ref[SIDE_Z] * rows, 16), rows), :] = mine_ref[...]
    out_ref[pl.ds(pl.multiple_of((1 - at_ref[SIDE_Z]) * rows, 16), rows), :] = other_ref[...]


def finish_kernel(_, mine_ref, other_ref, *refs):
    out_ref = refs[-1]
    i, half = pl.program_id(0), pl.num_programs(0) // 2

    @pl.when(i < half)
    def _():
        out_ref[...] = mine_ref[...].astype(F32)

    @pl.when(i >= half)
    def _():
        out_ref[...] = other_ref[...].astype(F32)


def copy_kernel(_, in_ref, out_ref):
    out_ref[...] = in_ref[...]


def two_kernel(at, mine_ref, other_ref, first_ref, second_ref):
    first = at[SIDE_Y] == 0
    mine, other = mine_ref[...].astype(F32), other_ref[...].astype(F32)
    first_ref[...] = jnp.where(first, mine, other)
    second_ref[...] = jnp.where(first, other, mine)


def pair_kernel(_, mine_ref, received_ref, out_ref):
    @pl.when(pl.program_id(0) == 0)
    def _():
        out_ref[...] = mine_ref[...]

    @pl.when(pl.program_id(0) == 1)
    def _():
        out_ref[...] = received_ref[...].astype(out_ref.dtype)


def append_kernel(_, first_ref, *refs):
    *vectors, out_ref, small_ref = refs
    rows = first_ref.shape[0]
    out_ref[:rows, :] = first_ref[...]
    flat = jnp.concatenate([vector[...].astype(F32).reshape(1, -1) for vector in vectors], axis=1)
    lines = [flat[:, start : start + D] for start in range(0, flat.shape[1], D)]
    small = jnp.concatenate(lines + [jnp.zeros((16 - len(lines), D), F32)], axis=0).astype(BF16)
    small_ref[...] = small
    out_ref[rows:, :] = small


def side_by_side_kernel(_, *refs):
    out_ref, at = refs[-1], 0
    for piece in refs[:-1]:
        out_ref[:, at : at + piece.shape[1]] = piece[...]
        at += piece.shape[1]


def split_kernel(_, in_ref, first_ref, second_ref):
    rows = first_ref.shape[0]
    first_ref[...] = in_ref[:rows, :]
    second_ref[...] = in_ref[rows:, :]


def parity(at):
    return (at[SIDE_Y] + at[SIDE_Z]) % 2


def remote_kernel(at, half_ref, third_ref, fourth_ref, *outs):
    columns = 0
    for out_ref in outs:
        width = out_ref.shape[1]
        place = slice(columns, columns + width)
        columns += width
        remote_rows(at, half_ref.at[:, place], third_ref.at[:, place], fourth_ref.at[:, place], out_ref)


def remote_rows(at, half_ref, third_ref, fourth_ref, out_ref):
    half, quarter = half_ref.shape[0], third_ref.shape[0]
    missing = (1 - parity(at)) * half
    out_ref[pl.ds(pl.multiple_of(parity(at) * half, 16), half), :] = half_ref[...]
    out_ref[pl.ds(pl.multiple_of(missing, 16), quarter), :] = third_ref[...]
    out_ref[pl.ds(pl.multiple_of(missing + quarter, 16), quarter), :] = fourth_ref[...]


def lines_kernel(at, down_ref, first_ref, delta_ref, up_ref, time_ref, out_ref):
    out_ref[0:8, :] = down_ref[...]
    out_ref[8:16, :] = first_ref[...]
    out_ref[16:24, :] = delta_ref[...]
    out_ref[24:28, :] = up_ref[0:4, :]
    row = lax.broadcasted_iota(jnp.int32, (4, D), 0)
    out_ref[28:32, :] = jnp.where(row == at[CHIP], time_ref[...], 0.0)


def per_device(n_dp, inputs, timestep, bucket_count, upstream, *params):
    query_weight, key_weight, value_weight, output_weight, up_weight, down_weight = params[:6]
    vectors = params[6:]
    device = lax.axis_index("fsdp")
    chip, core = device // 2, device % 2
    bucket = lax.axis_index("dp")
    half = inputs.shape[1]
    tokens = 2 * half
    hidden_width = up_weight.shape[1]
    side_y, side_z = bucket % 2, (bucket // 2) % 2
    place = jnp.stack([chip, core, side_y, side_z]).astype(jnp.int32)
    run = functools.partial(run_kernel, place)

    def swap(value, axis, bit):
        size = 4 if axis == "fsdp" else n_dp
        return lax.ppermute(value, axis, [(i, i ^ bit) for i in range(size)])

    swap_core = lambda value: swap(value, "fsdp", 1)
    swap_chip = lambda value: swap(value, "fsdp", 2)
    swap_y = lambda value: swap(value, "dp", 1)
    swap_z = lambda value: swap(value, "dp", 2)

    def pick(array, flip, *later_than):
        _, rows, columns = array.shape
        ins = [(array, (None, rows, columns), lambda _, at: (at[CHIP] ^ flip, 0, 0))]
        return run("pick", copy_kernel, (1,), ins, [whole_out((rows, columns), array.dtype)], later_than)

    def pack(arrays, *later_than):
        shape = (arrays[0].shape[0], sum(array.shape[1] for array in arrays))
        return run("pack", side_by_side_kernel, (1,), [whole(a) for a in arrays], [whole_out(shape, BF16)], later_than)

    def cut(shards, *later_than):
        rows = shards[0].shape[0]
        columns = sum(shard.shape[1] for shard in shards)
        ins = [(shard, (rows // 2, shard.shape[1]), lambda _, at: (parity(at), 0)) for shard in shards]
        outs = [whole_out((rows // 2, columns), BF16)]
        return run("cut", side_by_side_kernel, (1,), ins, outs, later_than)

    def split(first, *later_than):
        rows, columns = first.shape
        outs = [whole_out((rows // 2, columns), BF16)] * 2
        to_y, to_z = run("split", split_kernel, (1,), [whole(first)], outs, later_than)
        return (first, swap_y(to_y), swap_z(to_z)), to_y

    def remote(parts, widths, *later_than):
        outs = [whole_out((2 * parts[0].shape[0], width), BF16) for width in widths]
        return run("remote", remote_kernel, (1,), [whole(part) for part in parts], outs, later_than)

    tokens_away, small = run(
        "pick", append_kernel, (1,),
        [(inputs, (None, half, D), lambda _, at: (at[CHIP] ^ 1, 0, 0))] + [whole(vector) for vector in vectors],
        [whole_out((half + 16, D), BF16), whole_out((16, D), BF16)],
    )
    tokens_got = swap_chip(tokens_away)
    got_half = (tokens_got, (half, D), lambda *_: (0, 0))
    three = (query_weight, key_weight, value_weight)
    two_weights = (output_weight, up_weight)
    three_cut = cut(three, tokens_away)
    three_first = swap_chip(three_cut)
    three_own = pack(three, three_cut)
    three_sibling = swap_core(three_own)
    two_own = pack(two_weights, three_own)
    two_sibling = swap_core(two_own)
    two_cut = cut(two_weights, tokens_got, two_own)
    two_first = swap_chip(two_cut)
    down_copy = run("copy", copy_kernel, (1,), [whole(down_weight)], [whole_out(down_weight.shape, BF16)], (two_cut,))
    live = chip < bucket_count[bucket]
    seq_weight = live.astype(F32) * (2 * n_dp / jnp.sum(bucket_count).astype(F32))
    small_two = jnp.concatenate([small, tokens_got[half:]], axis=0)
    small_far = swap_core(small_two)
    three_parts, split_done = split(three_first, three_sibling, two_sibling, down_copy, small_far)
    down_matrix = lax.all_gather(down_copy, "fsdp", axis=0, tiled=True)
    tokens_mine = pick(inputs, 0, split_done)
    query_remote, kv_remote = remote(three_parts, (D, 2 * D), tokens_mine)
    lines, up_bias = run(
        "lines_in", lines_in_kernel, (1,),
        [whole(a) for a in (small_two, small_far, sinusoid(timestep), seq_weight.reshape(1, 1))],
        [whole_out((LINES, D), F32), whole_out((1, hidden_width), F32)], (kv_remote,),
    )
    kv_pieces = [three_own, kv_remote, three_sibling, swap_core(kv_remote)]
    query_pieces = [three_own, query_remote, three_sibling, swap_core(query_remote)]
    keys, values, qkv_matrix, lefts = run(
        "key_value", key_value_kernel, (2,),
        [whole(tokens_mine), got_half, whole(lines)] + pieces_in(kv_pieces, D, (1, 0, 1, 0)),
        [
            whole_out((tokens, D), BF16),
            whole_out((tokens, D), BF16),
            ((D, 3 * D), BF16, (D, D), lambda j, *_: (0, 1 + j)),
            ((tokens, 2 * D), BF16, (tokens, D), lambda j, *_: (0, 0)),
        ],
    )
    far_keys, far_values = swap_core(keys), swap_core(values)
    queries, qkv_matrix = run(
        "query", query_kernel, (1,),
        [(lefts, (tokens, D), lambda j, *_: (0, 0)), whole(lines)] + pieces_in(query_pieces, D, (0, 0, 0, 0))
        + [(qkv_matrix, None, None)],
        [((tokens, D), BF16, (tokens, D), lambda j, *_: (0, 0)), ((D, 3 * D), BF16, (D, D), lambda j, *_: (0, 0))],
        aliases={2 + len(query_pieces): 1},
    )
    groups = D // GROUP
    group_of = lambda array, first: (array, (array.shape[0], GROUP), lambda g, *_: (0, first + g))

    def attend(first, count, lefts, lse, *later_than):
        return run(
            "attend", attend_kernel, (count,),
            [group_of(a, first) for a in (queries, keys, values, far_keys, far_values)] + [(lefts, None, None)]
            + ([] if lse is None else [(lse, None, None)]),
            [
                ((tokens, 2 * D), BF16, (tokens, GROUP), lambda g, *_: (0, groups + first + g)),
                ((groups, GROUP_HEADS, tokens), F32, (1, GROUP_HEADS, tokens), lambda g, *_: (first + g, 0, 0)),
            ],
            later_than, aliases={5: 0} if lse is None else {5: 0, 6: 1}, vmem=32,
        )

    lefts, lse = attend(0, groups // 2, lefts, None)
    two_parts, split_done = split(two_first, lse)
    upstream_away = pick(upstream, 1, split_done)
    upstream_got = swap_chip(upstream_away)
    lefts, lse = attend(groups // 2, groups // 2, lefts, lse, upstream_away)
    two_remote = remote(two_parts, (two_own.shape[1],), lse)
    upstream_mine = pick(upstream, 0, two_remote)
    two_pieces = [two_own, two_remote, two_sibling, swap_core(two_remote)]
    output_matrix, unit1, scale1, first_low, lefts_away = run(
        "output", output_kernel, (1,),
        [(lefts, (tokens, D), lambda j, *_: (0, 0)), (lefts, (tokens, D), lambda j, *_: (0, 1))]
        + [whole(tokens_mine), got_half, whole(lines)]
        + pieces_in(two_pieces, D, (0, 0, 0, 0)),
        [
            whole_out((D, D), BF16),
            whole_out((tokens, D), F32),
            whole_out((tokens, 1), F32),
            whole_out((tokens, D), BF16),
            whole_out((tokens, 6 * D // 4), BF16),
        ],
        (upstream_mine,),
    )
    lefts_away = swap_core(lefts_away)
    width = hidden_width // 4
    hidden_block = lambda j: jnp.minimum(j, 3)
    results = run(
        "feed_forward", feed_forward_kernel, (12,),
        [held(first_low), (up_bias, (1, width), lambda j, *_: (0, hidden_block(j))), held(unit1), held(scale1)]
        + [held(upstream_mine), held(upstream_got), held(lines)]
        + [(down_matrix, (width, D), lambda j, *_: (jnp.where(j < 4, 0, j % 4), 0)), held(output_matrix)]
        + [(piece, (piece.shape[0], width), lambda j, *_: (0, D // width + hidden_block(j))) for piece in two_pieces],
        [
            ((tokens, hidden_width), BF16, (tokens, width), lambda j, *_: (0, hidden_block(j))),
            whole_out((tokens, 2 * width), BF16),
            whole_out((half, D), BF16),
            whole_out((half, D), BF16),
            whole_out((tokens, D), BF16),
            ((tokens, hidden_width), BF16, (tokens, width), lambda j, *_: (0, jnp.maximum(j - 8, 0))),
            whole_out((8, D), F32),
            whole_out((8, D), F32),
            whole_out((tokens, D), F32),
            whole_out((tokens, D), BF16),
            ((tokens, 4 * D), BF16, (tokens, D), lambda j, *_: (0, 3)),
            whole_out((tokens, D), BF16),
            whole_out((8, D), F32),
        ],
        (),
        [
            pltpu.VMEM((4, D, width), BF16),
            pltpu.VMEM((4, tokens, width), BF16),
            pltpu.VMEM((4, tokens, width), BF16),
            pltpu.VMEM((tokens, D), F32),
        ],
    )
    activated, active_away, final_mine, final_away, down_delta, up_delta, down_sums, up_sums = results[:8]
    input_part, out_delta, rights, mixed_grad, first_sums = results[8:]
    active_away, down_far = swap_core(active_away), swap_core(down_delta)
    up_far, out_far = swap_core(up_delta), swap_core(out_delta)

    block_rows = D // 4

    class Grads:
        def __init__(self, left, right, send, keep, fars, near, right_column):
            self.left, self.right, self.send_far, self.keep_far = left, right, send, keep
            self.fars, self.near, self.right_column = fars, near, right_column

        def ins(self, flip, far, block):
            far_left, far_column = far
            shard = lambda at: 2 * (at[CHIP] ^ flip) + at[CORE]
            return [
                (self.left, (tokens, block_rows), lambda i, at: (0, self.near(shard(at), block(i, at)))),
                (self.right, (tokens, D), lambda i, at: (0, self.right_column(block(i, at)))),
                (far_left, (tokens, block_rows), lambda i, at: (0, far_column(block(i, at)))),
            ]

        def far_ins(self, block, first, count):
            if len(self.fars) > 1:
                return [whole(a) for a in self.fars[first : first + count]]
            return [(self.fars[0], (tokens, D), lambda i, at: (0, self.right_column(block(i, at))))]

        def four(self, name, body, flip, far, more, *later_than):
            out = ((4 * block_rows, D), BF16, (block_rows, D), lambda i, at: (i, 0))
            block = lambda i, at: i
            ins = self.ins(flip, far, block) + more + self.far_ins(block, 0, 4)
            return run(name, body, (4,), ins, [out], later_than, [pltpu.VMEM((block_rows, D), F32)])

        def start(self, *later_than):
            sent = self.four("grad_x", grad_x_kernel, 1, self.send_far, [], *later_than)
            self.got = swap_chip(sent)
            return sent

    class Chunk:
        def __init__(self, grads, first, count):
            self.grads, self.first, self.half = grads, first, count // 2

        def over_y(self, last):
            grads, first, half = self.grads, self.first, self.half
            block = lambda i, at: first + jnp.where(
                i < half, (1 - at[SIDE_Y]) * half + i, at[SIDE_Y] * half + i - half
            )
            other = (grads.got, (block_rows, D), lambda i, at: (block(i, at), 0))
            shape = (half * block_rows, D)
            away, self.keep = run(
                "grad_y", grad_y_kernel, (2 * half,),
                grads.ins(0, grads.keep_far, block) + [other] + grads.far_ins(block, first, 2),
                [
                    (shape, BF16, (block_rows, D), lambda i, at: (jnp.minimum(i, half - 1), 0)),
                    (shape, BF16, (block_rows, D), lambda i, at: (jnp.maximum(i - half, 0), 0)),
                ],
                (last,), [pltpu.VMEM((block_rows, D), F32)],
            )
            self.got = swap_y(away)
            return self.keep

        def over_z(self, last):
            block = (self.keep.shape[0] // 2, D)
            kept = [(a, block, lambda _, at: (at[SIDE_Z], 0)) for a in (self.keep, self.got)]
            given = [(a, block, lambda _, at: (1 - at[SIDE_Z], 0)) for a in (self.keep, self.got)]
            self.keep, away = run("grad_z", fold_kernel, (1,), kept + given, [whole_out(block, BF16)] * 2, (last,))
            self.got = swap_z(away)
            return self.keep

        def add(self, bit, last):
            ins = [whole(self.keep), whole(self.got)]
            self.keep = run("grad_add", add_kernel, (1,), ins, [whole_out(self.keep.shape, BF16)], (last,))
            self.got = swap(self.keep, "dp", bit)
            return self.keep

        def add_high(self, last):
            for bit in high_bits:
                last = self.add(bit, last)
            return last

        def add_low(self, last):
            return self.add(2, last)

        def back(self, last):
            ins = [whole(self.keep), whole(self.got)]
            shape = (2 * self.keep.shape[0], D)
            self.keep = run("grad_join", join_kernel, (1,), ins, [whole_out(shape, BF16)], (last,))
            self.got = swap_y(self.keep)
            return self.keep

        def finish(self, last, shape, index):
            half = self.half
            ins = [
                (self.keep, (block_rows, D), lambda i, at: (jnp.minimum(i, half - 1), 0)),
                (self.got, (block_rows, D), lambda i, at: (jnp.maximum(i - half, 0), 0)),
            ]
            place = lambda i, at: jnp.where(i < half, at[SIDE_Y] * half + i, (1 - at[SIDE_Y]) * half + i - half)
            out = (shape, F32, (block_rows, D), lambda i, at: index(place(i, at)))
            return run("grad_out", finish_kernel, (2 * half,), ins, [out], (last,))

    def pair_of(mine, received, dtype, last):
        out = ((2, half, D), dtype, (None, half, D), lambda i, at: (at[CHIP] ^ i, 0, 0))
        return run("pair", pair_kernel, (2,), [whole(mine), whole(received)], [out], (last,))

    high_bits = [1 << i for i in range(2, n_dp.bit_length()) if 1 << i < n_dp]
    relay = lambda array, last: run("relay", copy_kernel, (1,), [whole(array)], [whole_out(array.shape, array.dtype)], (last,))

    grads_down = Grads(
        activated, down_delta, (active_away, lambda b: b), (active_away, lambda b: 4 + b), [down_far],
        lambda shard, b: shard * (hidden_width // D) + b, lambda b: 0,
    )
    grads_up = Grads(
        first_low, up_delta, (lefts_away, lambda b: 0), (lefts_away, lambda b: 1), [up_far],
        lambda shard, b: shard, lambda b: b,
    )

    def attend_back(first, count, later_than, rights, query_delta):
        return run(
            "attend_back", attend_back_kernel, (count,),
            [group_of(a, first) for a in (queries, keys, values, far_keys, far_values)]
            + [(lse, (1, GROUP_HEADS, tokens), lambda g, *_: (first + g, 0, 0)), group_of(mixed_grad, first)]
            + [(rights, None, None)] + ([] if query_delta is None else [(query_delta, None, None)]),
            [
                ((tokens, D), BF16, (tokens, GROUP), lambda g, *_: (0, first + g)),
                ((tokens, 4 * D), BF16, (tokens, GROUP), lambda g, *_: (0, first + g)),
                ((tokens, 2 * count * GROUP), F32, (tokens, 2 * GROUP), lambda g, *_: (0, g)),
                ((tokens, 2 * count * GROUP), BF16, (tokens, 2 * GROUP), lambda g, *_: (0, g)),
            ],
            later_than, [pltpu.VMEM((2 * tokens, GROUP_HEADS * tokens), BF16)] * 2, aliases={7: 1} if query_delta is None else {7: 1, 8: 0},
        )

    first_call = 1
    query_delta, rights, near1, far1 = attend_back(0, first_call, (mixed_grad,), rights, None)
    far1 = swap_core(far1)
    last = grads_down.start(near1)
    last = grads_up.start(last, out_far)
    query_delta, rights, near2, far2 = attend_back(first_call, groups - first_call, (last, far1), rights, query_delta)
    far2, query_far = swap_core(far2), swap_core(query_delta)
    last = input_part = run(
        "input_query", input_query_kernel, (2,),
        [
            (query_delta, (half, D), lambda i, *_: (i, 0)),
            (qkv_matrix, (D, D), lambda i, *_: (0, 0)),
            (input_part, (half, D), lambda i, *_: (i, 0)),
        ],
        [((tokens, D), F32, (half, D), lambda i, *_: (i, 0))], (near2,),
    )
    key_delta, value_delta, rights, delta_sums = run(
        "delta", delta_kernel, (2,),
        [
            (a, (tokens, GROUP), lambda i, *_, g=g: (0, 2 * g + i))
            for one, two in ((near1, near2), (far1, far2))
            for a, count in ((one, first_call), (two, groups - first_call))
            for g in range(count)
        ]
        + [whole(query_delta), (rights, None, None)],
        [
            whole_out((tokens, D), BF16),
            whole_out((tokens, D), BF16),
            ((tokens, 4 * D), BF16, (tokens, D), lambda i, *_: (0, 1 + i)),
            whole_out((8, D), F32),
        ],
        (last,), aliases={2 * groups + 1: 2},
    )
    key_far, value_far = swap_core(key_delta), swap_core(value_delta)
    step = D
    input_mine, input_away, time_sum = run(
        "input", input_kernel, (2,),
        [(rights, (tokens, D), lambda j, *_: (0, 1 + j)), (qkv_matrix, (D, D), lambda j, *_: (0, 1 + j)), whole(input_part)],
        [whole_out((half, D), F32), whole_out((half, D), BF16), whole_out((1, D), F32)],
        (delta_sums,), [pltpu.VMEM((tokens, D), F32)],
    )
    last_one = lambda b: jnp.where(b == 3, 1, 0)
    grads_four = Grads(
        lefts, rights, (lefts_away, lambda b: 2 + 2 * last_one(b)), (lefts_away, lambda b: 3 + 2 * last_one(b)),
        [query_far, key_far, value_far, out_far], lambda shard, b: shard + 4 * last_one(b), lambda b: b,
    )
    down, up = Chunk(grads_down, 0, 4), Chunk(grads_up, 0, 4)
    last = down.over_y(time_sum)
    last = grads_four.start(last)

    packed = run(
        "lines", lines_kernel, (1,), [whole(a) for a in (down_sums, first_sums, delta_sums, up_sums, time_sum)],
        [whole_out((32, D), F32)], (last,),
    )
    hops = [("fsdp", 1), ("fsdp", 2)] + [("dp", 1 << i) for i in range(n_dp.bit_length() - 1)]
    line_parts, line_got = [packed], [swap(packed, *hops[0])]

    def add_lines(last):
        ins = [whole(line_parts[-1]), whole(line_got[-1])]
        line_parts.append(run("lines_add", add_kernel, (1,), ins, [whole_out((32, D), F32)], (last,)))
        if len(line_parts) <= len(hops) - 0 and len(line_got) < len(hops):
            line_got.append(swap(line_parts[-1], *hops[len(line_got)]))
        return line_parts[-1]

    qk, vo = Chunk(grads_four, 0, 2), Chunk(grads_four, 2, 2)
    last = down.over_z(packed)
    last = add_lines(last)
    last = up.over_y(last)
    last = down.add_high(last)
    last = up.over_z(last)
    last = down.add_low(last)
    last = qk.over_y(last)
    last = vo.over_y(last)
    last = up.add_high(last)
    last = down.back(last)
    last = qk.over_z(last)
    last = vo.over_z(last)
    last = add_lines(last)
    last = final_away = relay(final_away, last)
    final_got = swap_chip(final_away)
    last = qk.add_high(last)
    last = vo.add_high(last)
    last = up.add_low(last)
    last = add_lines(last)
    last = down_grad = down.finish(last, down_weight.shape, lambda s: (s, 0))
    last = qk.add_low(last)
    last = vo.add_low(last)
    last = input_away = relay(input_away, last)
    input_got = swap_chip(input_away)
    last = up.back(last)
    last = final = pair_of(final_mine, final_got, BF16, last)
    last = qk.back(last)
    last = vo.back(last)
    while len(line_parts) < len(hops):
        last = add_lines(last)
    last = input_gradient = pair_of(input_mine, input_got, F32, last)
    last = up_grad = up.finish(last, up_weight.shape, lambda s: (0, s))
    last = add_lines(last)

    def two(chunk, last):
        outs = [whole_out((block_rows, D), F32)] * 2
        return run("two", two_kernel, (1,), [whole(chunk.keep), whole(chunk.got)], outs, (last,))

    query_grad, key_grad = two(qk, last)
    value_grad, output_grad = two(vo, query_grad)
    times = lax.dynamic_slice_in_dim(line_parts[2], device * (D // 4), D // 4, axis=1)
    time_gradient = times[28:30]
    packed = line_parts[-1]
    mine = lax.dynamic_slice_in_dim(packed, device * (D // 4), D // 4, axis=1)
    up_bias_grad = lax.dynamic_slice_in_dim(packed[24:28], device, 1, axis=0).reshape(-1)
    vector_grads = (mine[16], mine[18], mine[10], up_bias_grad, mine[2], mine[8], mine[9], mine[0], mine[1])

    return (
        final,
        input_gradient,
        time_gradient,
        query_grad,
        key_grad,
        value_grad,
        output_grad,
        up_grad,
        down_grad,
        *vector_grads,
    )


def solution(mesh):
    rows, wide, flat = P("dp", "fsdp", None), P("fsdp", None), P("fsdp")
    return jax.shard_map(
        functools.partial(per_device, mesh.shape["dp"]),
        mesh=mesh,
        in_specs=(rows, P("dp"), P(), rows) + (wide,) * 6 + (flat,) * 9,
        out_specs=(rows, rows, P("dp", "fsdp")) + (wide,) * 6 + (flat,) * 9,
        check_vma=False,
    )
```

```python
import functools
import math

import jax
import jax.numpy as jnp
from jax import lax
from jax.experimental import pallas as pl
from jax.experimental.pallas import tpu as pltpu
from jax.sharding import PartitionSpec as P

D = 1024
HEAD_DIM = 64
GROUP = 256
GROUP_HEADS = GROUP // HEAD_DIM
F32 = jnp.float32
BF16 = jnp.bfloat16
ROWS_ROWS = (((0,), (0,)), ((), ()))
COLS_COLS = (((1,), (1,)), ((), ()))
ANY = pl.BlockSpec(memory_space=pl.ANY)
VMEM_MB = dict(grad_z=16,grad_add=16,grad_join=16,lines_add=16,lines=16,relay=16,grad_y=24)
COST = 10**11
MICROSECONDS = dict(
    pick=2, cut=2, pack=3, split=2, copy=2, relay=2, columns=2, remote=3, key_value=7, query=4, attend=9, output=6,
    feed_forward=40, two=2, grad_x=8, grad_y=5, grad_z=3, grad_add=2, grad_join=3,
    grad_out=3, attend_back=15, delta=5, input=8, input_query=5, lines_in=2, lines=2, lines_add=1, pair=3,
)


def run_kernel(place, name, body, grid, ins, outs, later_than=(), scratch=(), aliases=None, vmem=16):
    count, waits = len(ins), len(later_than)

    def kernel(*refs):
        body(*refs[: 1 + count], *refs[1 + count + waits :])

    def spec(block, index, *buffers):
        if block is None:
            return ANY
        modes = dict(pipeline_mode=pl.Buffered(buffers[0])) if buffers else {}
        return pl.BlockSpec(block, index, **modes)

    shapes = [jax.ShapeDtypeStruct(shape, dtype) for shape, dtype, _, _ in outs]
    out_specs = [spec(block, index) for _, _, block, index in outs]
    single = len(outs) == 1
    return pl.pallas_call(
        kernel,
        grid_spec=pltpu.PrefetchScalarGridSpec(
            num_scalar_prefetch=1,
            grid=grid,
            in_specs=[spec(*one[1:]) for one in ins] + [ANY] * waits,
            out_specs=out_specs[0] if single else out_specs,
            scratch_shapes=list(scratch),
        ),
        out_shape=shapes[0] if single else shapes,
        input_output_aliases={1 + i: o for i, o in (aliases or {}).items()},
        compiler_params=pltpu.CompilerParams(vmem_limit_bytes=VMEM_MB.get(name, 60) * 2**20),
        cost_estimate=pl.CostEstimate(flops=int(MICROSECONDS[name] * COST), bytes_accessed=0, transcendentals=0),
        name=name,
    )(place, *[one[0] for one in ins], *later_than)


CHIP, CORE, SIDE_Y, SIDE_Z = range(4)
LINES = 16
QUERY_BIAS, VALUE_BIAS, OUTPUT_BIAS, DOWN_BIAS, GAIN1, SHIFT1, GAIN2, SHIFT2, EMBED, WEIGHT = range(10)


def device_of(at):
    return 2 * at[CHIP] + at[CORE]


def their(flip, at):
    return 2 * (at[CHIP] ^ flip) + (at[CORE] ^ 1)


def line(lines_ref, i):
    return lines_ref[i : i + 1, :]


def whole(array):
    return (array, array.shape, lambda *_: (0,) * array.ndim)


def held(array):
    return (*whole(array), 1)


def whole_out(shape, dtype):
    return (shape, dtype, shape, lambda *_: (0,) * len(shape))


def sinusoid(timestep):
    halves = D // 2
    frequency = jnp.exp(jnp.arange(halves, dtype=F32) * (-math.log(10000.0) / halves))
    angles = timestep.astype(F32)[:, None] * frequency[None, :]
    return jnp.concatenate([jnp.sin(angles), jnp.cos(angles)], axis=1)


def dot(left, right):
    return jnp.dot(left, right, preferred_element_type=F32)


def dot_back(left, right):
    return lax.dot_general(left, right, COLS_COLS, preferred_element_type=F32)


def outer(left, right):
    return lax.dot_general(left, right, ROWS_ROWS, preferred_element_type=F32)


def total(rows):
    return jnp.sum(rows, axis=0, keepdims=True)


def mean(rows):
    return jnp.mean(rows, axis=-1, keepdims=True)


def normalise(residual):
    centered = residual - mean(residual)
    scale = lax.rsqrt(mean(centered * centered) + 1e-05)
    return centered * scale, scale


def normalise_back(unit, scale, gain, grad):
    scaled = grad * gain
    return scale * (scaled - mean(scaled) - unit * mean(scaled * unit))


def gelu_and_slope(upward):
    size = jnp.abs(upward) * (2.0**-0.5)
    bell = jnp.exp(-0.5 * (upward * upward))
    t = 1.0 / (1.0 + 0.3275911 * size)
    series = t * (
        0.254829592
        + t * (-0.284496736 + t * (1.421413741 + t * (-1.453152027 + t * 1.061405429)))
    )
    tail = 0.5 * series * bell
    cdf = jnp.where(upward >= 0, 1.0 - tail, tail)
    return upward * cdf, cdf + upward * (bell * (2 * math.pi) ** -0.5)


def order_rows(at, pieces, weight_ref):
    for flip, piece in zip((0, 2, 1, 3), pieces):
        rows = piece.shape[0]
        start = pl.multiple_of((device_of(at) ^ flip) * rows, 16)
        weight_ref[pl.ds(start, rows), :] = piece[...]
    return weight_ref[...]


def pieces_in(pieces, step, firsts):
    return [(piece, (piece.shape[0], step), lambda j, *_, k=k: (0, k + j)) for piece, k in zip(pieces, firsts)]


def lines_in_kernel(at, own_ref, far_ref, embeds_ref, weight_ref, lines_ref, up_ref):
    share = D // 4
    extra = up_ref.shape[1] // D
    for flip, shares_ref, first in ((0, own_ref, 0), (2, own_ref, 16), (1, far_ref, 0), (3, far_ref, 16)):
        device = device_of(at) ^ flip
        rows = shares_ref[first : first + 16, :].astype(F32)
        piece = lambda i, rows=rows: rows[i // 4 : i // 4 + 1, i % 4 * share : (i % 4 + 1) * share]
        place = pl.ds(pl.multiple_of(device * share, share), share)
        for i in range(8):
            lines_ref[i : i + 1, place] = piece(i if i < 3 else i + extra)
        for e in range(extra):
            start = pl.multiple_of((device * extra + e) * share, share)
            up_ref[:, pl.ds(start, share)] = piece(3 + e)
    lines_ref[EMBED : EMBED + 1, :] = embeds_ref[pl.ds(at[CHIP], 1), :]
    lines_ref[WEIGHT:LINES, :] = jnp.broadcast_to(weight_ref[...], (LINES - WEIGHT, D))


def key_value_kernel(at, mine_ref, got_ref, lines_ref, *refs):
    *pieces, keys_ref, values_ref, weight_ref, rounded_ref = refs
    j = pl.program_id(0)

    @pl.when(j == 0)
    def _():
        half = mine_ref.shape[0]
        embed = line(lines_ref, EMBED)
        rounded_ref[:half, :] = (mine_ref[...].astype(F32) + embed).astype(BF16)
        rounded_ref[half:, :] = (got_ref[...].astype(F32) + embed).astype(BF16)

    product = dot(rounded_ref[...], order_rows(at, pieces, weight_ref))

    @pl.when(j == 0)
    def _():
        keys_ref[...] = product.astype(BF16)

    @pl.when(j == 1)
    def _():
        values_ref[...] = (product + line(lines_ref, VALUE_BIAS)).astype(BF16)


def query_kernel(at, rounded_ref, lines_ref, *refs):
    *pieces, _, out_ref, weight_ref = refs
    weight = order_rows(at, pieces, weight_ref)
    out_ref[...] = (dot(rounded_ref[...], weight) + line(lines_ref, QUERY_BIAS)).astype(BF16)


def head_mask(head):
    return lax.broadcasted_iota(jnp.int32, (1, GROUP), 1) // HEAD_DIM == head


def attend_kernel(_, q_ref, k1_ref, v1_ref, k2_ref, v2_ref, *refs):
    out_ref, lse_ref = refs[-2:]
    keys = jnp.concatenate([k1_ref[...], k2_ref[...]], axis=0)
    values_t = jnp.concatenate([v1_ref[...], v2_ref[...]], axis=0).T
    queries = q_ref[...] * jnp.asarray(HEAD_DIM**-0.5, BF16)
    outs = []
    for head in range(GROUP_HEADS):
        masked = jnp.where(head_mask(head), queries, jnp.zeros_like(queries))
        scores = dot_back(keys, masked)
        peak = jnp.max(scores, axis=0, keepdims=True)
        exponent = jnp.exp(scores - peak)
        summed = total(exponent)
        attention = (exponent * (1.0 / summed)).astype(BF16)
        lse_ref[0, head : head + 1, :] = peak + jnp.log(summed)
        outs.append(dot(values_t[head * HEAD_DIM : (head + 1) * HEAD_DIM, :], attention))
    out_ref[...] = jnp.concatenate(outs, axis=0).astype(BF16).T


def output_kernel(at, rounded_ref, mixed_ref, mine_ref, got_ref, lines_ref, *refs):
    *pieces, weight_ref, unit_ref, scale_ref, low_ref, away_ref = refs
    product = dot(mixed_ref[...], order_rows(at, pieces, weight_ref))
    half = mine_ref.shape[0]
    for start, tokens_ref in ((0, mine_ref), (half, got_ref)):
        place = pl.ds(start, half)
        hidden = tokens_ref[...].astype(F32) + line(lines_ref, EMBED)
        unit, scale = normalise(hidden + (product[start : start + half, :] + line(lines_ref, OUTPUT_BIAS)))
        unit_ref[place, :] = unit
        scale_ref[place, :] = scale
        low_ref[place, :] = (unit * line(lines_ref, GAIN1) + line(lines_ref, SHIFT1)).astype(BF16)
    width = D // 4
    for k, left_ref in enumerate((low_ref, rounded_ref, mixed_ref)):
        for flip in (1, 0):
            column = pl.multiple_of(their(flip, at) * width, width)
            block = 2 * k + 1 - flip
            away_ref[:, block * width : (block + 1) * width] = left_ref[:, pl.ds(column, width)]


def feed_forward_kernel(
    at, low_ref, bias_ref, unit1_ref, scale1_ref, mine_ref, got_ref, lines_ref, down_ref, output_ref, *refs
):
    pieces, refs = refs[:4], refs[4:]
    active_ref, active_away_ref, final_ref, away_ref, delta_ref, up_delta_ref, down_sums_ref, up_sums_ref = refs[:8]
    input_ref, out_ref, rights_ref, mixed_ref, first_sums_ref, up_all, active_all, slope_all, sum_ref = refs[8:]
    j = pl.program_id(0)
    row = lambda i: line(lines_ref, i)
    half = mine_ref.shape[0]

    @pl.when(j < 4)
    def _():
        weight = order_rows(at, pieces, up_all.at[j])
        for start in (0, half):
            place = pl.ds(start, half)
            active, slope = gelu_and_slope(dot(low_ref[place, :], weight) + bias_ref[...])
            active_ref[place, :] = active.astype(BF16)
            slope_all[j, place, :] = slope.astype(BF16)
        active_all[j] = active_ref[...]

    for flip in (1, 0):

        @pl.when(j == their(flip, at))
        def _(flip=flip):
            width = active_ref.shape[1]
            active_away_ref[:, (1 - flip) * width : (2 - flip) * width] = active_ref[...]

    @pl.when(j == 4)
    def _():
        sum_ref[...] = dot(active_all[0], down_ref[...])

    @pl.when((j > 4) & (j < 8))
    def _():
        sum_ref[...] += dot(active_all[j - 4], down_ref[...])

    @pl.when(j == 7)
    def _():
        sums = [0.0, 0.0, 0.0]
        for start, upstream_ref, one_ref in ((0, mine_ref, final_ref), (half, got_ref, away_ref)):
            place = pl.ds(start, half)
            first_norm = unit1_ref[place, :] * row(GAIN1) + row(SHIFT1)
            unit, scale = normalise(first_norm + (sum_ref[place, :] + row(DOWN_BIAS)))
            one_ref[...] = (unit * row(GAIN2) + row(SHIFT2)).astype(BF16)
            cotangent = upstream_ref[...].astype(F32) * row(WEIGHT)
            grad = normalise_back(unit, scale, row(GAIN2), cotangent)
            delta = grad.astype(BF16)
            sum_ref[place, :] = grad
            delta_ref[place, :] = delta
            parts = (cotangent * unit, cotangent, delta.astype(F32))
            sums = [one + total(part) for one, part in zip(sums, parts)]
        for i, one in enumerate(sums):
            down_sums_ref[i : i + 1, :] = one

    @pl.when(j >= 8)
    def _():
        k = j - 8
        delta = (dot_back(delta_ref[...], down_ref[...]) * slope_all[k].astype(F32)).astype(BF16)
        up_delta_ref[...] = delta
        up_sums_ref[pl.ds(k, 1), :] = total(delta.astype(F32))
        sum_ref[...] += dot_back(delta, up_all[k])

    @pl.when(j == 11)
    def _():
        sums = [0.0, 0.0, 0.0]
        for start in (0, half):
            place = pl.ds(start, half)
            grad, unit = sum_ref[place, :], unit1_ref[place, :]
            below = normalise_back(unit, scale1_ref[place, :], row(GAIN1), grad)
            delta = below.astype(BF16)
            input_ref[place, :] = below
            out_ref[place, :] = delta
            rights_ref[place, :] = delta
            mixed_ref[place, :] = dot_back(delta, output_ref[...]).astype(BF16)
            parts = (grad * unit, grad, delta.astype(F32))
            sums = [one + total(part) for one, part in zip(sums, parts)]
        for i, one in enumerate(sums):
            first_sums_ref[i : i + 1, :] = one


def attend_back_kernel(
    _, q_ref, k1_ref, v1_ref, k2_ref, v2_ref, lse_ref, grad_ref, *refs
):
    dq_ref, rights_ref, near_ref, far_ref, p_all, ds_all = refs[-6:]
    half, tokens = k1_ref.shape[0], q_ref.shape[0]
    keys = jnp.concatenate([k1_ref[...], k2_ref[...]], axis=0)
    values = jnp.concatenate([v1_ref[...], v2_ref[...]], axis=0)
    keys_t = keys.T
    queries = q_ref[...] * jnp.asarray(HEAD_DIM**-0.5, BF16)
    grads = grad_ref[...]
    query_parts, grad_parts, dq_parts = [], [], []
    for head in range(GROUP_HEADS):
        query_one = jnp.where(head_mask(head), queries, jnp.zeros_like(queries))
        grad_one = jnp.where(head_mask(head), grads, jnp.zeros_like(grads))
        attention = jnp.exp(dot_back(keys, query_one) - lse_ref[0, head : head + 1, :])
        prob_grad = dot_back(values, grad_one)
        weighted = total(attention * prob_grad)
        score_grad = (attention * (prob_grad - weighted)).astype(BF16)
        place = slice(head * tokens, (head + 1) * tokens)
        p_all[:, place] = attention.astype(BF16)
        ds_all[:, place] = score_grad
        dq_parts.append(dot(keys_t[head * HEAD_DIM : (head + 1) * HEAD_DIM, :], score_grad))
        query_parts.append(query_one)
        grad_parts.append(grad_one)
    value_grad = dot(p_all[...], jnp.concatenate(grad_parts, axis=0))
    key_grad = dot(ds_all[...], jnp.concatenate(query_parts, axis=0))
    dq_ref[...] = (jnp.concatenate(dq_parts, axis=0) * HEAD_DIM**-0.5).astype(BF16).T
    rights_ref[...] = dq_ref[...]
    near_ref[:, :GROUP] = key_grad[:half, :]
    near_ref[:, GROUP:] = value_grad[:half, :]
    far_ref[:, :GROUP] = key_grad[half:, :].astype(BF16)
    far_ref[:, GROUP:] = value_grad[half:, :].astype(BF16)


def delta_kernel(_, *refs):
    groups = D // GROUP
    nears, fars = refs[:groups], refs[groups : 2 * groups]
    queries_ref, __, keys_ref, values_ref, rights_ref, sums_ref = refs[2 * groups :]
    i = pl.program_id(0)
    for g in range(groups):
        place = slice(g * GROUP, (g + 1) * GROUP)
        rights_ref[:, place] = (nears[g][...] + fars[g][...].astype(F32)).astype(BF16)
    sums_ref[pl.ds(1 + i, 1), :] = total(rights_ref[...].astype(F32))

    @pl.when(i == 0)
    def _():
        sums_ref[0:1, :] = total(queries_ref[...].astype(F32))
        keys_ref[...] = rights_ref[...]

    @pl.when(i == 1)
    def _():
        values_ref[...] = rights_ref[...]


def input_query_kernel(_, delta_ref, weight_ref, grad_ref, out_ref):
    out_ref[...] = grad_ref[...] + dot_back(delta_ref[...], weight_ref[...])


def input_kernel(_, delta_ref, weight_ref, grad_ref, mine_ref, away_ref, time_ref, sum_ref):
    j = pl.program_id(0)
    part = dot_back(delta_ref[...], weight_ref[...])

    @pl.when(j == 0)
    def _():
        sum_ref[...] = grad_ref[...] + part

    @pl.when(j > 0)
    def _():
        sum_ref[...] += part

    @pl.when(j == pl.num_programs(0) - 1)
    def _():
        half = mine_ref.shape[0]
        mine_ref[...] = sum_ref[:half, :]
        away_ref[...] = sum_ref[half:, :].astype(BF16)
        time_ref[...] = total(sum_ref[...])


def grad_block(which, left_ref, right_ref, far_left_ref, fars, sum_ref, *more):
    for k, far_ref in enumerate(fars):

        @pl.when((which == k) if len(fars) > 1 else (which >= 0))
        def _(far_ref=far_ref):
            sum_ref[...] = outer(far_left_ref[...], far_ref[...])

    block = outer(left_ref[...], right_ref[...]) + sum_ref[...]
    for one_ref in more:
        block = block + one_ref[...].astype(F32)
    return block.astype(BF16)


def grad_x_kernel(_, left_ref, right_ref, far_left_ref, *refs):
    *fars, out_ref, sum_ref = refs
    out_ref[...] = grad_block(pl.program_id(0), left_ref, right_ref, far_left_ref, fars, sum_ref)


def grad_y_kernel(at_ref, left_ref, right_ref, far_left_ref, other_ref, *refs):
    *fars, away_ref, keep_ref, sum_ref = refs
    i, half = pl.program_id(0), pl.num_programs(0) // 2
    which = jnp.where(i < half, 1 - at_ref[SIDE_Y], at_ref[SIDE_Y])
    block = grad_block(which, left_ref, right_ref, far_left_ref, fars, sum_ref, other_ref)

    @pl.when(i < half)
    def _():
        away_ref[...] = block

    @pl.when(i >= half)
    def _():
        keep_ref[...] = block


def fold_kernel(_, keep1_ref, keep2_ref, away1_ref, away2_ref, keep_ref, away_ref):
    keep_ref[...] = (keep1_ref[...].astype(F32) + keep2_ref[...].astype(F32)).astype(BF16)
    away_ref[...] = (away1_ref[...].astype(F32) + away2_ref[...].astype(F32)).astype(BF16)


def add_kernel(_, one_ref, two_ref, out_ref):
    out_ref[...] = (one_ref[...].astype(F32) + two_ref[...].astype(F32)).astype(out_ref.dtype)


def join_kernel(at_ref, mine_ref, other_ref, out_ref):
    rows = mine_ref.shape[0]
    out_ref[pl.ds(pl.multiple_of(at_ref[SIDE_Z] * rows, 16), rows), :] = mine_ref[...]
    out_ref[pl.ds(pl.multiple_of((1 - at_ref[SIDE_Z]) * rows, 16), rows), :] = other_ref[...]


def finish_kernel(_, mine_ref, other_ref, *refs):
    out_ref = refs[-1]
    i, half = pl.program_id(0), pl.num_programs(0) // 2

    @pl.when(i < half)
    def _():
        out_ref[...] = mine_ref[...].astype(F32)

    @pl.when(i >= half)
    def _():
        out_ref[...] = other_ref[...].astype(F32)


def copy_kernel(_, in_ref, out_ref):
    out_ref[...] = in_ref[...]


def two_kernel(at, mine_ref, other_ref, first_ref, second_ref):
    first = at[SIDE_Y] == 0
    mine, other = mine_ref[...].astype(F32), other_ref[...].astype(F32)
    first_ref[...] = jnp.where(first, mine, other)
    second_ref[...] = jnp.where(first, other, mine)


def pair_kernel(_, mine_ref, received_ref, out_ref):
    @pl.when(pl.program_id(0) == 0)
    def _():
        out_ref[...] = mine_ref[...]

    @pl.when(pl.program_id(0) == 1)
    def _():
        out_ref[...] = received_ref[...].astype(out_ref.dtype)


def append_kernel(_, first_ref, *refs):
    *vectors, out_ref, small_ref = refs
    rows = first_ref.shape[0]
    out_ref[:rows, :] = first_ref[...]
    flat = jnp.concatenate([vector[...].astype(F32).reshape(1, -1) for vector in vectors], axis=1)
    lines = [flat[:, start : start + D] for start in range(0, flat.shape[1], D)]
    small = jnp.concatenate(lines + [jnp.zeros((16 - len(lines), D), F32)], axis=0).astype(BF16)
    small_ref[...] = small
    out_ref[rows:, :] = small


def side_by_side_kernel(_, *refs):
    out_ref, at = refs[-1], 0
    for piece in refs[:-1]:
        out_ref[:, at : at + piece.shape[1]] = piece[...]
        at += piece.shape[1]


def split_kernel(_, in_ref, first_ref, second_ref):
    rows = first_ref.shape[0]
    first_ref[...] = in_ref[:rows, :]
    second_ref[...] = in_ref[rows:, :]


def parity(at):
    return (at[SIDE_Y] + at[SIDE_Z]) % 2


def remote_kernel(at, half_ref, third_ref, fourth_ref, *outs):
    columns = 0
    for out_ref in outs:
        width = out_ref.shape[1]
        place = slice(columns, columns + width)
        columns += width
        remote_rows(at, half_ref.at[:, place], third_ref.at[:, place], fourth_ref.at[:, place], out_ref)


def remote_rows(at, half_ref, third_ref, fourth_ref, out_ref):
    half, quarter = half_ref.shape[0], third_ref.shape[0]
    missing = (1 - parity(at)) * half
    out_ref[pl.ds(pl.multiple_of(parity(at) * half, 16), half), :] = half_ref[...]
    out_ref[pl.ds(pl.multiple_of(missing, 16), quarter), :] = third_ref[...]
    out_ref[pl.ds(pl.multiple_of(missing + quarter, 16), quarter), :] = fourth_ref[...]


def lines_kernel(at, down_ref, first_ref, delta_ref, up_ref, time_ref, out_ref):
    out_ref[0:8, :] = down_ref[...]
    out_ref[8:16, :] = first_ref[...]
    out_ref[16:24, :] = delta_ref[...]
    out_ref[24:28, :] = up_ref[0:4, :]
    row = lax.broadcasted_iota(jnp.int32, (4, D), 0)
    out_ref[28:32, :] = jnp.where(row == at[CHIP], time_ref[...], 0.0)


def per_device(n_dp, inputs, timestep, bucket_count, upstream, *params):
    query_weight, key_weight, value_weight, output_weight, up_weight, down_weight = params[:6]
    vectors = params[6:]
    device = lax.axis_index("fsdp")
    chip, core = device // 2, device % 2
    bucket = lax.axis_index("dp")
    half = inputs.shape[1]
    tokens = 2 * half
    hidden_width = up_weight.shape[1]
    side_y, side_z = bucket % 2, (bucket // 2) % 2
    place = jnp.stack([chip, core, side_y, side_z]).astype(jnp.int32)
    run = functools.partial(run_kernel, place)

    def swap(value, axis, bit):
        size = 4 if axis == "fsdp" else n_dp
        return lax.ppermute(value, axis, [(i, i ^ bit) for i in range(size)])

    swap_core = lambda value: swap(value, "fsdp", 1)
    swap_chip = lambda value: swap(value, "fsdp", 2)
    swap_y = lambda value: swap(value, "dp", 1)
    swap_z = lambda value: swap(value, "dp", 2)

    def pick(array, flip, *later_than):
        _, rows, columns = array.shape
        ins = [(array, (None, rows, columns), lambda _, at: (at[CHIP] ^ flip, 0, 0))]
        return run("pick", copy_kernel, (1,), ins, [whole_out((rows, columns), array.dtype)], later_than)

    def pack(arrays, *later_than):
        shape = (arrays[0].shape[0], sum(array.shape[1] for array in arrays))
        return run("pack", side_by_side_kernel, (1,), [whole(a) for a in arrays], [whole_out(shape, BF16)], later_than)

    def cut(shards, *later_than):
        rows = shards[0].shape[0]
        columns = sum(shard.shape[1] for shard in shards)
        ins = [(shard, (rows // 2, shard.shape[1]), lambda _, at: (parity(at), 0)) for shard in shards]
        outs = [whole_out((rows // 2, columns), BF16)]
        return run("cut", side_by_side_kernel, (1,), ins, outs, later_than)

    def split(first, *later_than):
        rows, columns = first.shape
        outs = [whole_out((rows // 2, columns), BF16)] * 2
        to_y, to_z = run("split", split_kernel, (1,), [whole(first)], outs, later_than)
        return (first, swap_y(to_y), swap_z(to_z)), to_y

    def remote(parts, widths, *later_than):
        outs = [whole_out((2 * parts[0].shape[0], width), BF16) for width in widths]
        return run("remote", remote_kernel, (1,), [whole(part) for part in parts], outs, later_than)

    tokens_away, small = run(
        "pick", append_kernel, (1,),
        [(inputs, (None, half, D), lambda _, at: (at[CHIP] ^ 1, 0, 0))] + [whole(vector) for vector in vectors],
        [whole_out((half + 16, D), BF16), whole_out((16, D), BF16)],
    )
    tokens_got = swap_chip(tokens_away)
    got_half = (tokens_got, (half, D), lambda *_: (0, 0))
    three = (query_weight, key_weight, value_weight)
    two_weights = (output_weight, up_weight)
    three_cut = cut(three, tokens_away)
    three_first = swap_chip(three_cut)
    three_own = pack(three, three_cut)
    three_sibling = swap_core(three_own)
    two_own = pack(two_weights, three_own)
    two_sibling = swap_core(two_own)
    two_cut = cut(two_weights, tokens_got, two_own)
    two_first = swap_chip(two_cut)
    down_copy = run("copy", copy_kernel, (1,), [whole(down_weight)], [whole_out(down_weight.shape, BF16)], (two_cut,))
    live = chip < bucket_count[bucket]
    seq_weight = live.astype(F32) * (2 * n_dp / jnp.sum(bucket_count).astype(F32))
    small_two = jnp.concatenate([small, tokens_got[half:]], axis=0)
    small_far = swap_core(small_two)
    three_parts, split_done = split(three_first, three_sibling, two_sibling, down_copy, small_far)
    down_matrix = lax.all_gather(down_copy, "fsdp", axis=0, tiled=True)
    tokens_mine = pick(inputs, 0, split_done)
    query_remote, kv_remote = remote(three_parts, (D, 2 * D), tokens_mine)
    lines, up_bias = run(
        "lines_in", lines_in_kernel, (1,),
        [whole(a) for a in (small_two, small_far, sinusoid(timestep), seq_weight.reshape(1, 1))],
        [whole_out((LINES, D), F32), whole_out((1, hidden_width), F32)], (kv_remote,),
    )
    kv_pieces = [three_own, kv_remote, three_sibling, swap_core(kv_remote)]
    query_pieces = [three_own, query_remote, three_sibling, swap_core(query_remote)]
    keys, values, qkv_matrix, lefts = run(
        "key_value", key_value_kernel, (2,),
        [whole(tokens_mine), got_half, whole(lines)] + pieces_in(kv_pieces, D, (1, 0, 1, 0)),
        [
            whole_out((tokens, D), BF16),
            whole_out((tokens, D), BF16),
            ((D, 3 * D), BF16, (D, D), lambda j, *_: (0, 1 + j)),
            ((tokens, 2 * D), BF16, (tokens, D), lambda j, *_: (0, 0)),
        ],
    )
    far_keys, far_values = swap_core(keys), swap_core(values)
    queries, qkv_matrix = run(
        "query", query_kernel, (1,),
        [(lefts, (tokens, D), lambda j, *_: (0, 0)), whole(lines)] + pieces_in(query_pieces, D, (0, 0, 0, 0))
        + [(qkv_matrix, None, None)],
        [((tokens, D), BF16, (tokens, D), lambda j, *_: (0, 0)), ((D, 3 * D), BF16, (D, D), lambda j, *_: (0, 0))],
        aliases={2 + len(query_pieces): 1},
    )
    groups = D // GROUP
    group_of = lambda array, first: (array, (array.shape[0], GROUP), lambda g, *_: (0, first + g))

    def attend(first, count, lefts, lse, *later_than):
        return run(
            "attend", attend_kernel, (count,),
            [group_of(a, first) for a in (queries, keys, values, far_keys, far_values)] + [(lefts, None, None)]
            + ([] if lse is None else [(lse, None, None)]),
            [
                ((tokens, 2 * D), BF16, (tokens, GROUP), lambda g, *_: (0, groups + first + g)),
                ((groups, GROUP_HEADS, tokens), F32, (1, GROUP_HEADS, tokens), lambda g, *_: (first + g, 0, 0)),
            ],
            later_than, aliases={5: 0} if lse is None else {5: 0, 6: 1}, vmem=32,
        )

    lefts, lse = attend(0, groups // 2, lefts, None)
    two_parts, split_done = split(two_first, lse)
    upstream_away = pick(upstream, 1, split_done)
    upstream_got = swap_chip(upstream_away)
    lefts, lse = attend(groups // 2, groups // 2, lefts, lse, upstream_away)
    two_remote = remote(two_parts, (two_own.shape[1],), lse)
    upstream_mine = pick(upstream, 0, two_remote)
    two_pieces = [two_own, two_remote, two_sibling, swap_core(two_remote)]
    output_matrix, unit1, scale1, first_low, lefts_away = run(
        "output", output_kernel, (1,),
        [(lefts, (tokens, D), lambda j, *_: (0, 0)), (lefts, (tokens, D), lambda j, *_: (0, 1))]
        + [whole(tokens_mine), got_half, whole(lines)]
        + pieces_in(two_pieces, D, (0, 0, 0, 0)),
        [
            whole_out((D, D), BF16),
            whole_out((tokens, D), F32),
            whole_out((tokens, 1), F32),
            whole_out((tokens, D), BF16),
            whole_out((tokens, 6 * D // 4), BF16),
        ],
        (upstream_mine,),
    )
    lefts_away = swap_core(lefts_away)
    width = hidden_width // 4
    hidden_block = lambda j: jnp.minimum(j, 3)
    results = run(
        "feed_forward", feed_forward_kernel, (12,),
        [held(first_low), (up_bias, (1, width), lambda j, *_: (0, hidden_block(j))), held(unit1), held(scale1)]
        + [held(upstream_mine), held(upstream_got), held(lines)]
        + [(down_matrix, (width, D), lambda j, *_: (jnp.where(j < 4, 0, j % 4), 0)), held(output_matrix)]
        + [(piece, (piece.shape[0], width), lambda j, *_: (0, D // width + hidden_block(j))) for piece in two_pieces],
        [
            ((tokens, hidden_width), BF16, (tokens, width), lambda j, *_: (0, hidden_block(j))),
            whole_out((tokens, 2 * width), BF16),
            whole_out((half, D), BF16),
            whole_out((half, D), BF16),
            whole_out((tokens, D), BF16),
            ((tokens, hidden_width), BF16, (tokens, width), lambda j, *_: (0, jnp.maximum(j - 8, 0))),
            whole_out((8, D), F32),
            whole_out((8, D), F32),
            whole_out((tokens, D), F32),
            whole_out((tokens, D), BF16),
            ((tokens, 4 * D), BF16, (tokens, D), lambda j, *_: (0, 3)),
            whole_out((tokens, D), BF16),
            whole_out((8, D), F32),
        ],
        (),
        [
            pltpu.VMEM((4, D, width), BF16),
            pltpu.VMEM((4, tokens, width), BF16),
            pltpu.VMEM((4, tokens, width), BF16),
            pltpu.VMEM((tokens, D), F32),
        ],
    )
    activated, active_away, final_mine, final_away, down_delta, up_delta, down_sums, up_sums = results[:8]
    input_part, out_delta, rights, mixed_grad, first_sums = results[8:]
    active_away, down_far = swap_core(active_away), swap_core(down_delta)
    up_far, out_far = swap_core(up_delta), swap_core(out_delta)

    block_rows = D // 4

    class Grads:
        def __init__(self, left, right, send, keep, fars, near, right_column):
            self.left, self.right, self.send_far, self.keep_far = left, right, send, keep
            self.fars, self.near, self.right_column = fars, near, right_column

        def ins(self, flip, far, block):
            far_left, far_column = far
            shard = lambda at: 2 * (at[CHIP] ^ flip) + at[CORE]
            return [
                (self.left, (tokens, block_rows), lambda i, at: (0, self.near(shard(at), block(i, at)))),
                (self.right, (tokens, D), lambda i, at: (0, self.right_column(block(i, at)))),
                (far_left, (tokens, block_rows), lambda i, at: (0, far_column(block(i, at)))),
            ]

        def far_ins(self, block, first, count):
            if len(self.fars) > 1:
                return [whole(a) for a in self.fars[first : first + count]]
            return [(self.fars[0], (tokens, D), lambda i, at: (0, self.right_column(block(i, at))))]

        def four(self, name, body, flip, far, more, *later_than):
            out = ((4 * block_rows, D), BF16, (block_rows, D), lambda i, at: (i, 0))
            block = lambda i, at: i
            ins = self.ins(flip, far, block) + more + self.far_ins(block, 0, 4)
            return run(name, body, (4,), ins, [out], later_than, [pltpu.VMEM((block_rows, D), F32)])

        def start(self, *later_than):
            sent = self.four("grad_x", grad_x_kernel, 1, self.send_far, [], *later_than)
            self.got = swap_chip(sent)
            return sent

    class Chunk:
        def __init__(self, grads, first, count):
            self.grads, self.first, self.half = grads, first, count // 2

        def over_y(self, last):
            grads, first, half = self.grads, self.first, self.half
            block = lambda i, at: first + jnp.where(
                i < half, (1 - at[SIDE_Y]) * half + i, at[SIDE_Y] * half + i - half
            )
            other = (grads.got, (block_rows, D), lambda i, at: (block(i, at), 0))
            shape = (half * block_rows, D)
            away, self.keep = run(
                "grad_y", grad_y_kernel, (2 * half,),
                grads.ins(0, grads.keep_far, block) + [other] + grads.far_ins(block, first, 2),
                [
                    (shape, BF16, (block_rows, D), lambda i, at: (jnp.minimum(i, half - 1), 0)),
                    (shape, BF16, (block_rows, D), lambda i, at: (jnp.maximum(i - half, 0), 0)),
                ],
                (last,), [pltpu.VMEM((block_rows, D), F32)],
            )
            self.got = swap_y(away)
            return self.keep

        def over_z(self, last):
            block = (self.keep.shape[0] // 2, D)
            kept = [(a, block, lambda _, at: (at[SIDE_Z], 0)) for a in (self.keep, self.got)]
            given = [(a, block, lambda _, at: (1 - at[SIDE_Z], 0)) for a in (self.keep, self.got)]
            self.keep, away = run("grad_z", fold_kernel, (1,), kept + given, [whole_out(block, BF16)] * 2, (last,))
            self.got = swap_z(away)
            return self.keep

        def add(self, bit, last):
            ins = [whole(self.keep), whole(self.got)]
            self.keep = run("grad_add", add_kernel, (1,), ins, [whole_out(self.keep.shape, BF16)], (last,))
            self.got = swap(self.keep, "dp", bit)
            return self.keep

        def add_high(self, last):
            for bit in high_bits:
                last = self.add(bit, last)
            return last

        def add_low(self, last):
            return self.add(2, last)

        def back(self, last):
            ins = [whole(self.keep), whole(self.got)]
            shape = (2 * self.keep.shape[0], D)
            self.keep = run("grad_join", join_kernel, (1,), ins, [whole_out(shape, BF16)], (last,))
            self.got = swap_y(self.keep)
            return self.keep

        def finish(self, last, shape, index):
            half = self.half
            ins = [
                (self.keep, (block_rows, D), lambda i, at: (jnp.minimum(i, half - 1), 0)),
                (self.got, (block_rows, D), lambda i, at: (jnp.maximum(i - half, 0), 0)),
            ]
            place = lambda i, at: jnp.where(i < half, at[SIDE_Y] * half + i, (1 - at[SIDE_Y]) * half + i - half)
            out = (shape, F32, (block_rows, D), lambda i, at: index(place(i, at)))
            return run("grad_out", finish_kernel, (2 * half,), ins, [out], (last,))

    def pair_of(mine, received, dtype, last):
        out = ((2, half, D), dtype, (None, half, D), lambda i, at: (at[CHIP] ^ i, 0, 0))
        return run("pair", pair_kernel, (2,), [whole(mine), whole(received)], [out], (last,))

    high_bits = [1 << i for i in range(2, n_dp.bit_length()) if 1 << i < n_dp]
    relay = lambda array, last: run("relay", copy_kernel, (1,), [whole(array)], [whole_out(array.shape, array.dtype)], (last,))

    grads_down = Grads(
        activated, down_delta, (active_away, lambda b: b), (active_away, lambda b: 4 + b), [down_far],
        lambda shard, b: shard * (hidden_width // D) + b, lambda b: 0,
    )
    grads_up = Grads(
        first_low, up_delta, (lefts_away, lambda b: 0), (lefts_away, lambda b: 1), [up_far],
        lambda shard, b: shard, lambda b: b,
    )

    def attend_back(first, count, later_than, rights, query_delta):
        return run(
            "attend_back", attend_back_kernel, (count,),
            [group_of(a, first) for a in (queries, keys, values, far_keys, far_values)]
            + [(lse, (1, GROUP_HEADS, tokens), lambda g, *_: (first + g, 0, 0)), group_of(mixed_grad, first)]
            + [(rights, None, None)] + ([] if query_delta is None else [(query_delta, None, None)]),
            [
                ((tokens, D), BF16, (tokens, GROUP), lambda g, *_: (0, first + g)),
                ((tokens, 4 * D), BF16, (tokens, GROUP), lambda g, *_: (0, first + g)),
                ((tokens, 2 * count * GROUP), F32, (tokens, 2 * GROUP), lambda g, *_: (0, g)),
                ((tokens, 2 * count * GROUP), BF16, (tokens, 2 * GROUP), lambda g, *_: (0, g)),
            ],
            later_than, [pltpu.VMEM((2 * tokens, GROUP_HEADS * tokens), BF16)] * 2, aliases={7: 1} if query_delta is None else {7: 1, 8: 0},
        )

    first_call = 1
    query_delta, rights, near1, far1 = attend_back(0, first_call, (mixed_grad,), rights, None)
    far1 = swap_core(far1)
    last = grads_down.start(near1)
    last = grads_up.start(last, out_far)
    query_delta, rights, near2, far2 = attend_back(first_call, groups - first_call, (last, far1), rights, query_delta)
    far2, query_far = swap_core(far2), swap_core(query_delta)
    last = input_part = run(
        "input_query", input_query_kernel, (2,),
        [
            (query_delta, (half, D), lambda i, *_: (i, 0)),
            (qkv_matrix, (D, D), lambda i, *_: (0, 0)),
            (input_part, (half, D), lambda i, *_: (i, 0)),
        ],
        [((tokens, D), F32, (half, D), lambda i, *_: (i, 0))], (near2,),
    )
    key_delta, value_delta, rights, delta_sums = run(
        "delta", delta_kernel, (2,),
        [
            (a, (tokens, GROUP), lambda i, *_, g=g: (0, 2 * g + i))
            for one, two in ((near1, near2), (far1, far2))
            for a, count in ((one, first_call), (two, groups - first_call))
            for g in range(count)
        ]
        + [whole(query_delta), (rights, None, None)],
        [
            whole_out((tokens, D), BF16),
            whole_out((tokens, D), BF16),
            ((tokens, 4 * D), BF16, (tokens, D), lambda i, *_: (0, 1 + i)),
            whole_out((8, D), F32),
        ],
        (last,), aliases={2 * groups + 1: 2},
    )
    key_far, value_far = swap_core(key_delta), swap_core(value_delta)
    step = D
    input_mine, input_away, time_sum = run(
        "input", input_kernel, (2,),
        [(rights, (tokens, D), lambda j, *_: (0, 1 + j)), (qkv_matrix, (D, D), lambda j, *_: (0, 1 + j)), whole(input_part)],
        [whole_out((half, D), F32), whole_out((half, D), BF16), whole_out((1, D), F32)],
        (delta_sums,), [pltpu.VMEM((tokens, D), F32)],
    )
    last_one = lambda b: jnp.where(b == 3, 1, 0)
    grads_four = Grads(
        lefts, rights, (lefts_away, lambda b: 2 + 2 * last_one(b)), (lefts_away, lambda b: 3 + 2 * last_one(b)),
        [query_far, key_far, value_far, out_far], lambda shard, b: shard + 4 * last_one(b), lambda b: b,
    )
    down, up = Chunk(grads_down, 0, 4), Chunk(grads_up, 0, 4)
    last = down.over_y(time_sum)
    last = grads_four.start(last)

    packed = run(
        "lines", lines_kernel, (1,), [whole(a) for a in (down_sums, first_sums, delta_sums, up_sums, time_sum)],
        [whole_out((32, D), F32)], (last,),
    )
    hops = [("fsdp", 1), ("fsdp", 2)] + [("dp", 1 << i) for i in range(n_dp.bit_length() - 1)]
    line_parts, line_got = [packed], [swap(packed, *hops[0])]

    def add_lines(last):
        ins = [whole(line_parts[-1]), whole(line_got[-1])]
        line_parts.append(run("lines_add", add_kernel, (1,), ins, [whole_out((32, D), F32)], (last,)))
        if len(line_parts) <= len(hops) - 0 and len(line_got) < len(hops):
            line_got.append(swap(line_parts[-1], *hops[len(line_got)]))
        return line_parts[-1]

    qk, vo = Chunk(grads_four, 0, 2), Chunk(grads_four, 2, 2)
    last = down.over_z(packed)
    last = add_lines(last)
    last = up.over_y(last)
    last = down.add_high(last)
    last = up.over_z(last)
    last = down.add_low(last)
    last = qk.over_y(last)
    last = vo.over_y(last)
    last = up.add_high(last)
    last = down.back(last)
    last = add_lines(last)
    last = qk.over_z(last)
    last = vo.over_z(last)
    last = final_away = relay(final_away, last)
    final_got = swap_chip(final_away)
    last = up.add_low(last)
    last = qk.add_high(last)
    last = vo.add_high(last)
    last = add_lines(last)
    last = down_grad = down.finish(last, down_weight.shape, lambda s: (s, 0))
    last = up.back(last)
    last = qk.add_low(last)
    last = vo.add_low(last)
    last = input_away = relay(input_away, last)
    input_got = swap_chip(input_away)
    last = final = pair_of(final_mine, final_got, BF16, last)
    last = qk.back(last)
    last = vo.back(last)
    while len(line_parts) < len(hops):
        last = add_lines(last)
    last = up_grad = up.finish(last, up_weight.shape, lambda s: (0, s))
    last = input_gradient = pair_of(input_mine, input_got, F32, last)
    last = add_lines(last)

    def two(chunk, last):
        outs = [whole_out((block_rows, D), F32)] * 2
        return run("two", two_kernel, (1,), [whole(chunk.keep), whole(chunk.got)], outs, (last,))

    query_grad, key_grad = two(qk, last)
    value_grad, output_grad = two(vo, query_grad)
    times = lax.dynamic_slice_in_dim(line_parts[2], device * (D // 4), D // 4, axis=1)
    time_gradient = times[28:30]
    packed = line_parts[-1]
    mine = lax.dynamic_slice_in_dim(packed, device * (D // 4), D // 4, axis=1)
    up_bias_grad = lax.dynamic_slice_in_dim(packed[24:28], device, 1, axis=0).reshape(-1)
    vector_grads = (mine[16], mine[18], mine[10], up_bias_grad, mine[2], mine[8], mine[9], mine[0], mine[1])

    return (
        final,
        input_gradient,
        time_gradient,
        query_grad,
        key_grad,
        value_grad,
        output_grad,
        up_grad,
        down_grad,
        *vector_grads,
    )


def solution(mesh):
    rows, wide, flat = P("dp", "fsdp", None), P("fsdp", None), P("fsdp")
    return jax.shard_map(
        functools.partial(per_device, mesh.shape["dp"]),
        mesh=mesh,
        in_specs=(rows, P("dp"), P(), rows) + (wide,) * 6 + (flat,) * 9,
        out_specs=(rows, rows, P("dp", "fsdp")) + (wide,) * 6 + (flat,) * 9,
        check_vma=False,
    )
```

```python
import functools
import math

import jax
import jax.numpy as jnp
from jax import lax
from jax.experimental import pallas as pl
from jax.experimental.pallas import tpu as pltpu
from jax.sharding import PartitionSpec as P

D = 1024
HEAD_DIM = 64
GROUP = 256
GROUP_HEADS = GROUP // HEAD_DIM
F32 = jnp.float32
BF16 = jnp.bfloat16
ROWS_ROWS = (((0,), (0,)), ((), ()))
COLS_COLS = (((1,), (1,)), ((), ()))
ANY = pl.BlockSpec(memory_space=pl.ANY)
VMEM_MB = dict(grad_z=16,grad_add=16,grad_join=16,lines_add=16,lines=16,relay=16,grad_y=24)
COST = 10**11
MICROSECONDS = dict(
    pick=2, cut=2, pack=3, split=2, copy=2, relay=2, columns=2, remote=3, key_value=7, query=4, attend=9, output=6,
    feed_forward=40, two=2, grad_x=8, grad_y=5, grad_z=3, grad_add=2, grad_join=3,
    grad_out=3, attend_back=15, delta=5, input=8, input_query=5, lines_in=2, lines=2, lines_add=1, pair=3,
)


def run_kernel(place, name, body, grid, ins, outs, later_than=(), scratch=(), aliases=None, vmem=16):
    count, waits = len(ins), len(later_than)

    def kernel(*refs):
        body(*refs[: 1 + count], *refs[1 + count + waits :])

    def spec(block, index, *buffers):
        if block is None:
            return ANY
        modes = dict(pipeline_mode=pl.Buffered(buffers[0])) if buffers else {}
        return pl.BlockSpec(block, index, **modes)

    shapes = [jax.ShapeDtypeStruct(shape, dtype) for shape, dtype, _, _ in outs]
    out_specs = [spec(block, index) for _, _, block, index in outs]
    single = len(outs) == 1
    return pl.pallas_call(
        kernel,
        grid_spec=pltpu.PrefetchScalarGridSpec(
            num_scalar_prefetch=1,
            grid=grid,
            in_specs=[spec(*one[1:]) for one in ins] + [ANY] * waits,
            out_specs=out_specs[0] if single else out_specs,
            scratch_shapes=list(scratch),
        ),
        out_shape=shapes[0] if single else shapes,
        input_output_aliases={1 + i: o for i, o in (aliases or {}).items()},
        compiler_params=pltpu.CompilerParams(vmem_limit_bytes=VMEM_MB.get(name, 60) * 2**20),
        cost_estimate=pl.CostEstimate(flops=int(MICROSECONDS[name] * COST), bytes_accessed=0, transcendentals=0),
        name=name,
    )(place, *[one[0] for one in ins], *later_than)


CHIP, CORE, SIDE_Y, SIDE_Z = range(4)
LINES = 16
QUERY_BIAS, VALUE_BIAS, OUTPUT_BIAS, DOWN_BIAS, GAIN1, SHIFT1, GAIN2, SHIFT2, EMBED, WEIGHT = range(10)


def device_of(at):
    return 2 * at[CHIP] + at[CORE]


def their(flip, at):
    return 2 * (at[CHIP] ^ flip) + (at[CORE] ^ 1)


def line(lines_ref, i):
    return lines_ref[i : i + 1, :]


def whole(array):
    return (array, array.shape, lambda *_: (0,) * array.ndim)


def held(array):
    return (*whole(array), 1)


def whole_out(shape, dtype):
    return (shape, dtype, shape, lambda *_: (0,) * len(shape))


def sinusoid(timestep):
    halves = D // 2
    frequency = jnp.exp(jnp.arange(halves, dtype=F32) * (-math.log(10000.0) / halves))
    angles = timestep.astype(F32)[:, None] * frequency[None, :]
    return jnp.concatenate([jnp.sin(angles), jnp.cos(angles)], axis=1)


def dot(left, right):
    return jnp.dot(left, right, preferred_element_type=F32)


def dot_back(left, right):
    return lax.dot_general(left, right, COLS_COLS, preferred_element_type=F32)


def outer(left, right):
    return lax.dot_general(left, right, ROWS_ROWS, preferred_element_type=F32)


def total(rows):
    return jnp.sum(rows, axis=0, keepdims=True)


def mean(rows):
    return jnp.mean(rows, axis=-1, keepdims=True)


def normalise(residual):
    centered = residual - mean(residual)
    scale = lax.rsqrt(mean(centered * centered) + 1e-05)
    return centered * scale, scale


def normalise_back(unit, scale, gain, grad):
    scaled = grad * gain
    return scale * (scaled - mean(scaled) - unit * mean(scaled * unit))


def gelu_and_slope(upward):
    size = jnp.abs(upward) * (2.0**-0.5)
    bell = jnp.exp(-0.5 * (upward * upward))
    t = 1.0 / (1.0 + 0.3275911 * size)
    series = t * (
        0.254829592
        + t * (-0.284496736 + t * (1.421413741 + t * (-1.453152027 + t * 1.061405429)))
    )
    tail = 0.5 * series * bell
    cdf = jnp.where(upward >= 0, 1.0 - tail, tail)
    return upward * cdf, cdf + upward * (bell * (2 * math.pi) ** -0.5)


def order_rows(at, pieces, weight_ref):
    for flip, piece in zip((0, 2, 1, 3), pieces):
        rows = piece.shape[0]
        start = pl.multiple_of((device_of(at) ^ flip) * rows, 16)
        weight_ref[pl.ds(start, rows), :] = piece[...]
    return weight_ref[...]


def pieces_in(pieces, step, firsts):
    return [(piece, (piece.shape[0], step), lambda j, *_, k=k: (0, k + j)) for piece, k in zip(pieces, firsts)]


def lines_in_kernel(at, own_ref, far_ref, embeds_ref, weight_ref, lines_ref, up_ref):
    share = D // 4
    extra = up_ref.shape[1] // D
    for flip, shares_ref, first in ((0, own_ref, 0), (2, own_ref, 16), (1, far_ref, 0), (3, far_ref, 16)):
        device = device_of(at) ^ flip
        rows = shares_ref[first : first + 16, :].astype(F32)
        piece = lambda i, rows=rows: rows[i // 4 : i // 4 + 1, i % 4 * share : (i % 4 + 1) * share]
        place = pl.ds(pl.multiple_of(device * share, share), share)
        for i in range(8):
            lines_ref[i : i + 1, place] = piece(i if i < 3 else i + extra)
        for e in range(extra):
            start = pl.multiple_of((device * extra + e) * share, share)
            up_ref[:, pl.ds(start, share)] = piece(3 + e)
    lines_ref[EMBED : EMBED + 1, :] = embeds_ref[pl.ds(at[CHIP], 1), :]
    lines_ref[WEIGHT:LINES, :] = jnp.broadcast_to(weight_ref[...], (LINES - WEIGHT, D))


def key_value_kernel(at, mine_ref, got_ref, lines_ref, *refs):
    *pieces, keys_ref, values_ref, weight_ref, rounded_ref = refs
    j = pl.program_id(0)

    @pl.when(j == 0)
    def _():
        half = mine_ref.shape[0]
        embed = line(lines_ref, EMBED)
        rounded_ref[:half, :] = (mine_ref[...].astype(F32) + embed).astype(BF16)
        rounded_ref[half:, :] = (got_ref[...].astype(F32) + embed).astype(BF16)

    product = dot(rounded_ref[...], order_rows(at, pieces, weight_ref))

    @pl.when(j == 0)
    def _():
        keys_ref[...] = product.astype(BF16)

    @pl.when(j == 1)
    def _():
        values_ref[...] = (product + line(lines_ref, VALUE_BIAS)).astype(BF16)


def query_kernel(at, rounded_ref, lines_ref, *refs):
    *pieces, _, out_ref, weight_ref = refs
    weight = order_rows(at, pieces, weight_ref)
    out_ref[...] = (dot(rounded_ref[...], weight) + line(lines_ref, QUERY_BIAS)).astype(BF16)


def head_mask(head):
    return lax.broadcasted_iota(jnp.int32, (1, GROUP), 1) // HEAD_DIM == head


def attend_kernel(_, q_ref, k1_ref, v1_ref, k2_ref, v2_ref, *refs):
    out_ref, lse_ref = refs[-2:]
    keys = jnp.concatenate([k1_ref[...], k2_ref[...]], axis=0)
    values_t = jnp.concatenate([v1_ref[...], v2_ref[...]], axis=0).T
    queries = q_ref[...] * jnp.asarray(HEAD_DIM**-0.5, BF16)
    outs = []
    for head in range(GROUP_HEADS):
        masked = jnp.where(head_mask(head), queries, jnp.zeros_like(queries))
        scores = dot_back(keys, masked)
        peak = jnp.max(scores, axis=0, keepdims=True)
        exponent = jnp.exp(scores - peak)
        summed = total(exponent)
        attention = (exponent * (1.0 / summed)).astype(BF16)
        lse_ref[0, head : head + 1, :] = peak + jnp.log(summed)
        outs.append(dot(values_t[head * HEAD_DIM : (head + 1) * HEAD_DIM, :], attention))
    out_ref[...] = jnp.concatenate(outs, axis=0).astype(BF16).T


def output_kernel(at, rounded_ref, mixed_ref, mine_ref, got_ref, lines_ref, *refs):
    *pieces, weight_ref, unit_ref, scale_ref, low_ref, away_ref = refs
    product = dot(mixed_ref[...], order_rows(at, pieces, weight_ref))
    half = mine_ref.shape[0]
    for start, tokens_ref in ((0, mine_ref), (half, got_ref)):
        place = pl.ds(start, half)
        hidden = tokens_ref[...].astype(F32) + line(lines_ref, EMBED)
        unit, scale = normalise(hidden + (product[start : start + half, :] + line(lines_ref, OUTPUT_BIAS)))
        unit_ref[place, :] = unit
        scale_ref[place, :] = scale
        low_ref[place, :] = (unit * line(lines_ref, GAIN1) + line(lines_ref, SHIFT1)).astype(BF16)
    width = D // 4
    for k, left_ref in enumerate((low_ref, rounded_ref, mixed_ref)):
        for flip in (1, 0):
            column = pl.multiple_of(their(flip, at) * width, width)
            block = 2 * k + 1 - flip
            away_ref[:, block * width : (block + 1) * width] = left_ref[:, pl.ds(column, width)]


def feed_forward_kernel(
    at, low_ref, bias_ref, unit1_ref, scale1_ref, mine_ref, got_ref, lines_ref, down_ref, output_ref, *refs
):
    pieces, refs = refs[:4], refs[4:]
    active_ref, active_away_ref, final_ref, away_ref, delta_ref, up_delta_ref, down_sums_ref, up_sums_ref = refs[:8]
    input_ref, out_ref, rights_ref, mixed_ref, first_sums_ref, up_all, active_all, slope_all, sum_ref = refs[8:]
    j = pl.program_id(0)
    row = lambda i: line(lines_ref, i)
    half = mine_ref.shape[0]

    @pl.when(j < 4)
    def _():
        weight = order_rows(at, pieces, up_all.at[j])
        for start in (0, half):
            place = pl.ds(start, half)
            active, slope = gelu_and_slope(dot(low_ref[place, :], weight) + bias_ref[...])
            active_ref[place, :] = active.astype(BF16)
            slope_all[j, place, :] = slope.astype(BF16)
        active_all[j] = active_ref[...]

    for flip in (1, 0):

        @pl.when(j == their(flip, at))
        def _(flip=flip):
            width = active_ref.shape[1]
            active_away_ref[:, (1 - flip) * width : (2 - flip) * width] = active_ref[...]

    @pl.when(j == 4)
    def _():
        sum_ref[...] = dot(active_all[0], down_ref[...])

    @pl.when((j > 4) & (j < 8))
    def _():
        sum_ref[...] += dot(active_all[j - 4], down_ref[...])

    @pl.when(j == 7)
    def _():
        sums = [0.0, 0.0, 0.0]
        for start, upstream_ref, one_ref in ((0, mine_ref, final_ref), (half, got_ref, away_ref)):
            place = pl.ds(start, half)
            first_norm = unit1_ref[place, :] * row(GAIN1) + row(SHIFT1)
            unit, scale = normalise(first_norm + (sum_ref[place, :] + row(DOWN_BIAS)))
            one_ref[...] = (unit * row(GAIN2) + row(SHIFT2)).astype(BF16)
            cotangent = upstream_ref[...].astype(F32) * row(WEIGHT)
            grad = normalise_back(unit, scale, row(GAIN2), cotangent)
            delta = grad.astype(BF16)
            sum_ref[place, :] = grad
            delta_ref[place, :] = delta
            parts = (cotangent * unit, cotangent, delta.astype(F32))
            sums = [one + total(part) for one, part in zip(sums, parts)]
        for i, one in enumerate(sums):
            down_sums_ref[i : i + 1, :] = one

    @pl.when(j >= 8)
    def _():
        k = j - 8
        delta = (dot_back(delta_ref[...], down_ref[...]) * slope_all[k].astype(F32)).astype(BF16)
        up_delta_ref[...] = delta
        up_sums_ref[pl.ds(k, 1), :] = total(delta.astype(F32))
        sum_ref[...] += dot_back(delta, up_all[k])

    @pl.when(j == 11)
    def _():
        sums = [0.0, 0.0, 0.0]
        for start in (0, half):
            place = pl.ds(start, half)
            grad, unit = sum_ref[place, :], unit1_ref[place, :]
            below = normalise_back(unit, scale1_ref[place, :], row(GAIN1), grad)
            delta = below.astype(BF16)
            input_ref[place, :] = below
            out_ref[place, :] = delta
            rights_ref[place, :] = delta
            mixed_ref[place, :] = dot_back(delta, output_ref[...]).astype(BF16)
            parts = (grad * unit, grad, delta.astype(F32))
            sums = [one + total(part) for one, part in zip(sums, parts)]
        for i, one in enumerate(sums):
            first_sums_ref[i : i + 1, :] = one


def attend_back_kernel(
    _, q_ref, k1_ref, v1_ref, k2_ref, v2_ref, lse_ref, grad_ref, *refs
):
    dq_ref, rights_ref, near_ref, far_ref, p_all, ds_all = refs[-6:]
    half, tokens = k1_ref.shape[0], q_ref.shape[0]
    keys = jnp.concatenate([k1_ref[...], k2_ref[...]], axis=0)
    values = jnp.concatenate([v1_ref[...], v2_ref[...]], axis=0)
    keys_t = keys.T
    queries = q_ref[...] * jnp.asarray(HEAD_DIM**-0.5, BF16)
    grads = grad_ref[...]
    query_parts, grad_parts, dq_parts = [], [], []
    for head in range(GROUP_HEADS):
        query_one = jnp.where(head_mask(head), queries, jnp.zeros_like(queries))
        grad_one = jnp.where(head_mask(head), grads, jnp.zeros_like(grads))
        attention = jnp.exp(dot_back(keys, query_one) - lse_ref[0, head : head + 1, :])
        prob_grad = dot_back(values, grad_one)
        weighted = total(attention * prob_grad)
        score_grad = (attention * (prob_grad - weighted)).astype(BF16)
        place = slice(head * tokens, (head + 1) * tokens)
        p_all[:, place] = attention.astype(BF16)
        ds_all[:, place] = score_grad
        dq_parts.append(dot(keys_t[head * HEAD_DIM : (head + 1) * HEAD_DIM, :], score_grad))
        query_parts.append(query_one)
        grad_parts.append(grad_one)
    value_grad = dot(p_all[...], jnp.concatenate(grad_parts, axis=0))
    key_grad = dot(ds_all[...], jnp.concatenate(query_parts, axis=0))
    dq_ref[...] = (jnp.concatenate(dq_parts, axis=0) * HEAD_DIM**-0.5).astype(BF16).T
    rights_ref[...] = dq_ref[...]
    near_ref[:, :GROUP] = key_grad[:half, :]
    near_ref[:, GROUP:] = value_grad[:half, :]
    far_ref[:, :GROUP] = key_grad[half:, :].astype(BF16)
    far_ref[:, GROUP:] = value_grad[half:, :].astype(BF16)


def delta_kernel(_, *refs):
    groups = D // GROUP
    nears, fars = refs[:groups], refs[groups : 2 * groups]
    queries_ref, __, keys_ref, values_ref, rights_ref, sums_ref = refs[2 * groups :]
    i = pl.program_id(0)
    for g in range(groups):
        place = slice(g * GROUP, (g + 1) * GROUP)
        rights_ref[:, place] = (nears[g][...] + fars[g][...].astype(F32)).astype(BF16)
    sums_ref[pl.ds(1 + i, 1), :] = total(rights_ref[...].astype(F32))

    @pl.when(i == 0)
    def _():
        sums_ref[0:1, :] = total(queries_ref[...].astype(F32))
        keys_ref[...] = rights_ref[...]

    @pl.when(i == 1)
    def _():
        values_ref[...] = rights_ref[...]


def input_query_kernel(_, delta_ref, weight_ref, grad_ref, out_ref):
    out_ref[...] = grad_ref[...] + dot_back(delta_ref[...], weight_ref[...])


def input_kernel(_, delta_ref, weight_ref, grad_ref, mine_ref, away_ref, time_ref, sum_ref):
    j = pl.program_id(0)
    part = dot_back(delta_ref[...], weight_ref[...])

    @pl.when(j == 0)
    def _():
        sum_ref[...] = grad_ref[...] + part

    @pl.when(j > 0)
    def _():
        sum_ref[...] += part

    @pl.when(j == pl.num_programs(0) - 1)
    def _():
        half = mine_ref.shape[0]
        mine_ref[...] = sum_ref[:half, :]
        away_ref[...] = sum_ref[half:, :].astype(BF16)
        time_ref[...] = total(sum_ref[...])


def grad_block(which, left_ref, right_ref, far_left_ref, fars, sum_ref, *more):
    for k, far_ref in enumerate(fars):

        @pl.when((which == k) if len(fars) > 1 else (which >= 0))
        def _(far_ref=far_ref):
            sum_ref[...] = outer(far_left_ref[...], far_ref[...])

    block = outer(left_ref[...], right_ref[...]) + sum_ref[...]
    for one_ref in more:
        block = block + one_ref[...].astype(F32)
    return block.astype(BF16)


def grad_x_kernel(_, left_ref, right_ref, far_left_ref, *refs):
    *fars, out_ref, sum_ref = refs
    out_ref[...] = grad_block(pl.program_id(0), left_ref, right_ref, far_left_ref, fars, sum_ref)


def grad_y_kernel(at_ref, left_ref, right_ref, far_left_ref, other_ref, *refs):
    *fars, away_ref, keep_ref, sum_ref = refs
    i, half = pl.program_id(0), pl.num_programs(0) // 2
    which = jnp.where(i < half, 1 - at_ref[SIDE_Y], at_ref[SIDE_Y])
    block = grad_block(which, left_ref, right_ref, far_left_ref, fars, sum_ref, other_ref)

    @pl.when(i < half)
    def _():
        away_ref[...] = block

    @pl.when(i >= half)
    def _():
        keep_ref[...] = block


def fold_kernel(_, keep1_ref, keep2_ref, away1_ref, away2_ref, keep_ref, away_ref):
    keep_ref[...] = (keep1_ref[...].astype(F32) + keep2_ref[...].astype(F32)).astype(BF16)
    away_ref[...] = (away1_ref[...].astype(F32) + away2_ref[...].astype(F32)).astype(BF16)


def add_kernel(_, one_ref, two_ref, out_ref):
    out_ref[...] = (one_ref[...].astype(F32) + two_ref[...].astype(F32)).astype(out_ref.dtype)


def join_kernel(at_ref, mine_ref, other_ref, out_ref):
    rows = mine_ref.shape[0]
    out_ref[pl.ds(pl.multiple_of(at_ref[SIDE_Z] * rows, 16), rows), :] = mine_ref[...]
    out_ref[pl.ds(pl.multiple_of((1 - at_ref[SIDE_Z]) * rows, 16), rows), :] = other_ref[...]


def finish_kernel(_, mine_ref, other_ref, *refs):
    out_ref = refs[-1]
    i, half = pl.program_id(0), pl.num_programs(0) // 2

    @pl.when(i < half)
    def _():
        out_ref[...] = mine_ref[...].astype(F32)

    @pl.when(i >= half)
    def _():
        out_ref[...] = other_ref[...].astype(F32)


def copy_kernel(_, in_ref, out_ref):
    out_ref[...] = in_ref[...]


def two_kernel(at, mine_ref, other_ref, first_ref, second_ref):
    first = at[SIDE_Y] == 0
    mine, other = mine_ref[...].astype(F32), other_ref[...].astype(F32)
    first_ref[...] = jnp.where(first, mine, other)
    second_ref[...] = jnp.where(first, other, mine)


def pair_kernel(_, mine_ref, received_ref, out_ref):
    @pl.when(pl.program_id(0) == 0)
    def _():
        out_ref[...] = mine_ref[...]

    @pl.when(pl.program_id(0) == 1)
    def _():
        out_ref[...] = received_ref[...].astype(out_ref.dtype)


def append_kernel(_, first_ref, *refs):
    *vectors, out_ref, small_ref = refs
    rows = first_ref.shape[0]
    out_ref[:rows, :] = first_ref[...]
    flat = jnp.concatenate([vector[...].astype(F32).reshape(1, -1) for vector in vectors], axis=1)
    lines = [flat[:, start : start + D] for start in range(0, flat.shape[1], D)]
    small = jnp.concatenate(lines + [jnp.zeros((16 - len(lines), D), F32)], axis=0).astype(BF16)
    small_ref[...] = small
    out_ref[rows:, :] = small


def side_by_side_kernel(_, *refs):
    out_ref, at = refs[-1], 0
    for piece in refs[:-1]:
        out_ref[:, at : at + piece.shape[1]] = piece[...]
        at += piece.shape[1]


def split_kernel(_, in_ref, first_ref, second_ref):
    rows = first_ref.shape[0]
    first_ref[...] = in_ref[:rows, :]
    second_ref[...] = in_ref[rows:, :]


def parity(at):
    return (at[SIDE_Y] + at[SIDE_Z]) % 2


def remote_kernel(at, half_ref, third_ref, fourth_ref, *outs):
    columns = 0
    for out_ref in outs:
        width = out_ref.shape[1]
        place = slice(columns, columns + width)
        columns += width
        remote_rows(at, half_ref.at[:, place], third_ref.at[:, place], fourth_ref.at[:, place], out_ref)


def remote_rows(at, half_ref, third_ref, fourth_ref, out_ref):
    half, quarter = half_ref.shape[0], third_ref.shape[0]
    missing = (1 - parity(at)) * half
    out_ref[pl.ds(pl.multiple_of(parity(at) * half, 16), half), :] = half_ref[...]
    out_ref[pl.ds(pl.multiple_of(missing, 16), quarter), :] = third_ref[...]
    out_ref[pl.ds(pl.multiple_of(missing + quarter, 16), quarter), :] = fourth_ref[...]


def lines_kernel(at, down_ref, first_ref, delta_ref, up_ref, time_ref, out_ref):
    out_ref[0:8, :] = down_ref[...]
    out_ref[8:16, :] = first_ref[...]
    out_ref[16:24, :] = delta_ref[...]
    out_ref[24:28, :] = up_ref[0:4, :]
    row = lax.broadcasted_iota(jnp.int32, (4, D), 0)
    out_ref[28:32, :] = jnp.where(row == at[CHIP], time_ref[...], 0.0)


def per_device(n_dp, inputs, timestep, bucket_count, upstream, *params):
    query_weight, key_weight, value_weight, output_weight, up_weight, down_weight = params[:6]
    vectors = params[6:]
    device = lax.axis_index("fsdp")
    chip, core = device // 2, device % 2
    bucket = lax.axis_index("dp")
    half = inputs.shape[1]
    tokens = 2 * half
    hidden_width = up_weight.shape[1]
    side_y, side_z = bucket % 2, (bucket // 2) % 2
    place = jnp.stack([chip, core, side_y, side_z]).astype(jnp.int32)
    run = functools.partial(run_kernel, place)

    def swap(value, axis, bit):
        size = 4 if axis == "fsdp" else n_dp
        return lax.ppermute(value, axis, [(i, i ^ bit) for i in range(size)])

    swap_core = lambda value: swap(value, "fsdp", 1)
    swap_chip = lambda value: swap(value, "fsdp", 2)
    swap_y = lambda value: swap(value, "dp", 1)
    swap_z = lambda value: swap(value, "dp", 2)

    def pick(array, flip, *later_than):
        _, rows, columns = array.shape
        ins = [(array, (None, rows, columns), lambda _, at: (at[CHIP] ^ flip, 0, 0))]
        return run("pick", copy_kernel, (1,), ins, [whole_out((rows, columns), array.dtype)], later_than)

    def pack(arrays, *later_than):
        shape = (arrays[0].shape[0], sum(array.shape[1] for array in arrays))
        return run("pack", side_by_side_kernel, (1,), [whole(a) for a in arrays], [whole_out(shape, BF16)], later_than)

    def cut(shards, *later_than):
        rows = shards[0].shape[0]
        columns = sum(shard.shape[1] for shard in shards)
        ins = [(shard, (rows // 2, shard.shape[1]), lambda _, at: (parity(at), 0)) for shard in shards]
        outs = [whole_out((rows // 2, columns), BF16)]
        return run("cut", side_by_side_kernel, (1,), ins, outs, later_than)

    def split(first, *later_than):
        rows, columns = first.shape
        outs = [whole_out((rows // 2, columns), BF16)] * 2
        to_y, to_z = run("split", split_kernel, (1,), [whole(first)], outs, later_than)
        return (first, swap_y(to_y), swap_z(to_z)), to_y

    def remote(parts, widths, *later_than):
        outs = [whole_out((2 * parts[0].shape[0], width), BF16) for width in widths]
        return run("remote", remote_kernel, (1,), [whole(part) for part in parts], outs, later_than)

    tokens_away, small = run(
        "pick", append_kernel, (1,),
        [(inputs, (None, half, D), lambda _, at: (at[CHIP] ^ 1, 0, 0))] + [whole(vector) for vector in vectors],
        [whole_out((half + 16, D), BF16), whole_out((16, D), BF16)],
    )
    tokens_got = swap_chip(tokens_away)
    got_half = (tokens_got, (half, D), lambda *_: (0, 0))
    three = (query_weight, key_weight, value_weight)
    two_weights = (output_weight, up_weight)
    three_cut = cut(three, tokens_away)
    three_first = swap_chip(three_cut)
    three_own = pack(three, three_cut)
    three_sibling = swap_core(three_own)
    two_own = pack(two_weights, three_own)
    two_sibling = swap_core(two_own)
    two_cut = cut(two_weights, tokens_got, two_own)
    two_first = swap_chip(two_cut)
    upstream_away = pick(upstream, 1, two_cut)
    upstream_got = swap_chip(upstream_away)
    tokens_mine = pick(inputs, 0, upstream_away)
    live = chip < bucket_count[bucket]
    seq_weight = live.astype(F32) * (2 * n_dp / jnp.sum(bucket_count).astype(F32))
    small_two = jnp.concatenate([small, tokens_got[half:]], axis=0)
    small_far = swap_core(small_two)
    three_parts, split_done = split(three_first, three_sibling, two_sibling, tokens_mine, small_far)
    down_copy = run("copy", copy_kernel, (1,), [whole(down_weight)], [whole_out(down_weight.shape, BF16)], (split_done,))
    down_matrix = lax.all_gather(down_copy, "fsdp", axis=0, tiled=True)
    query_remote, kv_remote = remote(three_parts, (D, 2 * D), down_copy)
    lines, up_bias = run(
        "lines_in", lines_in_kernel, (1,),
        [whole(a) for a in (small_two, small_far, sinusoid(timestep), seq_weight.reshape(1, 1))],
        [whole_out((LINES, D), F32), whole_out((1, hidden_width), F32)], (kv_remote,),
    )
    kv_pieces = [three_own, kv_remote, three_sibling, swap_core(kv_remote)]
    query_pieces = [three_own, query_remote, three_sibling, swap_core(query_remote)]
    keys, values, qkv_matrix, lefts = run(
        "key_value", key_value_kernel, (2,),
        [whole(tokens_mine), got_half, whole(lines)] + pieces_in(kv_pieces, D, (1, 0, 1, 0)),
        [
            whole_out((tokens, D), BF16),
            whole_out((tokens, D), BF16),
            ((D, 3 * D), BF16, (D, D), lambda j, *_: (0, 1 + j)),
            ((tokens, 2 * D), BF16, (tokens, D), lambda j, *_: (0, 0)),
        ],
    )
    far_keys, far_values = swap_core(keys), swap_core(values)
    queries, qkv_matrix = run(
        "query", query_kernel, (1,),
        [(lefts, (tokens, D), lambda j, *_: (0, 0)), whole(lines)] + pieces_in(query_pieces, D, (0, 0, 0, 0))
        + [(qkv_matrix, None, None)],
        [((tokens, D), BF16, (tokens, D), lambda j, *_: (0, 0)), ((D, 3 * D), BF16, (D, D), lambda j, *_: (0, 0))],
        aliases={2 + len(query_pieces): 1},
    )
    groups = D // GROUP
    group_of = lambda array, first: (array, (array.shape[0], GROUP), lambda g, *_: (0, first + g))

    def attend(first, count, lefts, lse, *later_than):
        return run(
            "attend", attend_kernel, (count,),
            [group_of(a, first) for a in (queries, keys, values, far_keys, far_values)] + [(lefts, None, None)]
            + ([] if lse is None else [(lse, None, None)]),
            [
                ((tokens, 2 * D), BF16, (tokens, GROUP), lambda g, *_: (0, groups + first + g)),
                ((groups, GROUP_HEADS, tokens), F32, (1, GROUP_HEADS, tokens), lambda g, *_: (first + g, 0, 0)),
            ],
            later_than, aliases={5: 0} if lse is None else {5: 0, 6: 1}, vmem=32,
        )

    lefts, lse = attend(0, groups // 2, lefts, None)
    two_parts, split_done = split(two_first, lse)
    lefts, lse = attend(groups // 2, groups // 2, lefts, lse, split_done)
    two_remote = remote(two_parts, (two_own.shape[1],), lse)
    upstream_mine = pick(upstream, 0, two_remote)
    two_pieces = [two_own, two_remote, two_sibling, swap_core(two_remote)]
    output_matrix, unit1, scale1, first_low, lefts_away = run(
        "output", output_kernel, (1,),
        [(lefts, (tokens, D), lambda j, *_: (0, 0)), (lefts, (tokens, D), lambda j, *_: (0, 1))]
        + [whole(tokens_mine), got_half, whole(lines)]
        + pieces_in(two_pieces, D, (0, 0, 0, 0)),
        [
            whole_out((D, D), BF16),
            whole_out((tokens, D), F32),
            whole_out((tokens, 1), F32),
            whole_out((tokens, D), BF16),
            whole_out((tokens, 6 * D // 4), BF16),
        ],
        (upstream_mine,),
    )
    lefts_away = swap_core(lefts_away)
    width = hidden_width // 4
    hidden_block = lambda j: jnp.minimum(j, 3)
    results = run(
        "feed_forward", feed_forward_kernel, (12,),
        [held(first_low), (up_bias, (1, width), lambda j, *_: (0, hidden_block(j))), held(unit1), held(scale1)]
        + [held(upstream_mine), held(upstream_got), held(lines)]
        + [(down_matrix, (width, D), lambda j, *_: (jnp.where(j < 4, 0, j % 4), 0)), held(output_matrix)]
        + [(piece, (piece.shape[0], width), lambda j, *_: (0, D // width + hidden_block(j))) for piece in two_pieces],
        [
            ((tokens, hidden_width), BF16, (tokens, width), lambda j, *_: (0, hidden_block(j))),
            whole_out((tokens, 2 * width), BF16),
            whole_out((half, D), BF16),
            whole_out((half, D), BF16),
            whole_out((tokens, D), BF16),
            ((tokens, hidden_width), BF16, (tokens, width), lambda j, *_: (0, jnp.maximum(j - 8, 0))),
            whole_out((8, D), F32),
            whole_out((8, D), F32),
            whole_out((tokens, D), F32),
            whole_out((tokens, D), BF16),
            ((tokens, 4 * D), BF16, (tokens, D), lambda j, *_: (0, 3)),
            whole_out((tokens, D), BF16),
            whole_out((8, D), F32),
        ],
        (),
        [
            pltpu.VMEM((4, D, width), BF16),
            pltpu.VMEM((4, tokens, width), BF16),
            pltpu.VMEM((4, tokens, width), BF16),
            pltpu.VMEM((tokens, D), F32),
        ],
    )
    activated, active_away, final_mine, final_away, down_delta, up_delta, down_sums, up_sums = results[:8]
    input_part, out_delta, rights, mixed_grad, first_sums = results[8:]
    active_away, down_far = swap_core(active_away), swap_core(down_delta)
    up_far, out_far = swap_core(up_delta), swap_core(out_delta)

    block_rows = D // 4

    class Grads:
        def __init__(self, left, right, send, keep, fars, near, right_column):
            self.left, self.right, self.send_far, self.keep_far = left, right, send, keep
            self.fars, self.near, self.right_column = fars, near, right_column

        def ins(self, flip, far, block):
            far_left, far_column = far
            shard = lambda at: 2 * (at[CHIP] ^ flip) + at[CORE]
            return [
                (self.left, (tokens, block_rows), lambda i, at: (0, self.near(shard(at), block(i, at)))),
                (self.right, (tokens, D), lambda i, at: (0, self.right_column(block(i, at)))),
                (far_left, (tokens, block_rows), lambda i, at: (0, far_column(block(i, at)))),
            ]

        def far_ins(self, block, first, count):
            if len(self.fars) > 1:
                return [whole(a) for a in self.fars[first : first + count]]
            return [(self.fars[0], (tokens, D), lambda i, at: (0, self.right_column(block(i, at))))]

        def four(self, name, body, flip, far, more, *later_than):
            out = ((4 * block_rows, D), BF16, (block_rows, D), lambda i, at: (i, 0))
            block = lambda i, at: i
            ins = self.ins(flip, far, block) + more + self.far_ins(block, 0, 4)
            return run(name, body, (4,), ins, [out], later_than, [pltpu.VMEM((block_rows, D), F32)])

        def start(self, *later_than):
            sent = self.four("grad_x", grad_x_kernel, 1, self.send_far, [], *later_than)
            self.got = swap_chip(sent)
            return sent

    class Chunk:
        def __init__(self, grads, first, count):
            self.grads, self.first, self.half = grads, first, count // 2

        def over_y(self, last):
            grads, first, half = self.grads, self.first, self.half
            block = lambda i, at: first + jnp.where(
                i < half, (1 - at[SIDE_Y]) * half + i, at[SIDE_Y] * half + i - half
            )
            other = (grads.got, (block_rows, D), lambda i, at: (block(i, at), 0))
            shape = (half * block_rows, D)
            away, self.keep = run(
                "grad_y", grad_y_kernel, (2 * half,),
                grads.ins(0, grads.keep_far, block) + [other] + grads.far_ins(block, first, 2),
                [
                    (shape, BF16, (block_rows, D), lambda i, at: (jnp.minimum(i, half - 1), 0)),
                    (shape, BF16, (block_rows, D), lambda i, at: (jnp.maximum(i - half, 0), 0)),
                ],
                (last,), [pltpu.VMEM((block_rows, D), F32)],
            )
            self.got = swap_y(away)
            return self.keep

        def over_z(self, last):
            block = (self.keep.shape[0] // 2, D)
            kept = [(a, block, lambda _, at: (at[SIDE_Z], 0)) for a in (self.keep, self.got)]
            given = [(a, block, lambda _, at: (1 - at[SIDE_Z], 0)) for a in (self.keep, self.got)]
            self.keep, away = run("grad_z", fold_kernel, (1,), kept + given, [whole_out(block, BF16)] * 2, (last,))
            self.got = swap_z(away)
            return self.keep

        def add(self, bit, last):
            ins = [whole(self.keep), whole(self.got)]
            self.keep = run("grad_add", add_kernel, (1,), ins, [whole_out(self.keep.shape, BF16)], (last,))
            self.got = swap(self.keep, "dp", bit)
            return self.keep

        def add_high(self, last):
            for bit in high_bits:
                last = self.add(bit, last)
            return last

        def add_low(self, last):
            return self.add(2, last)

        def back(self, last):
            ins = [whole(self.keep), whole(self.got)]
            shape = (2 * self.keep.shape[0], D)
            self.keep = run("grad_join", join_kernel, (1,), ins, [whole_out(shape, BF16)], (last,))
            self.got = swap_y(self.keep)
            return self.keep

        def finish(self, last, shape, index):
            half = self.half
            ins = [
                (self.keep, (block_rows, D), lambda i, at: (jnp.minimum(i, half - 1), 0)),
                (self.got, (block_rows, D), lambda i, at: (jnp.maximum(i - half, 0), 0)),
            ]
            place = lambda i, at: jnp.where(i < half, at[SIDE_Y] * half + i, (1 - at[SIDE_Y]) * half + i - half)
            out = (shape, F32, (block_rows, D), lambda i, at: index(place(i, at)))
            return run("grad_out", finish_kernel, (2 * half,), ins, [out], (last,))

    def pair_of(mine, received, dtype, last):
        out = ((2, half, D), dtype, (None, half, D), lambda i, at: (at[CHIP] ^ i, 0, 0))
        return run("pair", pair_kernel, (2,), [whole(mine), whole(received)], [out], (last,))

    high_bits = [1 << i for i in range(2, n_dp.bit_length()) if 1 << i < n_dp]
    relay = lambda array, last: run("relay", copy_kernel, (1,), [whole(array)], [whole_out(array.shape, array.dtype)], (last,))

    grads_down = Grads(
        activated, down_delta, (active_away, lambda b: b), (active_away, lambda b: 4 + b), [down_far],
        lambda shard, b: shard * (hidden_width // D) + b, lambda b: 0,
    )
    grads_up = Grads(
        first_low, up_delta, (lefts_away, lambda b: 0), (lefts_away, lambda b: 1), [up_far],
        lambda shard, b: shard, lambda b: b,
    )

    def attend_back(first, count, later_than, rights, query_delta):
        return run(
            "attend_back", attend_back_kernel, (count,),
            [group_of(a, first) for a in (queries, keys, values, far_keys, far_values)]
            + [(lse, (1, GROUP_HEADS, tokens), lambda g, *_: (first + g, 0, 0)), group_of(mixed_grad, first)]
            + [(rights, None, None)] + ([] if query_delta is None else [(query_delta, None, None)]),
            [
                ((tokens, D), BF16, (tokens, GROUP), lambda g, *_: (0, first + g)),
                ((tokens, 4 * D), BF16, (tokens, GROUP), lambda g, *_: (0, first + g)),
                ((tokens, 2 * count * GROUP), F32, (tokens, 2 * GROUP), lambda g, *_: (0, g)),
                ((tokens, 2 * count * GROUP), BF16, (tokens, 2 * GROUP), lambda g, *_: (0, g)),
            ],
            later_than, [pltpu.VMEM((2 * tokens, GROUP_HEADS * tokens), BF16)] * 2, aliases={7: 1} if query_delta is None else {7: 1, 8: 0},
        )

    first_call = 1
    query_delta, rights, near1, far1 = attend_back(0, first_call, (mixed_grad,), rights, None)
    far1 = swap_core(far1)
    last = grads_down.start(near1)
    last = grads_up.start(last, out_far)
    query_delta, rights, near2, far2 = attend_back(first_call, groups - first_call, (last, far1), rights, query_delta)
    far2, query_far = swap_core(far2), swap_core(query_delta)
    last = input_part = run(
        "input_query", input_query_kernel, (2,),
        [
            (query_delta, (half, D), lambda i, *_: (i, 0)),
            (qkv_matrix, (D, D), lambda i, *_: (0, 0)),
            (input_part, (half, D), lambda i, *_: (i, 0)),
        ],
        [((tokens, D), F32, (half, D), lambda i, *_: (i, 0))], (near2,),
    )
    key_delta, value_delta, rights, delta_sums = run(
        "delta", delta_kernel, (2,),
        [
            (a, (tokens, GROUP), lambda i, *_, g=g: (0, 2 * g + i))
            for one, two in ((near1, near2), (far1, far2))
            for a, count in ((one, first_call), (two, groups - first_call))
            for g in range(count)
        ]
        + [whole(query_delta), (rights, None, None)],
        [
            whole_out((tokens, D), BF16),
            whole_out((tokens, D), BF16),
            ((tokens, 4 * D), BF16, (tokens, D), lambda i, *_: (0, 1 + i)),
            whole_out((8, D), F32),
        ],
        (last,), aliases={2 * groups + 1: 2},
    )
    key_far, value_far = swap_core(key_delta), swap_core(value_delta)
    step = D
    input_mine, input_away, time_sum = run(
        "input", input_kernel, (2,),
        [(rights, (tokens, D), lambda j, *_: (0, 1 + j)), (qkv_matrix, (D, D), lambda j, *_: (0, 1 + j)), whole(input_part)],
        [whole_out((half, D), F32), whole_out((half, D), BF16), whole_out((1, D), F32)],
        (delta_sums,), [pltpu.VMEM((tokens, D), F32)],
    )
    last_one = lambda b: jnp.where(b == 3, 1, 0)
    grads_four = Grads(
        lefts, rights, (lefts_away, lambda b: 2 + 2 * last_one(b)), (lefts_away, lambda b: 3 + 2 * last_one(b)),
        [query_far, key_far, value_far, out_far], lambda shard, b: shard + 4 * last_one(b), lambda b: b,
    )
    down, up = Chunk(grads_down, 0, 4), Chunk(grads_up, 0, 4)
    last = down.over_y(time_sum)
    last = grads_four.start(last)

    packed = run(
        "lines", lines_kernel, (1,), [whole(a) for a in (down_sums, first_sums, delta_sums, up_sums, time_sum)],
        [whole_out((32, D), F32)], (last,),
    )
    hops = [("fsdp", 1), ("fsdp", 2)] + [("dp", 1 << i) for i in range(n_dp.bit_length() - 1)]
    line_parts, line_got = [packed], [swap(packed, *hops[0])]

    def add_lines(last):
        ins = [whole(line_parts[-1]), whole(line_got[-1])]
        line_parts.append(run("lines_add", add_kernel, (1,), ins, [whole_out((32, D), F32)], (last,)))
        if len(line_parts) <= len(hops) - 0 and len(line_got) < len(hops):
            line_got.append(swap(line_parts[-1], *hops[len(line_got)]))
        return line_parts[-1]

    qk, vo = Chunk(grads_four, 0, 2), Chunk(grads_four, 2, 2)
    last = down.over_z(packed)
    last = add_lines(last)
    last = up.over_y(last)
    last = down.add_high(last)
    last = up.over_z(last)
    last = down.add_low(last)
    last = qk.over_y(last)
    last = vo.over_y(last)
    last = up.add_high(last)
    last = down.back(last)
    last = add_lines(last)
    last = qk.over_z(last)
    last = vo.over_z(last)
    last = final_away = relay(final_away, last)
    final_got = swap_chip(final_away)
    last = up.add_low(last)
    last = qk.add_high(last)
    last = vo.add_high(last)
    last = add_lines(last)
    last = down_grad = down.finish(last, down_weight.shape, lambda s: (s, 0))
    last = up.back(last)
    last = qk.add_low(last)
    last = vo.add_low(last)
    last = input_away = relay(input_away, last)
    input_got = swap_chip(input_away)
    last = final = pair_of(final_mine, final_got, BF16, last)
    last = qk.back(last)
    last = vo.back(last)
    while len(line_parts) < len(hops):
        last = add_lines(last)
    last = up_grad = up.finish(last, up_weight.shape, lambda s: (0, s))
    last = input_gradient = pair_of(input_mine, input_got, F32, last)
    last = add_lines(last)

    def two(chunk, last):
        outs = [whole_out((block_rows, D), F32)] * 2
        return run("two", two_kernel, (1,), [whole(chunk.keep), whole(chunk.got)], outs, (last,))

    query_grad, key_grad = two(qk, last)
    value_grad, output_grad = two(vo, query_grad)
    times = lax.dynamic_slice_in_dim(line_parts[2], device * (D // 4), D // 4, axis=1)
    time_gradient = times[28:30]
    packed = line_parts[-1]
    mine = lax.dynamic_slice_in_dim(packed, device * (D // 4), D // 4, axis=1)
    up_bias_grad = lax.dynamic_slice_in_dim(packed[24:28], device, 1, axis=0).reshape(-1)
    vector_grads = (mine[16], mine[18], mine[10], up_bias_grad, mine[2], mine[8], mine[9], mine[0], mine[1])

    return (
        final,
        input_gradient,
        time_gradient,
        query_grad,
        key_grad,
        value_grad,
        output_grad,
        up_grad,
        down_grad,
        *vector_grads,
    )


def solution(mesh):
    rows, wide, flat = P("dp", "fsdp", None), P("fsdp", None), P("fsdp")
    return jax.shard_map(
        functools.partial(per_device, mesh.shape["dp"]),
        mesh=mesh,
        in_specs=(rows, P("dp"), P(), rows) + (wide,) * 6 + (flat,) * 9,
        out_specs=(rows, rows, P("dp", "fsdp")) + (wide,) * 6 + (flat,) * 9,
        check_vma=False,
    )
```
